32 devices in a mesh: dp: 4 (over x, core), fsdp: 8 (over z, y).
Axes of the slice: x: 2, y: 2, z: 4, core: 2. Of those that a mesh axis runs over, the one named last changes fastest.
Arguments:
- tokens: bfloat16 [16384, 768], P(('dp', 'fsdp')), may hold values from -6 to 6
- bucket_len: int32 [32], P(('dp', 'fsdp')), may hold values from 128 to 512, as said below
- valid: int32 [16384], P(('dp', 'fsdp')), may hold values from 0 to 1, as said below
- routes: int32 [16384, 1], P(('dp', 'fsdp')), may hold values from 0 to 3
- attn_gain: bfloat16 [768], P(('dp', 'fsdp')), may hold values from 0.5 to 1.5
- qkv_weight: bfloat16 [768, 2304], P(('dp', 'fsdp')), may hold values from -0.21875 to 0.21875
- out_weight: bfloat16 [768, 768], P(('dp', 'fsdp')), may hold values from -0.875 to 0.875
- relative_head_bias: float32 [12, 32], replicated, may hold values from -4 to 4
- ffn_gain: bfloat16 [768], P(('dp', 'fsdp')), may hold values from 0.5 to 1.5
- router_weight: bfloat16 [768, 4], P(('dp', 'fsdp')), may hold values from -0.15625 to 0.15625
- w_in: bfloat16 [3072, 4, 768], P(('dp', 'fsdp')), may hold values from -0.21875 to 0.21875
- w_out: bfloat16 [3072, 4, 768], P(('dp', 'fsdp')), may hold values from -0.625 to 0.625
- cotangent: bfloat16 [16384, 768], P(('dp', 'fsdp')), may hold values from -6 to 6
Outputs:
- layer_out: bfloat16 [16384, 768], P(('dp', 'fsdp'))
- tokens_grad: bfloat16 [16384, 768], P(('dp', 'fsdp'))
- attn_gain_grad: float32 [768], P(('dp', 'fsdp'))
- qkv_grad: float32 [768, 2304], P(('dp', 'fsdp'))
- out_grad: float32 [768, 768], P(('dp', 'fsdp'))
- rel_bias_grad: float32 [12, 32], replicated
- ffn_gain_grad: float32 [768], P(('dp', 'fsdp'))
- router_weight_gradient: float32 [768, 4], P(('dp', 'fsdp'))
- w_in_grad: float32 [3072, 4, 768], P(('dp', 'fsdp'))
- w_out_grad: float32 [3072, 4, 768], P(('dp', 'fsdp'))
- dispatched: int32 [4], replicated
- dropped: int32 [4], replicated
The draws below stay inside these ranges and needn't reach their ends.
Inputs may be any that keep to these rules, and one draw needn't show every extreme that they name: `bucket_len`: each block of 512 tokens holds one sequence (512) or 4 sequences of 128; both kinds occur. `valid`: in each sequence the ones form a prefix that covers more than half of it.
All inputs are finite; a program needn't handle non-finite values.
Results may differ from the reference program's by a relative error of at most 0.014.
Values may be sent and summed in bfloat16 or wider, within the bound.
A program may use at most 320 MiB of HBM per device.

```python
import math
import jax
import jax.numpy as jnp
from jax import lax

D = 768
HEADS = 12
HEAD = 64
FF = 3072
BUCKETS = 32
MAXDIST = 128
EXPERTS = 4
LONG = 512
SHORT = 128
TOK_DEV = 512
TOKENS = 16384
CAP = 160
N_DP = 4
N_FSDP = 8


def bucket_layout(key):
    block_total = TOKENS // LONG
    kinds = jax.random.randint(jax.random.fold_in(key, 11), (block_total,), 0, 3)
    lengths = jnp.where(kinds < 2, LONG, SHORT).astype(jnp.int32)
    return lengths.at[0].set(LONG).at[1].set(SHORT)


def draw_bucket_len(key, part):
    return bucket_layout(key)


def draw_valid(key, part):
    lengths = bucket_layout(key)
    own_key = jax.random.fold_in(key, 5)
    block_total = TOKENS // LONG
    slot_total = LONG // SHORT
    cut_draw = jax.random.randint(own_key, (block_total, slot_total), 0, LONG)
    seq_len = lengths[:, None]
    kept_len = seq_len - cut_draw % (seq_len // 2)
    kept_len = kept_len.at[0, 0].set(LONG).at[1, 0].set(SHORT // 2 + 1)
    position = jnp.arange(LONG, dtype=jnp.int32)
    within = position[None, :] % seq_len
    member = position[None, :] // seq_len
    bound_len = jnp.take_along_axis(kept_len, member, axis=1)
    return (within < bound_len).astype(jnp.int32).reshape(-1)


def draw_routes(key, part):
    key = jax.random.fold_in(key, 7)
    busiest = jax.random.randint(jax.random.fold_in(key, 1), (), 0, EXPERTS)
    lottery = jax.random.randint(jax.random.fold_in(key, 2), (TOKENS,), 0, 20)
    remaining = jax.random.randint(jax.random.fold_in(key, 3), (TOKENS,), 0, EXPERTS - 1)
    remaining = remaining + (remaining >= busiest).astype(jnp.int32)
    return jnp.where(lottery < 9, busiest, remaining).astype(jnp.int32).reshape(TOKENS, 1)


def block_levels(key, dims, cuts, low, high):
    level, own = 1.0, jax.random.fold_in(key, 6)
    for dim, blocks in cuts:
        steps = jnp.exp(jax.random.uniform(jax.random.fold_in(own, dim), (blocks,), jnp.float32, low / len(cuts), high / len(cuts)))
        level = level * jnp.repeat(steps, dims[dim] // blocks).reshape([-1 if axis == dim else 1 for axis in range(len(dims))])
    return level


def normal_values(stream_key, shape, spread, most, cuts=(), kind=jnp.bfloat16):
    loudness = block_levels(stream_key, shape, cuts, -0.22, 0.18) if cuts else 1.0
    array = jax.random.normal(stream_key, shape, jnp.float32) * spread * loudness
    return jnp.minimum(jnp.maximum(array, -most), most).astype(kind)


def setup_inputs(seed: int = 0) -> dict:
    arg_keys = jax.random.split(jax.random.key(seed), 14)
    tokens = normal_values(arg_keys[0], (TOKENS, D), 1.0, 6.0, ((0, 32),))
    bucket_len = draw_bucket_len(jax.random.fold_in(arg_keys[13], 71), 0)
    valid = draw_valid(jax.random.fold_in(arg_keys[13], 71), 0)
    routes = draw_routes(jax.random.fold_in(arg_keys[13], 71), 0)
    attn_gain = jnp.clip(1.0 + 0.1 * jax.random.normal(arg_keys[4], (D,), jnp.float32), 0.5, 1.5).astype(jnp.bfloat16)
    qkv_weight = normal_values(arg_keys[5], (D, 3 * D), D ** -0.5, 0.21875, ((0, 32),))
    out_weight = normal_values(arg_keys[6], (D, D), (D // 16) ** -0.5, 0.875, ((0, 32),))
    relative_head_bias = normal_values(arg_keys[7], (HEADS, BUCKETS), 1.0, 4.0, (), jnp.float32)
    ffn_gain = jnp.clip(1.0 + 0.1 * jax.random.normal(arg_keys[8], (D,), jnp.float32), 0.5, 1.5).astype(jnp.bfloat16)
    router_weight = normal_values(arg_keys[9], (D, EXPERTS), (2 * D) ** -0.5, 0.15625, ((0, 32),))
    w_in = normal_values(arg_keys[10], (FF, EXPERTS, D), D ** -0.5, 0.21875, ((0, 32),))
    w_out = normal_values(arg_keys[11], (FF, EXPERTS, D), (FF // 32) ** -0.5, 0.625, ((0, 32),))
    cotangent = normal_values(arg_keys[12], (TOKENS, D), 1.0, 6.0, ((0, 32),))
    return {"tokens": tokens, "bucket_len": bucket_len, "valid": valid, "routes": routes, "attn_gain": attn_gain, "qkv_weight": qkv_weight, "out_weight": out_weight, "relative_head_bias": relative_head_bias, "ffn_gain": ffn_gain, "router_weight": router_weight, "w_in": w_in, "w_out": w_out, "cotangent": cotangent}


epsilon = 1e-06

@jax.custom_vjp
def low(v):
    return lax.optimization_barrier(v.astype(jnp.bfloat16)).astype(jnp.float32)

@jax.custom_vjp
def low_back(v):
    return v

def low_keep(v):
    return (low(v), None)

def low_pass(kept, grad):
    return (grad,)

def back_keep(v):
    return (v, None)

def back_low(kept, grad):
    return (low(grad),)
low.defvjp(low_keep, low_pass)
low_back.defvjp(back_keep, back_low)

def bucket_codes(block_span, bucket_count, reach):
    position = jnp.arange(block_span, dtype=jnp.int32)
    offset_grid = position[None, :] - position[:, None]
    distance = jnp.abs(offset_grid)
    halfway = bucket_count // 2
    exact_span = halfway // 2
    distant = jnp.full(offset_grid.shape, exact_span, jnp.int32)
    for number in range(1, halfway - exact_span):
        threshold = math.ceil(exact_span * (reach / exact_span) ** (number / (halfway - exact_span)))
        distant = distant + (distance >= threshold).astype(jnp.int32)
    return jnp.where(distance < exact_span, distance, distant) + jnp.where(offset_grid > 0, halfway, 0)

def block_allowed(length, live_block):
    position = jnp.arange(live_block.shape[0], dtype=jnp.int32)
    segment = position // length
    return (segment[:, None] == segment[None, :]) & (live_block[None, :] > 0)

def route_table(chosen, live_row, capacity, expert_count):
    route_picks = (chosen[:, None] == jnp.arange(expert_count, dtype=jnp.int32)[None, :]) & (live_row[:, None] > 0)
    places = jnp.cumsum(route_picks.astype(jnp.int32), axis=0) - 1
    slot_place = lax.optimization_barrier(jnp.sum(jnp.where(route_picks, places, 0), axis=1))
    kept_rows = (live_row > 0) & (slot_place < capacity)
    slot_code = jnp.where(kept_rows, chosen * capacity + slot_place, -1)
    dispatch = (jnp.arange(expert_count * capacity, dtype=jnp.int32)[:, None] == slot_code[None, :]).astype(jnp.float32)
    sent_count = lax.optimization_barrier(jnp.sum((route_picks & kept_rows[:, None]).astype(jnp.int32), axis=0))
    lost_count = lax.optimization_barrier(jnp.sum((route_picks & ~kept_rows[:, None]).astype(jnp.int32), axis=0))
    return (dispatch, jnp.stack([sent_count, lost_count]))

def layer_forward(token_rows, weight_list, lengths, live_row, chosen, bucket_grid, dispatch):
    gain_attn, weight_qkv, weight_out, rel_table, gain_ffn, weight_router, expert_in, expert_out = weight_list
    top_probability = lax.Precision.HIGHEST
    row_count = token_rows.shape[0]
    normed = low(token_rows * lax.rsqrt(lax.optimization_barrier(jnp.mean(token_rows * token_rows, axis=-1, keepdims=True)) + epsilon) * gain_attn)
    qkv_rows = low(low_back(jnp.dot(normed, weight_qkv, precision=top_probability)))
    complete_position_bias = rel_table[:, bucket_grid]
    block_total = row_count // LONG

    def attend(packed):
        block_rows, length, live_block = packed
        queries = block_rows[:, :D].reshape(LONG, HEADS, HEAD)
        keys_part = block_rows[:, D:2 * D].reshape(LONG, HEADS, HEAD)
        values_part = block_rows[:, 2 * D:].reshape(LONG, HEADS, HEAD)
        scores = low_back(jnp.einsum('qhd,khd->hqk', queries, keys_part, precision=top_probability) * HEAD ** (-0.5) + complete_position_bias)
        scores = jnp.where(block_allowed(length, live_block)[None], scores, -1e+30)
        weights_low = low(jax.nn.softmax(scores, axis=-1))
        return jnp.einsum('hqk,khd->qhd', weights_low, values_part, precision=top_probability).reshape(LONG, D)
    mixed = lax.map(jax.checkpoint(attend), (qkv_rows.reshape(block_total, LONG, 3 * D), lengths, live_row.reshape(block_total, LONG)))
    mixed = low(low_back(mixed.reshape(row_count, D)))
    hidden = token_rows + low_back(jnp.dot(mixed, weight_out, precision=top_probability))
    normed_two = low(hidden * lax.rsqrt(lax.optimization_barrier(jnp.mean(hidden * hidden, axis=-1, keepdims=True)) + epsilon) * gain_ffn)
    router_probs = jax.nn.softmax(jnp.dot(normed_two, weight_router, precision=top_probability), axis=-1)
    route_hot = (chosen[:, None] == jnp.arange(EXPERTS, dtype=jnp.int32)[None, :]).astype(token_rows.dtype)
    gate_value = lax.optimization_barrier(jnp.sum(router_probs * route_hot, axis=1))
    slot_rows = jnp.dot(dispatch, normed_two, precision=top_probability).reshape(EXPERTS, CAP, D)
    expert_inner = low_back(jnp.einsum('ecd,fed->ecf', slot_rows, expert_in, precision=top_probability))
    active = low(jax.nn.gelu(expert_inner, approximate=True))
    result_slots = low(low_back(jnp.einsum('ecf,fed->ecd', active, expert_out, precision=top_probability)))
    returned = jnp.dot(dispatch.T, result_slots.reshape(EXPERTS * CAP, D), precision=top_probability)
    return hidden + gate_value[:, None] * returned

def reference(tokens, bucket_len, valid, routes, attn_gain, qkv_weight, out_weight, relative_head_bias, ffn_gain, router_weight, w_in, w_out, cotangent):
    device_total = N_DP * N_FSDP
    weights = tuple((weight_item.astype(jnp.float32) for weight_item in (attn_gain, qkv_weight, out_weight, relative_head_bias, ffn_gain, router_weight, w_in, w_out)))
    bucket_grid = bucket_codes(LONG, BUCKETS, MAXDIST)
    packed_all = (tokens.astype(jnp.float32).reshape(device_total, TOK_DEV, D), bucket_len.reshape(device_total, TOK_DEV // LONG), valid.reshape(device_total, TOK_DEV), routes[:, 0].reshape(device_total, TOK_DEV), cotangent.astype(jnp.float32).reshape(device_total, TOK_DEV, D))

    def one_device(totals, packed):
        token_rows, lengths, live_row, chosen, grad_rows = packed
        dispatch, counts = route_table(chosen, live_row, CAP, EXPERTS)

        def forward(rows_in, *weight_list):
            return layer_forward(rows_in, weight_list, lengths, live_row, chosen, bucket_grid, dispatch)
        result, pullback = jax.vjp(forward, token_rows, *weights)
        gradients = pullback(grad_rows)
        totals = tuple((running + fresh for running, fresh in zip(totals, gradients[1:])))
        return (totals, (result.astype(jnp.bfloat16), gradients[0].astype(jnp.bfloat16), counts))
    zero_grads = tuple((jnp.zeros_like(weight_item) for weight_item in weights))
    totals, (layer_out, tokens_grad, counts) = lax.scan(one_device, zero_grads, packed_all)
    count_sums = lax.optimization_barrier(jnp.sum(counts, axis=0))
    return (layer_out.reshape(TOKENS, D), tokens_grad.reshape(TOKENS, D), totals[0], totals[1], totals[2], totals[3], totals[4], totals[5], totals[6], totals[7], count_sums[0], count_sums[1])
```

```python
from functools import partial
import math

import jax
import jax.numpy as jnp
from jax import lax
from jax.experimental import pallas as pl
from jax.experimental.pallas import tpu as pltpu
from jax.sharding import PartitionSpec as P

F32 = jnp.float32
BF16 = jnp.bfloat16
MESH = pl.DeviceIdType.MESH

HEADS = 12
BUCKETS = 32
MAXDIST = 128
LONG = 512
NEG = -1e30
EPS = 1e-06
GELU_C = math.sqrt(2.0 / math.pi)


def nt(a, b):
    return lax.dot_general(a, b, (((1,), (1,)), ((), ())), preferred_element_type=F32)


def nn(a, b):
    return lax.dot_general(a, b, (((1,), (0,)), ((), ())), preferred_element_type=F32)


def tn(a, b):
    return lax.dot_general(a, b, (((0,), (0,)), ((), ())), preferred_element_type=F32)


def exact(a, b, dims):
    return lax.dot_general(
        a, b, (dims, ((), ())), precision=lax.Precision.HIGHEST, preferred_element_type=F32
    )


def iota(shape, axis):
    return lax.broadcasted_iota(jnp.int32, shape, axis)


def bucket_of(offset):
    distance = jnp.abs(offset)
    halfway = BUCKETS // 2
    exact_span = halfway // 2
    distant = jnp.full(offset.shape, exact_span, jnp.int32)
    for number in range(1, halfway - exact_span):
        threshold = math.ceil(
            exact_span * (MAXDIST / exact_span) ** (number / (halfway - exact_span))
        )
        distant = distant + jnp.where(distance >= threshold, 1, 0)
    return jnp.where(distance < exact_span, distance, distant) + jnp.where(offset > 0, halfway, 0)


def diagonal_sums(tile):
    wide = jnp.concatenate([tile, jnp.zeros((128, 128), F32)], axis=1)
    rows = 64
    while rows >= 8:
        wide = wide[:rows] + pltpu.roll(wide[rows : 2 * rows], 256 - rows, 1)
        rows //= 2
    while rows >= 1:
        wide = wide + pltpu.roll(pltpu.roll(wide, 256 - rows, 1), 8 - rows, 0)
        rows //= 2
    return wide[0:1]


VMEM_LIMIT = 63 << 20


def layer_kernel(
    tok, cot, routes, valid, length, rel, qshard, oshard, sshard, wi_hbm, wo_hbm,
    layer_out, tokens_grad, qkv_grad, out_grad, small_grad, wi_grad, wo_grad, p_hbm,
    aq, ar, wq, wo, sm_t, wb, xg, ycore, yx, ry, rz,
    qkvb, u1, obuf, u2, gobuf, hid, prob, code_row, cols, key_mask, tab, bias, pst, dst_s, gd, relg,
    smallp, lsc, lsx, lsy, lsz, fin,
    free,
    s1s, s1r, s3zs, s3ys, s3r, s3l, xs, xr, ycs, ycr, yxs, yxr, dys, dyr, dzs, dzr,
    rcs, rcr, rxs, rxr, rys, ryr, rzs, rzr, psem, fsem,
):
    dp = lax.axis_index("dp")
    fs = lax.axis_index("fsdp")
    x, c = dp // 2, lax.rem(dp, 2)
    z, y = fs // 2, lax.rem(fs, 2)
    xn, cn, yn = 1 - x, 1 - c, 1 - y
    NZ = 4
    NE = 4
    CAP = 160
    D = 768

    def at(xx, cc, zz, yy):
        return (xx * 2 + cc, zz * 2 + yy)

    core_d, x_d, y_d = at(x, cn, z, y), at(xn, c, z, y), at(x, c, z, yn)

    def zz_of(step):
        return lax.rem(z + step, NZ)

    def z_d(step):
        return at(x, c, zz_of(step), y)

    def remote(src, dst, ss, rs, where):
        return pltpu.make_async_remote_copy(
            src_ref=src, dst_ref=dst, send_sem=ss, recv_sem=rs, device_id=where, device_id_type=MESH
        )

    for s in range(3):
        for half in range(2):
            for k in range(3):
                aq[dp, z, y, s, :, half * 384 + k * 128 : half * 384 + k * 128 + 128] = qshard[
                    :, k * D + (2 * s + half) * 128 : k * D + (2 * s + half) * 128 + 128
                ]
    ar[dp, z, y, :, :D] = oshard[...]
    ar[dp, z, y, :, D:] = sshard[...]

    barrier = pltpu.get_barrier_semaphore()
    peers = [core_d, x_d, y_d, z_d(1), z_d(2), z_d(3)]
    for peer in peers:
        pl.semaphore_signal(barrier, inc=1, device_id=peer, device_id_type=MESH)
    pl.semaphore_wait(barrier, len(peers))

    def block(part, dpi, zi, yi):
        return (aq if part == 0 else ar).at[dpi, zi, yi]

    def s1(part, slot, dpi, zi, yi, where):
        ref = block(part, dpi, zi, yi)
        return remote(ref, ref, s1s.at[part, slot], s1r.at[part, dpi * 8 + zi * 2 + yi], where)

    started = []

    def go(copy):
        copy.start()
        started.append(copy)

    dpx, dpc = xn * 2 + c, x * 2 + cn
    for part in (0, 1):
        for st in (1, 2, 3):
            go(s1(part, st - 1, dp, z, y, z_d(st)))
        go(s1(part, 3, dp, z, y, y_d))
        go(s1(part, 7, dp, z, y, x_d))
        go(s1(part, 15, dp, z, y, core_d))

    route_v = routes[...]
    live_v = valid[...] > 0
    picks = jnp.where((iota((8, LONG), 0) == route_v) & live_v, 1.0, 0.0)
    upto = jnp.where(iota((LONG, LONG), 0) <= iota((LONG, LONG), 1), 1.0, 0.0).astype(BF16)
    counts = nn(picks.astype(BF16), upto)
    place = jnp.sum(picks * counts, axis=0, keepdims=True).astype(jnp.int32) - 1
    kept = live_v & (place < CAP)
    code = jnp.where(kept, route_v * CAP + place, -1)
    code_row[...] = code
    keptf = jnp.where(kept, 1.0, 0.0)
    sent = jnp.sum(picks * keptf, axis=1, keepdims=True)
    lost = jnp.sum(picks * (1.0 - keptf), axis=1, keepdims=True)
    lane128 = iota((8, 128), 1)
    relg[3] = jnp.zeros((16, 256), F32)
    relg[3, 0:8, 0:128] = jnp.where(lane128 == 64, sent, 0.0) + jnp.where(lane128 == 65, lost, 0.0)
    stacked = jnp.concatenate(
        [
            jnp.broadcast_to(code.astype(F32), (8, LONG)),
            jnp.broadcast_to(route_v.astype(F32), (8, LONG)),
            jnp.zeros((112, LONG), F32),
        ],
        axis=0,
    )
    cols[...] = jnp.transpose(stacked)
    same = (iota((8, LONG), 1) // 128 == iota((8, LONG), 0)) | (length[0] >= LONG)
    key_mask[...] = jnp.where(same & live_v, 0.0, NEG)

    for st in (1, 2, 3):
        zi = zz_of(st)
        for part in (0, 1):
            s1(part, 0, dp, zi, y, y_d).wait_recv()
            go(s1(part, 3 + st, dp, zi, y, y_d))
            go(s1(part, 7 + st, dp, zi, y, x_d))
            go(s1(part, 15 + st, dp, zi, y, core_d))

    rel16 = jnp.concatenate([rel[...], jnp.zeros((4, BUCKETS), F32)], axis=0)

    def bucket_hot(kind, axis):
        shape = (BUCKETS, 256) if axis == 0 else (256, BUCKETS)
        lane = iota(shape, 1 - axis)
        offset = jnp.where(lane < 128, lane, lane - 256) + (0, 128, -128)[kind]
        return jnp.where(bucket_of(offset) == iota(shape, axis), 1.0, 0.0)

    rows_by_kind = [exact(rel16, bucket_hot(kind, 0), ((1,), (0,))) for kind in range(3)]
    for b in (BUCKETS // 2 - 1, BUCKETS - 1):
        rows_by_kind.append(exact(rel16, jnp.where(iota((BUCKETS, 256), 0) == b, 1.0, 0.0), ((1,), (0,))))
    for head in range(HEADS):
        for kind in range(5):
            tab[head, kind : kind + 1, :] = rows_by_kind[kind][head : head + 1]

    for st in range(4):
        zi = zz_of(st)
        for part in (0, 1):
            s1(part, 0, dp, zi, yn, y_d).wait_recv()
            go(s1(part, 11 + st, dp, zi, yn, x_d))
            go(s1(part, 19 + st, dp, zi, yn, core_d))
    for yi_off in range(2):
        yi = y if yi_off == 0 else yn
        for st in range(4):
            zi = zz_of(st)
            for part in (0, 1):
                s1(part, 0, dpx, zi, yi, x_d).wait_recv()
                go(s1(part, 23 + yi_off * 4 + st, dpx, zi, yi, core_d))
    for dpi in (dpc, xn * 2 + cn):
        for yi in range(2):
            for zi in range(4):
                for part in (0, 1):
                    s1(part, 0, dpi, zi, yi, core_d).wait_recv()
    for copy in started:
        copy.wait_send()

    def s3_src(m, e):
        return (wi_hbm if m == 0 else wo_hbm).at[e]

    def s3_z(m, e, st):
        return remote(s3_src(m, e), wb.at[m, e, z, y], s3zs.at[m, e, st - 1], s3r.at[m, e, z, y], z_d(st))

    def s3_own(m, e):
        return pltpu.make_async_copy(s3_src(m, e), wb.at[m, e, z, y], s3l.at[m, e])

    def s3_y0(m, e):
        return remote(s3_src(m, e), wb.at[m, e, z, y], s3ys.at[m, e, 0], s3r.at[m, e, z, y], y_d)

    def s3_y(m, e, st):
        ref = wb.at[m, e, zz_of(st), y]
        return remote(ref, ref, s3ys.at[m, e, st], s3r.at[m, e, zz_of(st), y], y_d)

    def s3_arrival(m, e, zi, yi):
        ref = wb.at[m, e, zi, yi]
        return remote(ref, ref, s3ys.at[m, e, 0], s3r.at[m, e, zi, yi], y_d)

    def s3_issue(e):
        for m in range(2):
            for st in (1, 2, 3):
                s3_z(m, e, st).start()
            s3_y0(m, e).start()
            s3_own(m, e).start()

    def s3_forward(m, e, st):
        s3_arrival(m, e, zz_of(st), y).wait_recv()
        s3_y(m, e, st).start()

    def s3_finish(e):
        for m in range(2):
            s3_own(m, e).wait()
            for st in range(4):
                s3_arrival(m, e, zz_of(st), yn).wait_recv()

    def s3_sent(e):
        for m in range(2):
            for st in (1, 2, 3):
                s3_z(m, e, st).wait_send()
                s3_y(m, e, st).wait_send()
            s3_y0(m, e).wait_send()

    s3_issue(0)
    s3_issue(1)

    @pl.loop(0, 4)
    def _(dpi):
        for zi in range(4):
            base = pl.multiple_of((dpi * 8 + zi * 2) * 24, 16)
            for s in range(3):
                v = aq[dpi, zi, :, s].astype(F32).reshape(48, D)
                wq[s, pl.ds(base, 48)] = v.astype(BF16)
            v = ar[dpi, zi].astype(F32).reshape(48, 896)
            wo[pl.ds(base, 48)] = v.astype(BF16)

    for peer in peers:
        pl.semaphore_signal(free, inc=1, device_id=peer, device_id_type=MESH)
    sm_t[...] = jnp.transpose(wo[:, D:].astype(F32))
    gain1 = sm_t[0:1, :]
    gain2 = sm_t[1:2, :]

    @pl.loop(0, 4)
    def _(rb):
        rows = pl.ds(pl.multiple_of(rb * 128, 128), 128)
        xf = tok[rows].astype(F32)
        r1 = lax.rsqrt(jnp.mean(xf * xf, axis=-1, keepdims=True) + EPS)
        u1[rows] = (xf * r1 * gain1).astype(BF16)

    for s in range(3):
        qkvb[s] = nn(u1[...], wq[s]).astype(BF16)

    lane_low = iota((LONG, 128), 1) < 64

    def head_mask(v, h2):
        return jnp.where(lane_low if h2 == 0 else ~lane_low, v, jnp.zeros((), v.dtype))

    def p_copy(hp, out):
        slot = lax.rem(hp, 2)
        if out:
            return pltpu.make_async_copy(pst.at[slot], p_hbm.at[hp], psem.at[slot])
        return pltpu.make_async_copy(p_hbm.at[hp], pst.at[slot], psem.at[slot])

    @pl.loop(0, HEADS // 2)
    def _(hp):
        slot = lax.rem(hp, 2)
        s, base = hp // 2, pl.multiple_of(lax.rem(hp, 2) * 384, 128)
        q2 = qkvb[s, :, pl.ds(base, 128)]
        k2 = qkvb[s, :, pl.ds(base + 128, 128)]
        v2 = qkvb[s, :, pl.ds(base + 256, 128)]

        @pl.when(hp >= 2)
        def _():
            p_copy(hp, True).wait()

        for h2 in range(2):
            head = hp * 2 + h2
            qm = head_mask(q2, h2) * jnp.asarray(0.125, BF16)
            vm = head_mask(v2, h2)
            for kind in range(3):
                row = tab[head, kind : kind + 1, :]
                tile = pltpu.roll(jnp.broadcast_to(row, (128, 256)), 0, 1, stride=1, stride_axis=0)
                bias[kind] = tile[:, :128]
            left = jnp.broadcast_to(tab[head, 3:4, 0:128], (128, 128))
            right = jnp.broadcast_to(tab[head, 4:5, 0:128], (128, 128))
            for bi in range(4):
                rows = slice(bi * 128, bi * 128 + 128)
                sc = nt(qm[rows], k2)
                tiles = [
                    bias[0] if bj == bi else bias[1] if bj == bi + 1 else bias[2] if bj == bi - 1
                    else right if bj > bi else left
                    for bj in range(4)
                ]
                sc = sc + jnp.concatenate(tiles, axis=1) + key_mask[bi : bi + 1, :]
                peak = jnp.max(sc, axis=-1, keepdims=True)
                ex = jnp.exp(sc - peak)
                p = (ex * (1.0 / jnp.sum(ex, axis=-1, keepdims=True))).astype(BF16)
                pst[slot, h2, rows] = p
                part = nn(p, vm)
                if h2 == 0:
                    hid[rows, 0:128] = part
                else:
                    obuf[rows, pl.ds(pl.multiple_of(hp * 128, 128), 128)] = (
                        hid[rows, 0:128] + part
                    ).astype(BF16)
        p_copy(hp, True).start()
        s3_forward(hp // 3, 0, 1 + lax.rem(hp, 3))

    s3_issue(2)

    lane = iota((128, 128), 1)
    is_logit = (lane >= 2) & (lane < 2 + NE)

    def probs_of(logits):
        lm = jnp.where(is_logit, logits, NEG)
        ex = jnp.where(is_logit, jnp.exp(lm - jnp.max(lm, axis=-1, keepdims=True)), 0.0)
        return ex / jnp.sum(ex, axis=-1, keepdims=True)

    @pl.loop(0, 4)
    def _(rb):
        rows = pl.ds(pl.multiple_of(rb * 128, 128), 128)
        h = tok[rows].astype(F32) + nn(obuf[rows], wo[:, :D])
        hid[rows] = h
        r2 = lax.rsqrt(jnp.mean(h * h, axis=-1, keepdims=True) + EPS)
        u = (h * r2 * gain2).astype(BF16)
        u2[rows] = u
        pr = probs_of(nn(u, wo[:, D:]))
        prob[rows] = pr
        hot = (lane - 2) == cols[rows, 8:9].astype(jnp.int32)
        gate = jnp.sum(jnp.where(hot, pr, 0.0), axis=-1, keepdims=True)
        gobuf[rows] = (gate * cot[rows].astype(F32)).astype(BF16)

    def xg_send(kind, e):
        if kind == 0:
            return remote(xg.at[dp, e], xg.at[dp, e], xs.at[0, e], xr.at[dp, e], x_d)
        if kind == 1:
            return remote(xg.at[dp, e], xg.at[dp, e], xs.at[1, e], xr.at[dp, e], core_d)
        return remote(xg.at[dpx, e], xg.at[dpx, e], xs.at[2, e], xr.at[dpx, e], core_d)

    def xg_arrival(dpi, e):
        return remote(xg.at[dpi, e], xg.at[dpi, e], xs.at[0, e], xr.at[dpi, e], x_d)

    for e in range(NE):
        hot = jnp.where(iota((CAP, LONG), 0) + e * CAP == code_row[...], 1.0, 0.0).astype(BF16)
        xg[dp, e, 0] = nn(hot, u2[...]).astype(BF16)
        xg[dp, e, 1] = nn(hot, gobuf[...]).astype(BF16)
        xg_send(0, e).start()
        xg_send(1, e).start()

    for m in range(2):
        for st in (1, 2, 3):
            s3_forward(m, 1, st)
    s3_issue(3)

    def yc_send(xi, e):
        return remote(xg.at[xi * 2 + cn, e], ycore.at[xi, e], ycs.at[xi, e], ycr.at[xi, e], core_d)

    def yx_send(e):
        return remote(xg.at[dpx, e], yx.at[e], yxs.at[e], yxr.at[e], x_d)

    def dy_send(m, e):
        return remote(wb.at[m, e, :, yn], ry.at[m, e], dys.at[m, e], dyr.at[m, e], y_d)

    def dz_send(m, e, st):
        return remote(
            wb.at[m, e, zz_of(st), y], rz.at[m, e, st - 1], dzs.at[m, e, st - 1], dzr.at[m, e, st - 1], z_d(st)
        )

    def sum_x(e):
        for xi in range(2):
            yc_send(xi, e).wait_recv()
        xg[dpx, e] = (xg[dpx, e].astype(F32) + ycore[xn, e].astype(F32)).astype(BF16)
        yx_send(e).start()

    def sum_z(e):
        for m in range(2):
            dy_send(m, e).wait_recv()
            for st in (1, 2, 3, 0):
                zi = zz_of(st)
                wb[m, e, zi, y] = (wb[m, e, zi, y].astype(F32) + ry[m, e, zi].astype(F32)).astype(BF16)
                if st:
                    dz_send(m, e, st).start()

    def fin_copy(number):
        e, m = number // 2, number % 2
        return pltpu.make_async_copy(fin.at[m], (wi_grad if m == 0 else wo_grad).at[e], fsem.at[m])

    def grad_final(e):
        for m in range(2):
            total = wb[m, e, z, y].astype(F32)
            for st in (1, 2, 3):
                dz_send(m, e, st).wait_recv()
                total = total + rz[m, e, st - 1].astype(F32)
            number = e * 2 + m
            if number >= 2:
                fin_copy(number - 2).wait()
            fin[m] = total
            fin_copy(number).start()

    def forward_x(e):
        xg_arrival(dpx, e).wait_recv()
        xg_send(2, e).start()

    forward_x(0)
    for e in range(NE):
        xg_arrival(dpc, e).wait_recv()
        xg_arrival(xn * 2 + cn, e).wait_recv()
        s3_finish(e)
        for kind in range(3):
            xg_send(kind, e).wait_send()
        s3_sent(e)
        half = 4 * 96
        for fc in range(2):
            zs = slice(2 * fc, 2 * fc + 2)
            xv = xg[:, e, 0].reshape(4 * CAP, D)
            gv = xg[:, e, 1].reshape(4 * CAP, D)
            wi_v = wb[0, e, zs].reshape(half, D)
            wo_v = wb[1, e, zs].reshape(half, D)
            zv = nt(xv, wi_v)
            ga = nt(gv, wo_v)
            t = jnp.tanh(GELU_C * (zv + 0.044715 * (zv * zv * zv)))
            act = (0.5 * zv * (1.0 + t)).astype(BF16)
            slope = 0.5 * (1.0 + t) + (0.5 * GELU_C) * zv * (1.0 - t * t) * (
                1.0 + (3 * 0.044715) * (zv * zv)
            )
            gz = (ga * slope).astype(BF16)
            if fc == 0:
                yacc = nn(act, wo_v)
                gacc = nn(gz, wi_v)
                pst_y, pst_g = yacc, gacc
            else:
                pst_y = pst_y + nn(act, wo_v)
                pst_g = pst_g + nn(gz, wi_v)
            wb[1, e, zs] = tn(act, gv).astype(BF16).reshape(2, 2, 96, D)
            wb[0, e, zs] = tn(gz, xv).astype(BF16).reshape(2, 2, 96, D)
            if fc == 0 and e < NE - 1:
                forward_x(e + 1)
        xg[:, e, 0] = pst_y.astype(BF16).reshape(4, CAP, D)
        xg[:, e, 1] = pst_g.astype(BF16).reshape(4, CAP, D)
        for xi in range(2):
            yc_send(xi, e).start()
        for m in range(2):
            dy_send(m, e).start()
        if e < 2:
            for m in range(2):
                for st in (1, 2, 3):
                    s3_forward(m, e + 2, st)
        if e >= 1:
            sum_x(e - 1)
        if e >= 2:
            sum_z(e - 2)
    sum_x(NE - 1)

    for e in range(NE):
        yx_send(e).wait_recv()
        xg[dp, e] = (xg[dp, e].astype(F32) + ycore[x, e].astype(F32) + yx[e].astype(F32)).astype(BF16)
    gd[0:8] = jnp.zeros((8, D), F32)

    @pl.loop(0, 4)
    def _(rb):
        rows = pl.ds(pl.multiple_of(rb * 128, 128), 128)
        code_col = cols[rows, 0:1].astype(jnp.int32)
        back = jnp.where(iota((128, NE * CAP), 1) == code_col, 1.0, 0.0).astype(BF16)
        yt = nn(back, xg[dp, :, 0].reshape(NE * CAP, D))
        gxt = nn(back, xg[dp, :, 1].reshape(NE * CAP, D))
        h = hid[rows]
        g = cot[rows].astype(F32)
        pr = prob[rows]
        hot = (lane - 2) == cols[rows, 8:9].astype(jnp.int32)
        gate = jnp.sum(jnp.where(hot, pr, 0.0), axis=-1, keepdims=True)
        layer_out[rows] = (h + gate * yt).astype(BF16)
        ggate = jnp.sum(g * yt, axis=-1, keepdims=True)
        dprob = jnp.where(hot, ggate, 0.0)
        dlog = pr * (dprob - jnp.sum(pr * dprob, axis=-1, keepdims=True))
        prob[rows] = dlog
        hi = dlog.astype(BF16)
        lo = (dlog - hi.astype(F32)).astype(BF16)
        wr_t = sm_t[...].astype(BF16)
        gu = gxt + nn(hi, wr_t) + nn(lo, wr_t)
        r2 = lax.rsqrt(jnp.mean(h * h, axis=-1, keepdims=True) + EPS)
        n2 = h * r2
        gd[1:2] = gd[1:2] + jnp.sum(gu * n2, axis=0, keepdims=True)
        mm = gu * gain2
        gh = g + r2 * (mm - n2 * jnp.mean(mm * n2, axis=-1, keepdims=True))
        hid[rows] = gh
        ghb = gh.astype(BF16)
        gobuf[rows] = nt(ghb, wo[:, :D]).astype(BF16)
        tokens_grad[rows] = ghb

    dlog = prob[...]
    dlog_hi = dlog.astype(BF16)
    router_part = tn(u2[...], dlog_hi) + tn(u2[...], (dlog - dlog_hi.astype(F32)).astype(BF16))

    for e in range(NE):
        for xi in range(2):
            yc_send(xi, e).wait_send()
        yx_send(e).wait_send()
    pl.semaphore_wait(free, len(peers))

    def pack(unit, lanes, width, value):
        for d in range(32):
            xg[d // 8, d % 8 // 2, d % 2, unit * 32 : unit * 32 + 24, lanes] = value[
                24 * d : 24 * d + 24
            ].astype(BF16)

    def lands(unit):
        if unit == 4:
            return lsc, lsx, lsy, lsz
        if unit == 3:
            full = pl.ds(0, D)
            return (
                ar.at[0:2, :, :, :, full], ar.at[2, :, :, :, full],
                ar.at[3, :, 0, :, full], ar.at[3, 0:3, 1, :, full],
            )
        return aq.at[0:2, :, :, unit], aq.at[2, :, :, unit], aq.at[3, :, 0, unit], aq.at[3, 0:3, 1, unit]

    def part_ref(unit):
        if unit == 4:
            return smallp
        return xg.at[:, :, :, pl.ds(unit * 32, 24), :]

    def narrow(unit, v):
        return v if unit == 4 else v.astype(BF16)

    def rs_core(unit, xi):
        return remote(
            part_ref(unit).at[xi * 2 + cn], lands(unit)[0].at[xi], rcs.at[unit, xi], rcr.at[unit, xi], core_d
        )

    def rs_x(unit):
        return remote(part_ref(unit).at[dpx], lands(unit)[1], rxs.at[unit], rxr.at[unit], x_d)

    def rs_y(unit):
        return remote(part_ref(unit).at[dp, :, yn], lands(unit)[2], rys.at[unit], ryr.at[unit], y_d)

    def rs_z(unit, st):
        dst = lands(unit)[3].at[z] if unit == 4 else lands(unit)[3].at[st - 1]
        return remote(
            part_ref(unit).at[dp, zz_of(st), y], dst, rzs.at[unit, st - 1], rzr.at[unit, st - 1], z_d(st)
        )

    def st_core(unit):
        for xi in range(2):
            rs_core(unit, xi).start()

    def st_x(unit):
        mine, (lc, _, _, _) = part_ref(unit), lands(unit)
        for xi in range(2):
            rs_core(unit, xi).wait_recv()
        for zi in range(4):
            mine[dpx, zi] = narrow(unit, mine[dpx, zi].astype(F32) + lc[xn, zi].astype(F32))
        rs_x(unit).start()

    def st_y(unit):
        mine, (lc, lx, _, _) = part_ref(unit), lands(unit)
        rs_x(unit).wait_recv()
        for zi in range(4):
            mine[dp, zi] = narrow(
                unit, mine[dp, zi].astype(F32) + lc[x, zi].astype(F32) + lx[zi].astype(F32)
            )
        rs_y(unit).start()

    def st_z(unit):
        mine, (_, _, ly, _) = part_ref(unit), lands(unit)
        rs_y(unit).wait_recv()
        for zi in range(4):
            mine[dp, zi, y] = narrow(unit, mine[dp, zi, y].astype(F32) + ly[zi].astype(F32))
        for st in (1, 2, 3):
            rs_z(unit, st).start()

    def st_final(unit):
        mine, (_, _, _, lz) = part_ref(unit), lands(unit)
        for st in (1, 2, 3):
            rs_z(unit, st).wait_recv()
        if unit == 4:
            lz[z] = mine[dp, z, y]
            return (lz[0] + lz[1]) + (lz[2] + lz[3])
        total = mine[dp, z, y].astype(F32)
        for st in (1, 2, 3):
            total = total + lz[st - 1].astype(F32)
        return total

    def st_sent(unit):
        for xi in range(2):
            rs_core(unit, xi).wait_send()
        rs_x(unit).wait_send()
        rs_y(unit).wait_send()
        for st in (1, 2, 3):
            rs_z(unit, st).wait_send()

    for half in range(2):
        lanes = slice(half * 384, half * 384 + 384)
        pack(3, lanes, 384, tn(obuf[...], tokens_grad[:, lanes]))
    st_core(3)
    sum_z(2)

    relg[0] = jnp.zeros((16, 256), F32)
    relg[1] = jnp.zeros((16, 256), F32)
    relg[2] = jnp.zeros((16, 256), F32)
    p_copy(4, True).wait()
    p_copy(5, True).wait()
    p_copy(0, False).start()

    def backward(hp):
        slot = hp % 2
        s, base = hp // 2, (hp % 2) * 384
        p_copy(hp, False).wait()
        if hp < 5:
            p_copy(hp + 1, False).start()
        q2 = qkvb[s, :, base : base + 128]
        k2 = qkvb[s, :, base + 128 : base + 256]
        v2 = qkvb[s, :, base + 256 : base + 384]
        go2 = gobuf[:, hp * 128 : hp * 128 + 128]
        eighth = jnp.asarray(0.125, BF16)
        for h2 in range(2):
            head = hp * 2 + h2
            qm = head_mask(q2, h2) * eighth
            km = head_mask(k2, h2) * eighth
            gm = head_mask(go2, h2)
            tiles = [None] * 5
            for bi in range(4):
                rows = slice(bi * 128, bi * 128 + 128)
                pv = pst[slot, h2, rows].astype(F32)
                dpv = nt(gm[rows], v2)
                ds = pv * (dpv - jnp.sum(pv * dpv, axis=-1, keepdims=True))
                dst_s[rows] = ds.astype(BF16)
                for bj in range(4):
                    kind = 0 if bj == bi else 1 if bj == bi + 1 else 2 if bj == bi - 1 else 4 if bj > bi else 3
                    tile = ds[:, bj * 128 : bj * 128 + 128]
                    tiles[kind] = tile if tiles[kind] is None else tiles[kind] + tile
            for kind in range(3):
                relg[kind, head : head + 1, :] = diagonal_sums(tiles[kind])
            relg[3, head : head + 1, 128:256] = jnp.sum(tiles[3], axis=0, keepdims=True)
            relg[4, head : head + 1, 0:128] = jnp.sum(tiles[4], axis=0, keepdims=True)
            dsb = dst_s[...]
            dq = nn(dsb, km)
            dk = tn(dsb, qm)
            dv = tn(pst[slot, h2], gm)
            if h2 == 0:
                grad3 = [dq, dk, dv]
            else:
                grad3 = [a + b for a, b in zip(grad3, (dq, dk, dv))]
        for k in range(3):
            qkvb[s, :, base + k * 128 : base + k * 128 + 128] = grad3[k].astype(BF16)
        pack(s, slice(base, base + 384), 384, tn(u1[...], qkvb[s, :, base : base + 384]))

    backward(0)
    st_x(3)
    backward(1)
    st_core(0)
    st_y(3)
    sum_z(3)
    backward(2)
    st_x(0)
    st_z(3)
    backward(3)
    st_core(1)
    st_y(0)
    backward(4)
    st_x(1)
    st_z(0)
    backward(5)
    st_core(2)
    st_y(1)

    @pl.loop(0, 4)
    def _(rb):
        rows = pl.ds(pl.multiple_of(rb * 128, 128), 128)
        gu = nt(qkvb[0, rows], wq[0]) + nt(qkvb[1, rows], wq[1]) + nt(qkvb[2, rows], wq[2])
        xf = tok[rows].astype(F32)
        r1 = lax.rsqrt(jnp.mean(xf * xf, axis=-1, keepdims=True) + EPS)
        n1 = xf * r1
        gd[0:1] = gd[0:1] + jnp.sum(gu * n1, axis=0, keepdims=True)
        mm = gu * gain1
        grad = hid[rows] + r1 * (mm - n1 * jnp.mean(mm * n1, axis=-1, keepdims=True))
        tokens_grad[rows] = grad.astype(BF16)

    st_x(2)
    st_z(1)

    gains = jnp.concatenate([gd[0:8], jnp.zeros((120, D), F32)], axis=0)
    gain_cols = jnp.transpose(gains)
    lane768 = iota((D, 128), 1)
    small_cols = jnp.where(lane768 < 2, gain_cols, jnp.where(lane768 < 2 + NE, router_part, 0.0))
    table = jnp.zeros((16, BUCKETS), F32)
    for kind in range(3):
        table = table + exact(relg[kind], bucket_hot(kind, 1), ((1,), (0,)))
    far_b = iota((128, BUCKETS), 1)
    table = table + exact(
        relg[3, :, 128:256], jnp.where(far_b == BUCKETS // 2 - 1, 1.0, 0.0), ((1,), (0,))
    )
    table = table + exact(relg[4, :, 0:128], jnp.where(far_b == BUCKETS - 1, 1.0, 0.0), ((1,), (0,)))
    extra = jnp.concatenate(
        [
            jnp.zeros((16, 32), F32),
            table,
            relg[3, :, 64:128],
        ],
        axis=1,
    )
    extra = jnp.concatenate([extra, jnp.zeros((8, 128), F32)], axis=0)
    for d in range(32):
        smallp[d // 8, d % 8 // 2, d % 2] = small_cols[24 * d : 24 * d + 24] + extra
    st_core(4)
    st_y(2)
    st_x(4)
    grad_final(0)
    grad_final(1)
    st_z(2)
    st_y(4)
    grad_final(2)
    out_grad[...] = st_final(3)
    st_z(4)

    def write_qkv(unit):
        total = st_final(unit)
        for half in range(2):
            for k in range(3):
                qkv_grad[:, k * D + (2 * unit + half) * 128 : k * D + (2 * unit + half) * 128 + 128] = total[
                    :, half * 384 + k * 128 : half * 384 + k * 128 + 128
                ]

    write_qkv(0)
    write_qkv(1)
    grad_final(3)
    write_qkv(2)
    small_grad[...] = st_final(4)
    fin_copy(2 * NE - 2).wait()
    fin_copy(2 * NE - 1).wait()

    for e in range(NE):
        for m in range(2):
            dy_send(m, e).wait_send()
            for st in (1, 2, 3):
                dz_send(m, e, st).wait_send()
    for unit in range(5):
        st_sent(unit)


def fused(
    tokens, bucket_len, valid, routes, attn_gain, qkv_weight, out_weight, rel, ffn_gain, router_weight,
    w_in, w_out, cotangent,
):
    tok_n, D = tokens.shape
    small = jnp.concatenate(
        [attn_gain[:, None], ffn_gain[:, None], router_weight, jnp.zeros((attn_gain.shape[0], 122), BF16)], axis=1
    )
    vm = pl.BlockSpec(memory_space=pltpu.VMEM)
    hbm = pl.BlockSpec(memory_space=pl.ANY)
    sds = jax.ShapeDtypeStruct
    V = pltpu.VMEM
    sem = lambda *s: pltpu.SemaphoreType.DMA(s)
    outs = pl.pallas_call(
        layer_kernel,
        out_shape=(
            sds((512, 768), BF16), sds((512, 768), BF16), sds((24, 2304), F32), sds((24, 768), F32),
            sds((24, 128), F32), sds((4, 96, 768), F32), sds((4, 96, 768), F32), sds((6, 2, 512, 512), BF16),
        ),
        in_specs=[vm, vm, vm, vm, pl.BlockSpec(memory_space=pltpu.SMEM), vm, vm, vm, vm, hbm, hbm],
        out_specs=(vm,) * 5 + (hbm,) * 3,
        scratch_shapes=[
            V((4, 4, 2, 3, 24, 768), BF16),
            V((4, 4, 2, 24, 896), BF16),
            V((3, 768, 768), BF16),
            V((768, 896), BF16),
            V((128, 768), F32),
            V((2, 4, 4, 2, 96, 768), BF16),
            V((4, 4, 2, 160, 768), BF16),
            V((2, 4, 2, 160, 768), BF16),
            V((4, 2, 160, 768), BF16),
            V((2, 4, 4, 96, 768), BF16),
            V((2, 4, 3, 96, 768), BF16),
            V((3, 512, 768), BF16),
            V((512, 768), BF16),
            V((512, 768), BF16),
            V((512, 768), BF16),
            V((512, 768), BF16),
            V((512, 768), F32),
            V((512, 128), F32),
            V((1, 512), jnp.int32),
            V((512, 128), F32),
            V((8, 512), F32),
            V((12, 8, 256), F32),
            V((3, 128, 128), F32),
            V((2, 2, 512, 512), BF16),
            V((512, 512), BF16),
            V((8, 768), F32),
            V((5, 16, 256), F32),
            V((4, 4, 2, 24, 128), F32),
            V((2, 4, 2, 24, 128), F32),
            V((4, 2, 24, 128), F32),
            V((4, 24, 128), F32),
            V((4, 24, 128), F32),
            V((2, 96, 768), F32),
            pltpu.SemaphoreType.REGULAR,
            sem(2, 31), sem(2, 32), sem(2, 4, 3), sem(2, 4, 4), sem(2, 4, 4, 2), sem(2, 4),
            sem(3, 4), sem(4, 4), sem(2, 4), sem(2, 4), sem(4), sem(4), sem(2, 4), sem(2, 4),
            sem(2, 4, 3), sem(2, 4, 3),
            sem(5, 2), sem(5, 2), sem(5), sem(5), sem(5), sem(5), sem(5, 3), sem(5, 4), sem(2), sem(2),
        ],
        compiler_params=pltpu.CompilerParams(
            collective_id=0, has_side_effects=True, vmem_limit_bytes=VMEM_LIMIT
        ),
        cost_estimate=pl.CostEstimate(flops=40_000_000_000, bytes_accessed=30_000_000, transcendentals=8_000_000),
    )(
        tokens, cotangent, routes.reshape(1, tok_n), valid.reshape(1, tok_n), bucket_len, rel,
        qkv_weight, out_weight, small, jnp.transpose(w_in, (1, 0, 2)), jnp.transpose(w_out, (1, 0, 2)),
    )
    lo, tg, qg, og, sg, wig, wog, _ = outs
    counts = sg[:4, 64:66].astype(jnp.int32)
    return (
        lo, tg, sg[:, 0], qg, og, sg[:12, 32:64], sg[:, 1], sg[:, 2:6],
        jnp.transpose(wig, (1, 0, 2)), jnp.transpose(wog, (1, 0, 2)), counts[:, 0], counts[:, 1],
    )


epsilon = 1e-06


def bucket_codes(block_span, bucket_count, reach):
    position = jnp.arange(block_span, dtype=jnp.int32)
    offset_grid = position[None, :] - position[:, None]
    distance = jnp.abs(offset_grid)
    halfway = bucket_count // 2
    exact_span = halfway // 2
    distant = jnp.full(offset_grid.shape, exact_span, jnp.int32)
    for number in range(1, halfway - exact_span):
        threshold = math.ceil(
            exact_span * (reach / exact_span) ** (number / (halfway - exact_span))
        )
        distant = distant + (distance >= threshold).astype(jnp.int32)
    return jnp.where(distance < exact_span, distance, distant) + jnp.where(
        offset_grid > 0, halfway, 0
    )


def block_allowed(length, live_block):
    position = jnp.arange(live_block.shape[0], dtype=jnp.int32)
    segment = position // length
    return (segment[:, None] == segment[None, :]) & (live_block[None, :] > 0)


def rms_forward(values, gain_vector):
    inverse = lax.rsqrt(jnp.mean(values * values, axis=-1, keepdims=True) + epsilon)
    normed = values * inverse
    return (normed, inverse, normed * gain_vector)


def rms_backward(normed, inverse, gain_vector, grad_scaled):
    weighted = grad_scaled * gain_vector
    return inverse * (weighted - normed * jnp.mean(weighted * normed, axis=-1, keepdims=True))


def split_heads(block_rows):
    block_span = block_rows.shape[0]
    model_width = block_rows.shape[1] // 3
    head_size = model_width // HEADS
    return tuple(
        (
            block_rows[:, part_index * model_width : (part_index + 1) * model_width].reshape(
                block_span, HEADS, head_size
            )
            for part_index in range(3)
        )
    )


def block_scores(queries, keys_part, complete_position_bias, allowed):
    score_scale = queries.shape[-1] ** (-0.5)
    scores = (
        jnp.einsum("qhd,khd->hqk", queries, keys_part, preferred_element_type=jnp.float32)
        * score_scale
        + complete_position_bias
    )
    return jnp.where(allowed[None], scores, -1e30)


def attend_forward(complete_position_bias, packed):
    block_rows, length, live_block = packed
    queries, keys_part, values_part = split_heads(block_rows)
    scores = block_scores(
        queries, keys_part, complete_position_bias, block_allowed(length, live_block)
    )
    row_peak = jnp.max(scores, axis=-1, keepdims=True)
    exponent = jnp.exp(scores - row_peak)
    row_total = jnp.sum(exponent, axis=-1, keepdims=True)
    weights_low = (exponent / row_total).astype(jnp.bfloat16)
    mixed_rows = jnp.einsum(
        "hqk,khd->qhd", weights_low, values_part, preferred_element_type=jnp.float32
    )
    return (
        mixed_rows.reshape(block_rows.shape[0], -1).astype(jnp.bfloat16),
        (row_peak + jnp.log(row_total))[..., 0],
    )


def attend_backward(complete_position_bias, bucket_indicator, packed):
    block_rows, length, live_block, grad_mixed, log_total = packed
    queries, keys_part, values_part = split_heads(block_rows)
    scores = block_scores(
        queries, keys_part, complete_position_bias, block_allowed(length, live_block)
    )
    probs_full = jnp.exp(scores - log_total[:, :, None])
    grad_heads = grad_mixed.reshape(queries.shape)
    grad_probs = jnp.einsum(
        "qhd,khd->hqk", grad_heads, values_part, preferred_element_type=jnp.float32
    )
    score_gradient_rows = (
        probs_full * (grad_probs - jnp.sum(probs_full * grad_probs, axis=-1, keepdims=True))
    ).astype(jnp.bfloat16)
    score_scale = queries.shape[-1] ** (-0.5)
    grad_queries = (
        jnp.einsum(
            "hqk,khd->qhd", score_gradient_rows, keys_part, preferred_element_type=jnp.float32
        )
        * score_scale
    )
    grad_keys = (
        jnp.einsum("hqk,qhd->khd", score_gradient_rows, queries, preferred_element_type=jnp.float32)
        * score_scale
    )
    grad_values = jnp.einsum(
        "hqk,qhd->khd",
        probs_full.astype(jnp.bfloat16),
        grad_heads,
        preferred_element_type=jnp.float32,
    )
    table_grad = jnp.einsum(
        "wif,nif->wn", score_gradient_rows, bucket_indicator, preferred_element_type=jnp.float32
    )
    block_span = block_rows.shape[0]
    joined = jnp.concatenate(
        [
            grad_queries.reshape(block_span, -1),
            grad_keys.reshape(block_span, -1),
            grad_values.reshape(block_span, -1),
        ],
        axis=1,
    )
    return (joined.astype(jnp.bfloat16), table_grad)


def per_device(
    tokens,
    bucket_len,
    valid,
    routes,
    attn_gain,
    qkv_weight,
    out_weight,
    relative_head_bias,
    ffn_gain,
    router_weight,
    w_in,
    w_out,
    cotangent,
):
    top_probability = lax.Precision.HIGHEST
    gain_attn, weight_qkv, weight_out, gain_ffn, weight_router = (
        lax.all_gather(attn_gain, ("dp", "fsdp"), axis=0, tiled=True),
        lax.all_gather(qkv_weight, ("dp", "fsdp"), axis=0, tiled=True),
        lax.all_gather(out_weight, ("dp", "fsdp"), axis=0, tiled=True),
        lax.all_gather(ffn_gain, ("dp", "fsdp"), axis=0, tiled=True),
        lax.all_gather(router_weight, ("dp", "fsdp"), axis=0, tiled=True),
    )
    expert_in, expert_out = (
        lax.all_gather(w_in, "fsdp", axis=0, tiled=True),
        lax.all_gather(w_out, "fsdp", axis=0, tiled=True),
    )
    token_count, model_width = tokens.shape
    block_total = token_count // LONG
    expert_count = expert_in.shape[1]
    capacity = (5 * token_count + 4 * expert_count - 1) // (4 * expert_count)
    bucket_grid = bucket_codes(LONG, BUCKETS, MAXDIST)
    selected_bucket = bucket_grid[None] == jnp.arange(BUCKETS, dtype=jnp.int32)[:, None, None]
    bucket_indicator = selected_bucket.astype(jnp.bfloat16)
    complete_position_bias = jnp.einsum(
        "eo,ozm->ezm",
        relative_head_bias,
        selected_bucket.astype(jnp.float32),
        precision=top_probability,
    )
    live_blocks = valid.reshape(block_total, LONG)
    rows_in = tokens.astype(jnp.float32)
    normed_one, inverse_one, scaled_one = rms_forward(rows_in, gain_attn.astype(jnp.float32))
    normed_low = scaled_one.astype(jnp.bfloat16)
    qkv_low = jnp.dot(normed_low, weight_qkv, preferred_element_type=jnp.float32).astype(
        jnp.bfloat16
    )
    qkv_blocks = qkv_low.reshape(block_total, LONG, 3 * model_width)
    mixed_blocks, log_totals = lax.map(
        partial(attend_forward, complete_position_bias), (qkv_blocks, bucket_len, live_blocks)
    )
    mixed_low = mixed_blocks.reshape(token_count, model_width)
    hidden = rows_in + jnp.dot(mixed_low, weight_out, preferred_element_type=jnp.float32)
    normed_two, inverse_two, scaled_two = rms_forward(hidden, gain_ffn.astype(jnp.float32))
    normed_two_low = scaled_two.astype(jnp.bfloat16)
    normed_two_full = normed_two_low.astype(jnp.float32)
    router_probs = jax.nn.softmax(
        jnp.dot(normed_two_full, weight_router.astype(jnp.float32), precision=top_probability),
        axis=-1,
    )
    chosen = routes[:, 0]
    route_hot = chosen[:, None] == jnp.arange(expert_count, dtype=jnp.int32)[None, :]
    gate_value = jnp.sum(jnp.where(route_hot, router_probs, 0.0), axis=1)
    surviving_rows = valid > 0
    route_picks = route_hot & surviving_rows[:, None]
    places = jnp.cumsum(route_picks.astype(jnp.int32), axis=0) - 1
    slot_place = jnp.sum(jnp.where(route_picks, places, 0), axis=1)
    kept_rows = surviving_rows & (slot_place < capacity)
    slot_code = jnp.where(kept_rows, chosen * capacity + slot_place, 0)
    slot_match = (
        jnp.arange(expert_count * capacity, dtype=jnp.int32)[:, None]
        == jnp.where(kept_rows, slot_code, -1)[None, :]
    )
    slot_filled = jnp.any(slot_match, axis=1)
    slot_token = jnp.sum(
        jnp.where(slot_match, jnp.arange(token_count, dtype=jnp.int32)[None, :], 0), axis=1
    )
    slot_rows = jnp.where(
        slot_filled[:, None], normed_two_low[slot_token], jnp.zeros((), jnp.bfloat16)
    ).reshape(expert_count, capacity, model_width)
    slot_rows = lax.all_gather(slot_rows, "dp", axis=1, tiled=True)
    expert_inner = jnp.einsum(
        "ecd,fed->ecf", slot_rows, expert_in, preferred_element_type=jnp.float32
    )
    active_low = jax.nn.gelu(expert_inner, approximate=True).astype(jnp.bfloat16)
    result_low = (
        lax.psum_scatter(
            jnp.einsum("ecf,fed->ecd", active_low, expert_out, preferred_element_type=jnp.float32),
            "dp",
            scatter_dimension=1,
            tiled=True,
        )
        .astype(jnp.bfloat16)
        .reshape(expert_count * capacity, model_width)
    )
    returned = jnp.where(kept_rows[:, None], result_low[slot_code].astype(jnp.float32), 0.0)
    layer_out = (hidden + gate_value[:, None] * returned).astype(jnp.bfloat16)
    sent_local = jnp.sum((route_picks & kept_rows[:, None]).astype(jnp.int32), axis=0)
    lost_local = jnp.sum((route_picks & ~kept_rows[:, None]).astype(jnp.int32), axis=0)
    count_sums = lax.psum(jnp.stack([sent_local, lost_local]), ("dp", "fsdp"))
    grad_out = cotangent.astype(jnp.float32)
    grad_gate = jnp.sum(grad_out * returned, axis=1)
    grad_back = gate_value[:, None] * grad_out
    grad_result = (
        jnp.where(slot_filled[:, None], grad_back[slot_token], 0.0)
        .astype(jnp.bfloat16)
        .reshape(expert_count, capacity, model_width)
    )
    grad_result = lax.all_gather(grad_result, "dp", axis=1, tiled=True)
    grad_active = jnp.einsum(
        "ecd,fed->ecf", grad_result, expert_out, preferred_element_type=jnp.float32
    )
    unused_value, gelu_pullback = jax.vjp(partial(jax.nn.gelu, approximate=True), expert_inner)
    grad_inner = gelu_pullback(grad_active)[0].astype(jnp.bfloat16)
    grad_slots = lax.psum_scatter(
        jnp.einsum("ecf,fed->ecd", grad_inner, expert_in, preferred_element_type=jnp.float32),
        "dp",
        scatter_dimension=1,
        tiled=True,
    ).reshape(expert_count * capacity, model_width)
    grad_normed_two = jnp.where(kept_rows[:, None], grad_slots[slot_code], 0.0)
    grad_probs = jnp.where(route_hot, grad_gate[:, None], 0.0)
    grad_logits = router_probs * (
        grad_probs - jnp.sum(router_probs * grad_probs, axis=1, keepdims=True)
    )
    grad_normed_two = grad_normed_two + jnp.dot(
        grad_logits, weight_router.astype(jnp.float32).T, precision=top_probability
    )
    grad_hidden = (
        rms_backward(normed_two, inverse_two, gain_ffn.astype(jnp.float32), grad_normed_two)
        + grad_out
    )
    grad_hidden_low = grad_hidden.astype(jnp.bfloat16)
    grad_mixed = jnp.dot(grad_hidden_low, weight_out.T, preferred_element_type=jnp.float32).astype(
        jnp.bfloat16
    )
    joined_blocks, table_grads = lax.map(
        partial(attend_backward, complete_position_bias, bucket_indicator),
        (
            qkv_blocks,
            bucket_len,
            live_blocks,
            grad_mixed.reshape(block_total, LONG, model_width),
            log_totals,
        ),
    )
    grad_qkv = joined_blocks.reshape(token_count, 3 * model_width)
    grad_normed_one = jnp.dot(grad_qkv, weight_qkv.T, preferred_element_type=jnp.float32)
    grad_rows = rms_backward(
        normed_one, inverse_one, gain_attn.astype(jnp.float32), grad_normed_one
    )
    tokens_grad = (grad_rows + grad_hidden).astype(jnp.bfloat16)
    table_grad = lax.psum(jnp.sum(table_grads, axis=0), ("dp", "fsdp"))
    attn_term = jnp.sum(grad_normed_one * normed_one, axis=0)
    qkv_term = jnp.dot(normed_low.T, grad_qkv, preferred_element_type=jnp.float32)
    out_term = jnp.dot(mixed_low.T, grad_hidden_low, preferred_element_type=jnp.float32)
    ffn_term = jnp.sum(grad_normed_two * normed_two, axis=0)
    router_term = jnp.dot(normed_two_full.T, grad_logits, precision=top_probability)
    layer_summed = lax.psum_scatter(
        jnp.concatenate(
            [attn_term[:, None], qkv_term, out_term, ffn_term[:, None], router_term], axis=1
        ),
        ("dp", "fsdp"),
        scatter_dimension=0,
        tiled=True,
    )
    out_term = jnp.einsum(
        "ecf,ecd->fed", active_low, grad_result, preferred_element_type=jnp.float32
    )
    in_term = jnp.einsum("ecd,ecf->fed", slot_rows, grad_inner, preferred_element_type=jnp.float32)
    w_in_grad = lax.psum_scatter(in_term, "fsdp", scatter_dimension=0, tiled=True)
    w_out_grad = lax.psum_scatter(out_term, "fsdp", scatter_dimension=0, tiled=True)
    attn_gain_grad = layer_summed[:, 0]
    qkv_grad = layer_summed[:, 1 : 1 + 3 * model_width]
    out_grad = layer_summed[:, 1 + 3 * model_width : 1 + 4 * model_width]
    ffn_gain_grad = layer_summed[:, 1 + 4 * model_width]
    router_weight_gradient = layer_summed[:, 2 + 4 * model_width :]
    return (
        layer_out,
        tokens_grad,
        attn_gain_grad,
        qkv_grad,
        out_grad,
        table_grad,
        ffn_gain_grad,
        router_weight_gradient,
        w_in_grad,
        w_out_grad,
        count_sums[0],
        count_sums[1],
    )


def solution(mesh):
    both = ("dp", "fsdp")
    body = fused if (mesh.shape["dp"], mesh.shape["fsdp"]) == (4, 8) else per_device
    placed = (
        P(both, None), P(both), P(both), P(both, None), P(both), P(both, None), P(both, None), P(), P(both),
        P(both, None), P(both, None, None), P(both, None, None), P(both, None),
    )
    return jax.shard_map(
        body,
        mesh=mesh,
        in_specs=placed,
        out_specs=(
            P(both, None), P(both, None), P(both), P(both, None), P(both, None), P(), P(both), P(both, None),
            P(both, None, None), P(both, None, None), P(), P(),
        ),
        check_vma=False,
    )
```

```python
from functools import partial
import math

import jax
import jax.numpy as jnp
from jax import lax
from jax.experimental import pallas as pl
from jax.experimental.pallas import tpu as pltpu
from jax.sharding import PartitionSpec as P

F32 = jnp.float32
BF16 = jnp.bfloat16
MESH = pl.DeviceIdType.MESH

HEADS = 12
BUCKETS = 32
MAXDIST = 128
LONG = 512
NEG = -1e30
EPS = 1e-06
GELU_C = math.sqrt(2.0 / math.pi)


def nt(a, b):
    return lax.dot_general(a, b, (((1,), (1,)), ((), ())), preferred_element_type=F32)


def nn(a, b):
    return lax.dot_general(a, b, (((1,), (0,)), ((), ())), preferred_element_type=F32)


def tn(a, b):
    return lax.dot_general(a, b, (((0,), (0,)), ((), ())), preferred_element_type=F32)


def exact(a, b, dims):
    return lax.dot_general(
        a, b, (dims, ((), ())), precision=lax.Precision.HIGHEST, preferred_element_type=F32
    )


def iota(shape, axis):
    return lax.broadcasted_iota(jnp.int32, shape, axis)


def bucket_of(offset):
    distance = jnp.abs(offset)
    halfway = BUCKETS // 2
    exact_span = halfway // 2
    distant = jnp.full(offset.shape, exact_span, jnp.int32)
    for number in range(1, halfway - exact_span):
        threshold = math.ceil(
            exact_span * (MAXDIST / exact_span) ** (number / (halfway - exact_span))
        )
        distant = distant + jnp.where(distance >= threshold, 1, 0)
    return jnp.where(distance < exact_span, distance, distant) + jnp.where(offset > 0, halfway, 0)


def diagonal_sums(tile):
    wide = jnp.concatenate([tile, jnp.zeros((128, 128), F32)], axis=1)
    rows = 64
    while rows >= 8:
        wide = wide[:rows] + pltpu.roll(wide[rows : 2 * rows], 256 - rows, 1)
        rows //= 2
    while rows >= 1:
        wide = wide + pltpu.roll(pltpu.roll(wide, 256 - rows, 1), 8 - rows, 0)
        rows //= 2
    return wide[0:1]


VMEM_LIMIT = 63 << 20


def layer_kernel(
    tok, cot, routes, valid, length, rel, gain_a, gain_f, rshard, qshard, oshard, wi_hbm, wo_hbm,
    layer_out, tokens_grad, qkv_grad, out_grad, small_grad, wi_grad, wo_grad, p_hbm,
    aq, ar, ao, wq, wo, sm_t, wb, xg, ycore, yx, ry, rz,
    qkvb, u1, obuf, u2, gobuf, hid, prob, code_row, cols, key_mask, tab, bias, pst, dst_s, gd, relg,
    smallp, lsc, lsx, lsy, lsz, fin,
    free,
    s1s, s1r, s3zs, s3ys, s3r, s3l, xs, xr, ycs, ycr, yxs, yxr, dys, dyr, dzs, dzr,
    rcs, rcr, rxs, rxr, rys, ryr, rzs, rzr, psem, fsem,
):
    dp = lax.axis_index("dp")
    fs = lax.axis_index("fsdp")
    x, c = dp // 2, lax.rem(dp, 2)
    z, y = fs // 2, lax.rem(fs, 2)
    xn, cn, yn = 1 - x, 1 - c, 1 - y
    NZ = 4
    NE = 4
    CAP = 160
    D = 768

    def at(xx, cc, zz, yy):
        return (xx * 2 + cc, zz * 2 + yy)

    core_d, x_d, y_d = at(x, cn, z, y), at(xn, c, z, y), at(x, c, z, yn)

    def zz_of(step):
        return lax.rem(z + step, NZ)

    def zb_of(step):
        return lax.rem(z - step + NZ, NZ)

    def z_d(step):
        return at(x, c, zz_of(step), y)

    def remote(src, dst, ss, rs, where):
        return pltpu.make_async_remote_copy(
            src_ref=src, dst_ref=dst, send_sem=ss, recv_sem=rs, device_id=where, device_id_type=MESH
        )

    for s in range(3):
        for half in range(2):
            for k in range(3):
                lanes = slice(half * 384 + k * 128, half * 384 + k * 128 + 128)
                piece = qshard[:, k * D + (2 * s + half) * 128 : k * D + (2 * s + half) * 128 + 128]
                if s < 2:
                    aq[dp, z, y, s, :, lanes] = piece
                else:
                    ar[dp, z, y, :, lanes] = piece
    ao[dp, z, y] = oshard[...]
    diagonal = iota((24, 24), 0) == iota((24, 24), 1)
    gain_cols = [
        jnp.sum(jnp.where(diagonal, g[...].astype(F32), 0.0), axis=1, keepdims=True) for g in (gain_a, gain_f)
    ]
    lane24 = iota((24, 128), 1)
    place4 = jnp.where(iota((NE, 128), 1) == iota((NE, 128), 0) + 2, 1.0, 0.0).astype(BF16)
    small = jnp.where(lane24 == 0, gain_cols[0], jnp.where(lane24 == 1, gain_cols[1], nn(rshard[...], place4)))
    ar[dp, z, y, :, D:] = small.astype(BF16)

    barrier = pltpu.get_barrier_semaphore()
    peers = [core_d, x_d, y_d, z_d(1), z_d(2), z_d(3)]
    for peer in peers:
        pl.semaphore_signal(barrier, inc=1, device_id=peer, device_id_type=MESH)
    pl.semaphore_wait(barrier, len(peers))

    def s1(part, slot, dpi, zi, yi, where):
        ref = (aq, ar, ao)[part].at[dpi, zi, yi]
        return remote(ref, ref, s1s.at[part, slot], s1r.at[part, dpi * 8 + zi * 2 + yi], where)

    started = ([], [], [])

    def go(part, *rest):
        copy = s1(part, *rest)
        copy.start()
        started[part].append(copy)

    dpx, dpc, dpd = xn * 2 + c, x * 2 + cn, xn * 2 + cn

    def s1_spread(part, st, zi):
        go(part, 3 + st, dp, zi, y, y_d)
        go(part, 7 + st, dp, zi, y, x_d)
        go(part, 15 + st, dp, zi, y, core_d)

    def s1_z(part, st):
        s1(part, 0, dp, zb_of(st), y, y_d).wait_recv()
        s1_spread(part, st, zb_of(st))

    def s1_second(part, st):
        zi = zb_of(st)
        if part == 0:
            s1(part, 0, dp, zi, yn, y_d).wait_recv()
            go(part, 11 + st, dp, zi, yn, x_d)
            go(part, 19 + st, dp, zi, yn, core_d)
        else:
            s1(part, 0, dpx, zi, y, x_d).wait_recv()
            go(part, 11 + st, dpx, zi, y, y_d)
            go(part, 19 + st, dpx, zi, y, core_d)

    def s1_third(part, st):
        zi = zb_of(st)
        for number, yi in ((0, y), (1, yn)):
            if part == 0:
                dpi, yj, where = dpx, yi, x_d
            else:
                dpi, yj, where = (dp, dpx)[number], yn, y_d
            s1(part, 0, dpi, zi, yj, where).wait_recv()
            go(part, 23 + number * 4 + st, dpi, zi, yj, core_d)

    def s1_end(part):
        for dpi in (dpc, dpd):
            for yi in range(2):
                for zi in range(4):
                    s1(part, 0, dpi, zi, yi, core_d).wait_recv()
        for copy in started[part]:
            copy.wait_send()

    for part in (0, 1):
        for st in (1, 2, 3):
            go(part, st - 1, dp, z, y, z_d(st))
        s1_spread(part, 0, z)

    LAST = 2 * NE - 1
    up_d, down_d = at(x, c, jnp.minimum(z + 1, NZ - 1), y), at(x, c, jnp.maximum(z - 1, 0), y)

    def s3_src(m, e):
        return (wi_hbm if m == 0 else wo_hbm).at[e]

    def s3_own(m, e):
        return pltpu.make_async_copy(s3_src(m, e), wb.at[m, e, z, y], s3l.at[m, e])

    def s3_y0(m, e):
        return remote(s3_src(m, e), wb.at[m, e, z, y], s3ys.at[m, e, 0], s3r.at[m, e, z, y], y_d)

    def s3_y(m, e, zi):
        ref = wb.at[m, e, zi, y]
        return remote(ref, ref, s3ys.at[m, e, lax.rem(zi - z + NZ, NZ)], s3r.at[m, e, zi, y], y_d)

    def s3_arrival(m, e, zi, yi):
        ref = wb.at[m, e, zi, yi]
        return remote(ref, ref, s3ys.at[m, e, 0], s3r.at[m, e, zi, yi], y_d)

    def s3_line(m, e, zi, yi, way, slot, src=None):
        dst = wb.at[m, e, zi, yi]
        return remote(
            dst if src is None else src, dst, s3zs.at[m, e, way * 8 + slot], s3r.at[m, e, zi, yi], (up_d, down_d)[way]
        )

    def onward(way):
        return z < NZ - 1 if way == 0 else z > 0

    def s3_issue_line():
        for i in range(2 * NE):
            m, e = i % 2, i // 2
            for way in (0, 1):
                pl.when(onward(way))(lambda: s3_line(m, e, z, y, way, 0, s3_src(m, e)).start())
            s3_own(m, e).start()

    def s3_issue_y():
        for i in range(2 * NE):
            s3_y0(i % 2, i // 2).start()

    def s3_pair(i, dist, across=False):
        m, e = (i % 2, i // 2) if isinstance(i, int) else (lax.rem(i, 2), i // 2)
        yi = yn if across else y
        for way in (0, 1):
            zi = z - dist if way == 0 else z + dist
            here = zi >= 0 if way == 0 else zi < NZ
            zi = jnp.clip(zi, 0, NZ - 1)

            @pl.when(here)
            def _():
                s3_arrival(m, e, zi, yi).wait_recv()

                @pl.when(onward(way))
                def _():
                    s3_line(m, e, zi, yi, way, dist + (4 if across else 0)).start()

                if not (isinstance(i, int) and i == LAST):
                    s3_y(m, e, zi).start()

    def s3_across():
        m, e = 1, NE - 1
        s3_arrival(m, e, z, yn).wait_recv()
        for way in (0, 1):
            pl.when(onward(way))(lambda: s3_line(m, e, z, yn, way, 4).start())

    def s3_finish(e):
        for m in range(2):
            s3_own(m, e).wait()
            if 2 * e + m != LAST:
                for st in range(4):
                    s3_arrival(m, e, zz_of(st), yn).wait_recv()

    def s3_sent(e):
        for m in range(2):
            last = 2 * e + m == LAST
            s3_y0(m, e).wait_send()
            for st in (1, 2, 3):
                if not last:
                    s3_y(m, e, zz_of(st)).wait_send()
            for way in (0, 1):
                for dist in range(4):
                    origin = z >= dist if way == 0 else z + dist < NZ
                    for slot in (dist, dist + 4)[: 2 if last else 1]:
                        pl.when(origin & onward(way))(lambda: s3_line(m, e, z, y, way, slot).wait_send())

    route_v = routes[...]
    live_v = valid[...] > 0
    picks = jnp.where((iota((8, LONG), 0) == route_v) & live_v, 1.0, 0.0)
    upto = jnp.where(iota((LONG, LONG), 0) <= iota((LONG, LONG), 1), 1.0, 0.0).astype(BF16)
    counts = nn(picks.astype(BF16), upto)
    place = jnp.sum(picks * counts, axis=0, keepdims=True).astype(jnp.int32) - 1
    kept = live_v & (place < CAP)
    code = jnp.where(kept, route_v * CAP + place, -1)
    code_row[...] = code
    keptf = jnp.where(kept, 1.0, 0.0)
    sent = jnp.sum(picks * keptf, axis=1, keepdims=True)
    lost = jnp.sum(picks * (1.0 - keptf), axis=1, keepdims=True)
    lane128 = iota((8, 128), 1)
    relg[3] = jnp.zeros((16, 256), F32)
    relg[3, 0:8, 0:128] = jnp.where(lane128 == 64, sent, 0.0) + jnp.where(lane128 == 65, lost, 0.0)
    stacked = jnp.concatenate(
        [
            jnp.broadcast_to(code.astype(F32), (8, LONG)),
            jnp.broadcast_to(route_v.astype(F32), (8, LONG)),
            jnp.zeros((112, LONG), F32),
        ],
        axis=0,
    )
    cols[...] = jnp.transpose(stacked)
    same = (iota((8, LONG), 1) // 128 == iota((8, LONG), 0)) | (length[0] >= LONG)
    key_mask[...] = jnp.where(same & live_v, 0.0, NEG)

    for st in (1, 2, 3):
        for part in (0, 1):
            s1_z(part, st)
    for st in (1, 2, 3):
        go(2, st - 1, dp, z, y, z_d(st))
    s3_issue_line()

    rel16 = jnp.concatenate([rel[...], jnp.zeros((4, BUCKETS), F32)], axis=0)

    def bucket_hot(kind, axis):
        shape = (BUCKETS, 256) if axis == 0 else (256, BUCKETS)
        lane = iota(shape, 1 - axis)
        offset = jnp.where(lane < 128, lane, lane - 256) + (0, 128, -128)[kind]
        return jnp.where(bucket_of(offset) == iota(shape, axis), 1.0, 0.0)

    rows_by_kind = [exact(rel16, bucket_hot(kind, 0), ((1,), (0,))) for kind in range(3)]
    for b in (BUCKETS // 2 - 1, BUCKETS - 1):
        rows_by_kind.append(exact(rel16, jnp.where(iota((BUCKETS, 256), 0) == b, 1.0, 0.0), ((1,), (0,))))
    for head in range(HEADS):
        for kind in range(5):
            tab[head, kind : kind + 1, :] = rows_by_kind[kind][head : head + 1]

    for st in range(4):
        for part in (0, 1):
            s1_second(part, st)
    for st in range(4):
        for part in (0, 1):
            s1_third(part, st)
    for part in (0, 1):
        s1_end(part)
    s1_spread(2, 0, z)
    for st in (1, 2, 3):
        s1_z(2, st)
    s3_issue_y()
    for pair in range(3):
        s3_pair(0, 1 + pair)

    @pl.loop(0, 4)
    def _(dpi):
        for zi in range(4):
            base = pl.multiple_of((dpi * 8 + zi * 2) * 24, 16)
            for s in range(2):
                v = aq[dpi, zi, :, s].astype(F32).reshape(48, D)
                wq[s, pl.ds(base, 48)] = v.astype(BF16)
            v = ar[dpi, zi].astype(F32).reshape(48, D + 128).astype(BF16)
            wq[2, pl.ds(base, 48)] = v[:, :D]
            wo[pl.ds(base, 48), D:] = v[:, D:]

    sm_t[...] = jnp.transpose(wo[:, D:].astype(F32))
    gain1 = sm_t[0:1, :]
    gain2 = sm_t[1:2, :]

    @pl.loop(0, 4)
    def _(rb):
        rows = pl.ds(pl.multiple_of(rb * 128, 128), 128)
        xf = tok[rows].astype(F32)
        r1 = lax.rsqrt(jnp.mean(xf * xf, axis=-1, keepdims=True) + EPS)
        u1[rows] = (xf * r1 * gain1).astype(BF16)

    for s in range(3):
        qkvb[s] = nn(u1[...], wq[s]).astype(BF16)

    lane_low = iota((LONG, 128), 1) < 64

    def head_mask(v, h2):
        return jnp.where(lane_low if h2 == 0 else ~lane_low, v, jnp.zeros((), v.dtype))

    def p_copy(hp, out):
        slot = lax.rem(hp, 2)
        if out:
            return pltpu.make_async_copy(pst.at[slot], p_hbm.at[hp], psem.at[slot])
        return pltpu.make_async_copy(p_hbm.at[hp], pst.at[slot], psem.at[slot])

    def forward(hp):
        slot = lax.rem(hp, 2)
        s, base = hp // 2, pl.multiple_of(lax.rem(hp, 2) * 384, 128)
        q2 = qkvb[s, :, pl.ds(base, 128)]
        k2 = qkvb[s, :, pl.ds(base + 128, 128)]
        v2 = qkvb[s, :, pl.ds(base + 256, 128)]

        @pl.when(hp >= 2)
        def _():
            p_copy(hp, True).wait()

        for h2 in range(2):
            head = hp * 2 + h2
            qm = head_mask(q2, h2) * jnp.asarray(0.125, BF16)
            vm = head_mask(v2, h2)
            for kind in range(3):
                row = tab[head, kind : kind + 1, :]
                tile = pltpu.roll(jnp.broadcast_to(row, (128, 256)), 0, 1, stride=1, stride_axis=0)
                bias[kind] = tile[:, :128]
            left = jnp.broadcast_to(tab[head, 3:4, 0:128], (128, 128))
            right = jnp.broadcast_to(tab[head, 4:5, 0:128], (128, 128))
            for bi in range(4):
                rows = slice(bi * 128, bi * 128 + 128)
                sc = nt(qm[rows], k2)
                tiles = [
                    bias[0] if bj == bi else bias[1] if bj == bi + 1 else bias[2] if bj == bi - 1
                    else right if bj > bi else left
                    for bj in range(4)
                ]
                sc = sc + jnp.concatenate(tiles, axis=1) + key_mask[bi : bi + 1, :]
                peak = jnp.max(sc, axis=-1, keepdims=True)
                ex = jnp.exp(sc - peak)
                p = (ex * (1.0 / jnp.sum(ex, axis=-1, keepdims=True))).astype(BF16)
                pst[slot, h2, rows] = p
                part = nn(p, vm)
                if h2 == 0:
                    hid[rows, 0:128] = part
                else:
                    obuf[rows, pl.ds(pl.multiple_of(hp * 128, 128), 128)] = (
                        hid[rows, 0:128] + part
                    ).astype(BF16)
        p_copy(hp, True).start()
        for number in range(2):
            pair = 3 + 2 * hp + number
            s3_pair(pair // 3, 1 + lax.rem(pair, 3))


    pl.loop(0, 2)(forward)
    for st in range(4):
        s1_second(2, st)
    pl.loop(2, 4)(forward)
    for st in range(4):
        s1_third(2, st)
    pl.loop(4, HEADS // 2)(forward)
    s1_end(2)
    s3_across()
    @pl.loop(0, 4)
    def _(dpi):
        for zi in range(4):
            base = pl.multiple_of((dpi * 8 + zi * 2) * 24, 16)
            wo[pl.ds(base, 48), :D] = ao[dpi, zi].astype(F32).reshape(48, D).astype(BF16)

    for peer in peers:
        pl.semaphore_signal(free, inc=1, device_id=peer, device_id_type=MESH)

    lane = iota((128, 128), 1)
    is_logit = (lane >= 2) & (lane < 2 + NE)

    def probs_of(logits):
        lm = jnp.where(is_logit, logits, NEG)
        ex = jnp.where(is_logit, jnp.exp(lm - jnp.max(lm, axis=-1, keepdims=True)), 0.0)
        return ex / jnp.sum(ex, axis=-1, keepdims=True)

    @pl.loop(0, 4)
    def _(rb):
        rows = pl.ds(pl.multiple_of(rb * 128, 128), 128)
        h = tok[rows].astype(F32) + nn(obuf[rows], wo[:, :D])
        hid[rows] = h
        r2 = lax.rsqrt(jnp.mean(h * h, axis=-1, keepdims=True) + EPS)
        u = (h * r2 * gain2).astype(BF16)
        u2[rows] = u
        pr = probs_of(nn(u, wo[:, D:]))
        prob[rows] = pr
        hot = (lane - 2) == cols[rows, 8:9].astype(jnp.int32)
        gate = jnp.sum(jnp.where(hot, pr, 0.0), axis=-1, keepdims=True)
        gobuf[rows] = (gate * cot[rows].astype(F32)).astype(BF16)

    def xg_send(kind, e):
        if kind == 0:
            return remote(xg.at[dp, e], xg.at[dp, e], xs.at[0, e], xr.at[dp, e], x_d)
        if kind == 1:
            return remote(xg.at[dp, e], xg.at[dp, e], xs.at[1, e], xr.at[dp, e], core_d)
        return remote(xg.at[dpx, e], xg.at[dpx, e], xs.at[2, e], xr.at[dpx, e], core_d)

    def xg_arrival(dpi, e):
        return remote(xg.at[dpi, e], xg.at[dpi, e], xs.at[0, e], xr.at[dpi, e], x_d)

    for e in range(NE):
        hot = jnp.where(iota((CAP, LONG), 0) + e * CAP == code_row[...], 1.0, 0.0).astype(BF16)
        xg[dp, e, 0] = nn(hot, u2[...]).astype(BF16)
        xg[dp, e, 1] = nn(hot, gobuf[...]).astype(BF16)
        xg_send(0, e).start()
        xg_send(1, e).start()

    for dist in (1, 2, 3):
        s3_pair(5, dist)

    def yc_send(xi, e):
        return remote(xg.at[xi * 2 + cn, e], ycore.at[xi, e], ycs.at[xi, e], ycr.at[xi, e], core_d)

    def yx_send(e):
        return remote(xg.at[dpx, e], yx.at[e], yxs.at[e], yxr.at[e], x_d)

    def dy_send(m, e):
        return remote(wb.at[m, e, :, yn], ry.at[m, e], dys.at[m, e], dyr.at[m, e], y_d)

    z1 = z + 1 - 2 * lax.rem(z, 2)
    z2 = zz_of(2)
    z3 = lax.rem(z1 + 2, NZ)

    def dz_send(m, e, slot):
        zi, zd = ((z1, z1), (z3, z1), (z2, z2))[slot]
        return remote(
            wb.at[m, e, zi, y], rz.at[m, e, slot], dzs.at[m, e, slot], dzr.at[m, e, slot], at(x, c, zd, y)
        )

    def sum_x(e):
        for xi in range(2):
            yc_send(xi, e).wait_recv()
        xg[dpx, e] = (xg[dpx, e].astype(F32) + ycore[xn, e].astype(F32)).astype(BF16)
        yx_send(e).start()

    def sum_z(e):
        for m in range(2):
            dy_send(m, e).wait_recv()
            for zi, slot in ((z3, 1), (z1, 0), (z2, None), (z, None)):
                wb[m, e, zi, y] = (wb[m, e, zi, y].astype(F32) + ry[m, e, zi].astype(F32)).astype(BF16)
                if slot is not None:
                    dz_send(m, e, slot).start()

    def sum_w(e):
        for m in range(2):
            dz_send(m, e, 1).wait_recv()
            wb[m, e, z2, y] = (wb[m, e, z2, y].astype(F32) + rz[m, e, 1].astype(F32)).astype(BF16)
            dz_send(m, e, 2).start()

    def fin_copy(number):
        e, m = number // 2, number % 2
        return pltpu.make_async_copy(fin.at[m], (wi_grad if m == 0 else wo_grad).at[e], fsem.at[m])

    def grad_final(e):
        for m in range(2):
            total = wb[m, e, z, y].astype(F32)
            for slot in (0, 2):
                dz_send(m, e, slot).wait_recv()
                total = total + rz[m, e, slot].astype(F32)
            number = e * 2 + m
            if number >= 2:
                fin_copy(number - 2).wait()
            fin[m] = total
            fin_copy(number).start()

    def forward_x(e):
        xg_arrival(dpx, e).wait_recv()
        xg_send(2, e).start()

    PAIRS = (
        ((6, 1),), ((6, 2),), ((6, 3),), ((LAST, 1), (LAST, 1, True)),
        ((LAST, 2), (LAST, 2, True)), ((LAST, 3), (LAST, 3, True)), (), (),
    )
    forward_x(0)
    for e in range(NE):
        xg_arrival(dpc, e).wait_recv()
        xg_arrival(xn * 2 + cn, e).wait_recv()
        s3_finish(e)
        for kind in range(3):
            xg_send(kind, e).wait_send()
        s3_sent(e)
        half = 4 * 96
        for fc in range(2):
            zs = slice(2 * fc, 2 * fc + 2)
            xv = xg[:, e, 0].reshape(4 * CAP, D)
            gv = xg[:, e, 1].reshape(4 * CAP, D)
            wi_v = wb[0, e, zs].reshape(half, D)
            wo_v = wb[1, e, zs].reshape(half, D)
            zv = nt(xv, wi_v)
            ga = nt(gv, wo_v)
            t = jnp.tanh(GELU_C * (zv + 0.044715 * (zv * zv * zv)))
            act = (0.5 * zv * (1.0 + t)).astype(BF16)
            slope = 0.5 * (1.0 + t) + (0.5 * GELU_C) * zv * (1.0 - t * t) * (
                1.0 + (3 * 0.044715) * (zv * zv)
            )
            gz = (ga * slope).astype(BF16)
            if fc == 0:
                yacc = nn(act, wo_v)
                gacc = nn(gz, wi_v)
                pst_y, pst_g = yacc, gacc
            else:
                pst_y = pst_y + nn(act, wo_v)
                pst_g = pst_g + nn(gz, wi_v)
            wb[1, e, zs] = tn(act, gv).astype(BF16).reshape(2, 2, 96, D)
            wb[0, e, zs] = tn(gz, xv).astype(BF16).reshape(2, 2, 96, D)
            if fc == 0 and e < NE - 1:
                forward_x(e + 1)
            for pair in PAIRS[e * 2 + fc]:
                s3_pair(*pair)
        xg[:, e, 0] = pst_y.astype(BF16).reshape(4, CAP, D)
        xg[:, e, 1] = pst_g.astype(BF16).reshape(4, CAP, D)
        for xi in range(2):
            yc_send(xi, e).start()
        for m in range(2):
            dy_send(m, e).start()
        if e >= 1:
            sum_x(e - 1)
        if e >= 2:
            sum_z(e - 2)
        if e >= 3:
            sum_w(e - 3)
    sum_x(NE - 1)

    for e in range(NE):
        yx_send(e).wait_recv()
        xg[dp, e] = (xg[dp, e].astype(F32) + ycore[x, e].astype(F32) + yx[e].astype(F32)).astype(BF16)
    gd[0:8] = jnp.zeros((8, D), F32)

    @pl.loop(0, 4)
    def _(rb):
        rows = pl.ds(pl.multiple_of(rb * 128, 128), 128)
        code_col = cols[rows, 0:1].astype(jnp.int32)
        back = jnp.where(iota((128, NE * CAP), 1) == code_col, 1.0, 0.0).astype(BF16)
        yt = nn(back, xg[dp, :, 0].reshape(NE * CAP, D))
        gxt = nn(back, xg[dp, :, 1].reshape(NE * CAP, D))
        h = hid[rows]
        g = cot[rows].astype(F32)
        pr = prob[rows]
        hot = (lane - 2) == cols[rows, 8:9].astype(jnp.int32)
        gate = jnp.sum(jnp.where(hot, pr, 0.0), axis=-1, keepdims=True)
        layer_out[rows] = (h + gate * yt).astype(BF16)
        ggate = jnp.sum(g * yt, axis=-1, keepdims=True)
        dprob = jnp.where(hot, ggate, 0.0)
        dlog = pr * (dprob - jnp.sum(pr * dprob, axis=-1, keepdims=True))
        prob[rows] = dlog
        hi = dlog.astype(BF16)
        lo = (dlog - hi.astype(F32)).astype(BF16)
        wr_t = sm_t[...].astype(BF16)
        gu = gxt + nn(hi, wr_t) + nn(lo, wr_t)
        r2 = lax.rsqrt(jnp.mean(h * h, axis=-1, keepdims=True) + EPS)
        n2 = h * r2
        gd[1:2] = gd[1:2] + jnp.sum(gu * n2, axis=0, keepdims=True)
        mm = gu * gain2
        gh = g + r2 * (mm - n2 * jnp.mean(mm * n2, axis=-1, keepdims=True))
        hid[rows] = gh
        ghb = gh.astype(BF16)
        gobuf[rows] = nt(ghb, wo[:, :D]).astype(BF16)
        tokens_grad[rows] = ghb

    dlog = prob[...]
    dlog_hi = dlog.astype(BF16)
    router_part = tn(u2[...], dlog_hi) + tn(u2[...], (dlog - dlog_hi.astype(F32)).astype(BF16))

    for e in range(NE):
        for xi in range(2):
            yc_send(xi, e).wait_send()
        yx_send(e).wait_send()
    pl.semaphore_wait(free, len(peers))

    def pack(unit, lanes, width, value):
        for d in range(32):
            xg[d // 8, d % 8 // 2, d % 2, unit * 32 : unit * 32 + 24, lanes] = value[
                24 * d : 24 * d + 24
            ].astype(BF16)

    def lands(unit):
        if unit == 4:
            return lsc, lsx, lsy, lsz
        if unit == 3:
            return ao.at[0:2], ao.at[2], ao.at[3, :, 0], ao.at[3, 0:3, 1]
        if unit == 2:
            full = pl.ds(0, D)
            return (
                ar.at[0:2, :, :, :, full], ar.at[2, :, :, :, full],
                ar.at[3, :, 0, :, full], ar.at[3, 0:3, 1, :, full],
            )
        return aq.at[0:2, :, :, unit], aq.at[2, :, :, unit], aq.at[3, :, 0, unit], aq.at[3, 0:3, 1, unit]

    def part_ref(unit):
        if unit == 4:
            return smallp
        return xg.at[:, :, :, pl.ds(unit * 32, 24), :]

    def narrow(unit, v):
        return v if unit == 4 else v.astype(BF16)

    def rs_core(unit, xi):
        return remote(
            part_ref(unit).at[xi * 2 + cn], lands(unit)[0].at[xi], rcs.at[unit, xi], rcr.at[unit, xi], core_d
        )

    def rs_x(unit):
        return remote(part_ref(unit).at[dpx], lands(unit)[1], rxs.at[unit], rxr.at[unit], x_d)

    def rs_y(unit):
        return remote(part_ref(unit).at[dp, :, yn], lands(unit)[2], rys.at[unit], ryr.at[unit], y_d)

    def rs_z(unit, st):
        dst = lands(unit)[3].at[z] if unit == 4 else lands(unit)[3].at[st - 1]
        return remote(
            part_ref(unit).at[dp, zz_of(st), y], dst, rzs.at[unit, st - 1], rzr.at[unit, st - 1], z_d(st)
        )

    def st_core(unit):
        for xi in range(2):
            rs_core(unit, xi).start()

    def st_x(unit):
        mine, (lc, _, _, _) = part_ref(unit), lands(unit)
        for xi in range(2):
            rs_core(unit, xi).wait_recv()
        for zi in range(4):
            mine[dpx, zi] = narrow(unit, mine[dpx, zi].astype(F32) + lc[xn, zi].astype(F32))
        rs_x(unit).start()

    def st_y(unit):
        mine, (lc, lx, _, _) = part_ref(unit), lands(unit)
        rs_x(unit).wait_recv()
        for zi in range(4):
            mine[dp, zi] = narrow(
                unit, mine[dp, zi].astype(F32) + lc[x, zi].astype(F32) + lx[zi].astype(F32)
            )
        rs_y(unit).start()

    def st_z(unit):
        mine, (_, _, ly, _) = part_ref(unit), lands(unit)
        rs_y(unit).wait_recv()
        for zi in range(4):
            mine[dp, zi, y] = narrow(unit, mine[dp, zi, y].astype(F32) + ly[zi].astype(F32))
        for st in (1, 2, 3):
            rs_z(unit, st).start()

    def st_final(unit):
        mine, (_, _, _, lz) = part_ref(unit), lands(unit)
        for st in (1, 2, 3):
            rs_z(unit, st).wait_recv()
        if unit == 4:
            lz[z] = mine[dp, z, y]
            return (lz[0] + lz[1]) + (lz[2] + lz[3])
        total = mine[dp, z, y].astype(F32)
        for st in (1, 2, 3):
            total = total + lz[st - 1].astype(F32)
        return total

    def st_sent(unit):
        for xi in range(2):
            rs_core(unit, xi).wait_send()
        rs_x(unit).wait_send()
        rs_y(unit).wait_send()
        for st in (1, 2, 3):
            rs_z(unit, st).wait_send()

    for half in range(2):
        lanes = slice(half * 384, half * 384 + 384)
        pack(3, lanes, 384, tn(obuf[...], tokens_grad[:, lanes]))
    st_core(3)
    sum_z(2)
    sum_w(1)

    relg[0] = jnp.zeros((16, 256), F32)
    relg[1] = jnp.zeros((16, 256), F32)
    relg[2] = jnp.zeros((16, 256), F32)
    p_copy(4, True).wait()
    p_copy(5, True).wait()
    p_copy(0, False).start()

    def backward(hp):
        slot = hp % 2
        s, base = hp // 2, (hp % 2) * 384
        p_copy(hp, False).wait()
        if hp < 5:
            p_copy(hp + 1, False).start()
        q2 = qkvb[s, :, base : base + 128]
        k2 = qkvb[s, :, base + 128 : base + 256]
        v2 = qkvb[s, :, base + 256 : base + 384]
        go2 = gobuf[:, hp * 128 : hp * 128 + 128]
        eighth = jnp.asarray(0.125, BF16)
        for h2 in range(2):
            head = hp * 2 + h2
            qm = head_mask(q2, h2) * eighth
            km = head_mask(k2, h2) * eighth
            gm = head_mask(go2, h2)
            tiles = [None] * 5
            for bi in range(4):
                rows = slice(bi * 128, bi * 128 + 128)
                pv = pst[slot, h2, rows].astype(F32)
                dpv = nt(gm[rows], v2)
                ds = pv * (dpv - jnp.sum(pv * dpv, axis=-1, keepdims=True))
                dst_s[rows] = ds.astype(BF16)
                for bj in range(4):
                    kind = 0 if bj == bi else 1 if bj == bi + 1 else 2 if bj == bi - 1 else 4 if bj > bi else 3
                    tile = ds[:, bj * 128 : bj * 128 + 128]
                    tiles[kind] = tile if tiles[kind] is None else tiles[kind] + tile
            for kind in range(3):
                relg[kind, head : head + 1, :] = diagonal_sums(tiles[kind])
            relg[3, head : head + 1, 128:256] = jnp.sum(tiles[3], axis=0, keepdims=True)
            relg[4, head : head + 1, 0:128] = jnp.sum(tiles[4], axis=0, keepdims=True)
            dsb = dst_s[...]
            dq = nn(dsb, km)
            dk = tn(dsb, qm)
            dv = tn(pst[slot, h2], gm)
            if h2 == 0:
                grad3 = [dq, dk, dv]
            else:
                grad3 = [a + b for a, b in zip(grad3, (dq, dk, dv))]
        for k in range(3):
            qkvb[s, :, base + k * 128 : base + k * 128 + 128] = grad3[k].astype(BF16)
        pack(s, slice(base, base + 384), 384, tn(u1[...], qkvb[s, :, base : base + 384]))

    backward(0)
    st_x(3)
    backward(1)
    st_core(0)
    st_y(3)
    sum_z(3)
    sum_w(2)
    backward(2)
    st_x(0)
    st_z(3)
    backward(3)
    st_core(1)
    st_y(0)
    backward(4)
    sum_w(3)
    st_x(1)
    st_z(0)
    backward(5)
    st_core(2)
    st_y(1)

    @pl.loop(0, 4)
    def _(rb):
        rows = pl.ds(pl.multiple_of(rb * 128, 128), 128)
        gu = nt(qkvb[0, rows], wq[0]) + nt(qkvb[1, rows], wq[1]) + nt(qkvb[2, rows], wq[2])
        xf = tok[rows].astype(F32)
        r1 = lax.rsqrt(jnp.mean(xf * xf, axis=-1, keepdims=True) + EPS)
        n1 = xf * r1
        gd[0:1] = gd[0:1] + jnp.sum(gu * n1, axis=0, keepdims=True)
        mm = gu * gain1
        grad = hid[rows] + r1 * (mm - n1 * jnp.mean(mm * n1, axis=-1, keepdims=True))
        tokens_grad[rows] = grad.astype(BF16)

    st_x(2)
    st_z(1)

    gains = jnp.concatenate([gd[0:8], jnp.zeros((120, D), F32)], axis=0)
    gain_cols = jnp.transpose(gains)
    lane768 = iota((D, 128), 1)
    small_cols = jnp.where(lane768 < 2, gain_cols, jnp.where(lane768 < 2 + NE, router_part, 0.0))
    table = jnp.zeros((16, BUCKETS), F32)
    for kind in range(3):
        table = table + exact(relg[kind], bucket_hot(kind, 1), ((1,), (0,)))
    far_b = iota((128, BUCKETS), 1)
    table = table + exact(
        relg[3, :, 128:256], jnp.where(far_b == BUCKETS // 2 - 1, 1.0, 0.0), ((1,), (0,))
    )
    table = table + exact(relg[4, :, 0:128], jnp.where(far_b == BUCKETS - 1, 1.0, 0.0), ((1,), (0,)))
    extra = jnp.concatenate(
        [
            jnp.zeros((16, 32), F32),
            table,
            relg[3, :, 64:128],
        ],
        axis=1,
    )
    extra = jnp.concatenate([extra, jnp.zeros((8, 128), F32)], axis=0)
    for d in range(32):
        smallp[d // 8, d % 8 // 2, d % 2] = small_cols[24 * d : 24 * d + 24] + extra
    st_core(4)
    st_y(2)
    st_x(4)
    grad_final(0)
    grad_final(1)
    st_z(2)
    st_y(4)
    grad_final(2)
    out_grad[...] = st_final(3)
    st_z(4)

    def write_qkv(unit):
        total = st_final(unit)
        for half in range(2):
            for k in range(3):
                qkv_grad[:, k * D + (2 * unit + half) * 128 : k * D + (2 * unit + half) * 128 + 128] = total[
                    :, half * 384 + k * 128 : half * 384 + k * 128 + 128
                ]

    write_qkv(0)
    write_qkv(1)
    grad_final(3)
    write_qkv(2)
    small_grad[...] = st_final(4)
    fin_copy(2 * NE - 2).wait()
    fin_copy(2 * NE - 1).wait()

    for e in range(NE):
        for m in range(2):
            dy_send(m, e).wait_send()
            for slot in range(3):
                dz_send(m, e, slot).wait_send()
    for unit in range(5):
        st_sent(unit)


def fused(
    tokens, bucket_len, valid, routes, attn_gain, qkv_weight, out_weight, rel, ffn_gain, router_weight,
    w_in, w_out, cotangent,
):
    tok_n, D = tokens.shape
    vm = pl.BlockSpec(memory_space=pltpu.VMEM)
    hbm = pl.BlockSpec(memory_space=pl.ANY)
    sds = jax.ShapeDtypeStruct
    V = pltpu.VMEM
    sem = lambda *s: pltpu.SemaphoreType.DMA(s)
    outs = pl.pallas_call(
        layer_kernel,
        out_shape=(
            sds((512, 768), BF16), sds((512, 768), BF16), sds((24, 2304), F32), sds((24, 768), F32),
            sds((24, 128), F32), sds((4, 96, 768), F32), sds((4, 96, 768), F32), sds((6, 2, 512, 512), BF16),
        ),
        in_specs=[vm, vm, vm, vm, pl.BlockSpec(memory_space=pltpu.SMEM), vm, vm, vm, vm, vm, vm, hbm, hbm],
        out_specs=(vm,) * 5 + (hbm,) * 3,
        scratch_shapes=[
            V((4, 4, 2, 2, 24, 768), BF16),
            V((4, 4, 2, 24, 896), BF16),
            V((4, 4, 2, 24, 768), BF16),
            V((3, 768, 768), BF16),
            V((768, 896), BF16),
            V((128, 768), F32),
            V((2, 4, 4, 2, 96, 768), BF16),
            V((4, 4, 2, 160, 768), BF16),
            V((2, 4, 2, 160, 768), BF16),
            V((4, 2, 160, 768), BF16),
            V((2, 4, 4, 96, 768), BF16),
            V((2, 4, 3, 96, 768), BF16),
            V((3, 512, 768), BF16),
            V((512, 768), BF16),
            V((512, 768), BF16),
            V((512, 768), BF16),
            V((512, 768), BF16),
            V((512, 768), F32),
            V((512, 128), F32),
            V((1, 512), jnp.int32),
            V((512, 128), F32),
            V((8, 512), F32),
            V((12, 8, 256), F32),
            V((3, 128, 128), F32),
            V((2, 2, 512, 512), BF16),
            V((512, 512), BF16),
            V((8, 768), F32),
            V((5, 16, 256), F32),
            V((4, 4, 2, 24, 128), F32),
            V((2, 4, 2, 24, 128), F32),
            V((4, 2, 24, 128), F32),
            V((4, 24, 128), F32),
            V((4, 24, 128), F32),
            V((2, 96, 768), F32),
            pltpu.SemaphoreType.REGULAR,
            sem(3, 31), sem(3, 32), sem(2, 4, 16), sem(2, 4, 4), sem(2, 4, 4, 2), sem(2, 4),
            sem(3, 4), sem(4, 4), sem(2, 4), sem(2, 4), sem(4), sem(4), sem(2, 4), sem(2, 4),
            sem(2, 4, 3), sem(2, 4, 3),
            sem(5, 2), sem(5, 2), sem(5), sem(5), sem(5), sem(5), sem(5, 3), sem(5, 4), sem(2), sem(2),
        ],
        compiler_params=pltpu.CompilerParams(
            collective_id=0, has_side_effects=True, vmem_limit_bytes=VMEM_LIMIT
        ),
        cost_estimate=pl.CostEstimate(flops=40_000_000_000, bytes_accessed=30_000_000, transcendentals=8_000_000),
    )(
        tokens, cotangent, routes.reshape(1, tok_n), valid.reshape(1, tok_n), bucket_len, rel,
        attn_gain[None, :], ffn_gain[None, :], router_weight, qkv_weight, out_weight, jnp.transpose(w_in, (1, 0, 2)), jnp.transpose(w_out, (1, 0, 2)),
    )
    lo, tg, qg, og, sg, wig, wog, _ = outs
    counts = sg[:4, 64:66].astype(jnp.int32)
    return (
        lo, tg, sg[:, 0], qg, og, sg[:12, 32:64], sg[:, 1], sg[:, 2:6],
        jnp.transpose(wig, (1, 0, 2)), jnp.transpose(wog, (1, 0, 2)), counts[:, 0], counts[:, 1],
    )


epsilon = 1e-06


def bucket_codes(block_span, bucket_count, reach):
    position = jnp.arange(block_span, dtype=jnp.int32)
    offset_grid = position[None, :] - position[:, None]
    distance = jnp.abs(offset_grid)
    halfway = bucket_count // 2
    exact_span = halfway // 2
    distant = jnp.full(offset_grid.shape, exact_span, jnp.int32)
    for number in range(1, halfway - exact_span):
        threshold = math.ceil(
            exact_span * (reach / exact_span) ** (number / (halfway - exact_span))
        )
        distant = distant + (distance >= threshold).astype(jnp.int32)
    return jnp.where(distance < exact_span, distance, distant) + jnp.where(
        offset_grid > 0, halfway, 0
    )


def block_allowed(length, live_block):
    position = jnp.arange(live_block.shape[0], dtype=jnp.int32)
    segment = position // length
    return (segment[:, None] == segment[None, :]) & (live_block[None, :] > 0)


def rms_forward(values, gain_vector):
    inverse = lax.rsqrt(jnp.mean(values * values, axis=-1, keepdims=True) + epsilon)
    normed = values * inverse
    return (normed, inverse, normed * gain_vector)


def rms_backward(normed, inverse, gain_vector, grad_scaled):
    weighted = grad_scaled * gain_vector
    return inverse * (weighted - normed * jnp.mean(weighted * normed, axis=-1, keepdims=True))


def split_heads(block_rows):
    block_span = block_rows.shape[0]
    model_width = block_rows.shape[1] // 3
    head_size = model_width // HEADS
    return tuple(
        (
            block_rows[:, part_index * model_width : (part_index + 1) * model_width].reshape(
                block_span, HEADS, head_size
            )
            for part_index in range(3)
        )
    )


def block_scores(queries, keys_part, complete_position_bias, allowed):
    score_scale = queries.shape[-1] ** (-0.5)
    scores = (
        jnp.einsum("qhd,khd->hqk", queries, keys_part, preferred_element_type=jnp.float32)
        * score_scale
        + complete_position_bias
    )
    return jnp.where(allowed[None], scores, -1e30)


def attend_forward(complete_position_bias, packed):
    block_rows, length, live_block = packed
    queries, keys_part, values_part = split_heads(block_rows)
    scores = block_scores(
        queries, keys_part, complete_position_bias, block_allowed(length, live_block)
    )
    row_peak = jnp.max(scores, axis=-1, keepdims=True)
    exponent = jnp.exp(scores - row_peak)
    row_total = jnp.sum(exponent, axis=-1, keepdims=True)
    weights_low = (exponent / row_total).astype(jnp.bfloat16)
    mixed_rows = jnp.einsum(
        "hqk,khd->qhd", weights_low, values_part, preferred_element_type=jnp.float32
    )
    return (
        mixed_rows.reshape(block_rows.shape[0], -1).astype(jnp.bfloat16),
        (row_peak + jnp.log(row_total))[..., 0],
    )


def attend_backward(complete_position_bias, bucket_indicator, packed):
    block_rows, length, live_block, grad_mixed, log_total = packed
    queries, keys_part, values_part = split_heads(block_rows)
    scores = block_scores(
        queries, keys_part, complete_position_bias, block_allowed(length, live_block)
    )
    probs_full = jnp.exp(scores - log_total[:, :, None])
    grad_heads = grad_mixed.reshape(queries.shape)
    grad_probs = jnp.einsum(
        "qhd,khd->hqk", grad_heads, values_part, preferred_element_type=jnp.float32
    )
    score_gradient_rows = (
        probs_full * (grad_probs - jnp.sum(probs_full * grad_probs, axis=-1, keepdims=True))
    ).astype(jnp.bfloat16)
    score_scale = queries.shape[-1] ** (-0.5)
    grad_queries = (
        jnp.einsum(
            "hqk,khd->qhd", score_gradient_rows, keys_part, preferred_element_type=jnp.float32
        )
        * score_scale
    )
    grad_keys = (
        jnp.einsum("hqk,qhd->khd", score_gradient_rows, queries, preferred_element_type=jnp.float32)
        * score_scale
    )
    grad_values = jnp.einsum(
        "hqk,qhd->khd",
        probs_full.astype(jnp.bfloat16),
        grad_heads,
        preferred_element_type=jnp.float32,
    )
    table_grad = jnp.einsum(
        "wif,nif->wn", score_gradient_rows, bucket_indicator, preferred_element_type=jnp.float32
    )
    block_span = block_rows.shape[0]
    joined = jnp.concatenate(
        [
            grad_queries.reshape(block_span, -1),
            grad_keys.reshape(block_span, -1),
            grad_values.reshape(block_span, -1),
        ],
        axis=1,
    )
    return (joined.astype(jnp.bfloat16), table_grad)


def per_device(
    tokens,
    bucket_len,
    valid,
    routes,
    attn_gain,
    qkv_weight,
    out_weight,
    relative_head_bias,
    ffn_gain,
    router_weight,
    w_in,
    w_out,
    cotangent,
):
    top_probability = lax.Precision.HIGHEST
    gain_attn, weight_qkv, weight_out, gain_ffn, weight_router = (
        lax.all_gather(attn_gain, ("dp", "fsdp"), axis=0, tiled=True),
        lax.all_gather(qkv_weight, ("dp", "fsdp"), axis=0, tiled=True),
        lax.all_gather(out_weight, ("dp", "fsdp"), axis=0, tiled=True),
        lax.all_gather(ffn_gain, ("dp", "fsdp"), axis=0, tiled=True),
        lax.all_gather(router_weight, ("dp", "fsdp"), axis=0, tiled=True),
    )
    expert_in, expert_out = (
        lax.all_gather(w_in, "fsdp", axis=0, tiled=True),
        lax.all_gather(w_out, "fsdp", axis=0, tiled=True),
    )
    token_count, model_width = tokens.shape
    block_total = token_count // LONG
    expert_count = expert_in.shape[1]
    capacity = (5 * token_count + 4 * expert_count - 1) // (4 * expert_count)
    bucket_grid = bucket_codes(LONG, BUCKETS, MAXDIST)
    selected_bucket = bucket_grid[None] == jnp.arange(BUCKETS, dtype=jnp.int32)[:, None, None]
    bucket_indicator = selected_bucket.astype(jnp.bfloat16)
    complete_position_bias = jnp.einsum(
        "eo,ozm->ezm",
        relative_head_bias,
        selected_bucket.astype(jnp.float32),
        precision=top_probability,
    )
    live_blocks = valid.reshape(block_total, LONG)
    rows_in = tokens.astype(jnp.float32)
    normed_one, inverse_one, scaled_one = rms_forward(rows_in, gain_attn.astype(jnp.float32))
    normed_low = scaled_one.astype(jnp.bfloat16)
    qkv_low = jnp.dot(normed_low, weight_qkv, preferred_element_type=jnp.float32).astype(
        jnp.bfloat16
    )
    qkv_blocks = qkv_low.reshape(block_total, LONG, 3 * model_width)
    mixed_blocks, log_totals = lax.map(
        partial(attend_forward, complete_position_bias), (qkv_blocks, bucket_len, live_blocks)
    )
    mixed_low = mixed_blocks.reshape(token_count, model_width)
    hidden = rows_in + jnp.dot(mixed_low, weight_out, preferred_element_type=jnp.float32)
    normed_two, inverse_two, scaled_two = rms_forward(hidden, gain_ffn.astype(jnp.float32))
    normed_two_low = scaled_two.astype(jnp.bfloat16)
    normed_two_full = normed_two_low.astype(jnp.float32)
    router_probs = jax.nn.softmax(
        jnp.dot(normed_two_full, weight_router.astype(jnp.float32), precision=top_probability),
        axis=-1,
    )
    chosen = routes[:, 0]
    route_hot = chosen[:, None] == jnp.arange(expert_count, dtype=jnp.int32)[None, :]
    gate_value = jnp.sum(jnp.where(route_hot, router_probs, 0.0), axis=1)
    surviving_rows = valid > 0
    route_picks = route_hot & surviving_rows[:, None]
    places = jnp.cumsum(route_picks.astype(jnp.int32), axis=0) - 1
    slot_place = jnp.sum(jnp.where(route_picks, places, 0), axis=1)
    kept_rows = surviving_rows & (slot_place < capacity)
    slot_code = jnp.where(kept_rows, chosen * capacity + slot_place, 0)
    slot_match = (
        jnp.arange(expert_count * capacity, dtype=jnp.int32)[:, None]
        == jnp.where(kept_rows, slot_code, -1)[None, :]
    )
    slot_filled = jnp.any(slot_match, axis=1)
    slot_token = jnp.sum(
        jnp.where(slot_match, jnp.arange(token_count, dtype=jnp.int32)[None, :], 0), axis=1
    )
    slot_rows = jnp.where(
        slot_filled[:, None], normed_two_low[slot_token], jnp.zeros((), jnp.bfloat16)
    ).reshape(expert_count, capacity, model_width)
    slot_rows = lax.all_gather(slot_rows, "dp", axis=1, tiled=True)
    expert_inner = jnp.einsum(
        "ecd,fed->ecf", slot_rows, expert_in, preferred_element_type=jnp.float32
    )
    active_low = jax.nn.gelu(expert_inner, approximate=True).astype(jnp.bfloat16)
    result_low = (
        lax.psum_scatter(
            jnp.einsum("ecf,fed->ecd", active_low, expert_out, preferred_element_type=jnp.float32),
            "dp",
            scatter_dimension=1,
            tiled=True,
        )
        .astype(jnp.bfloat16)
        .reshape(expert_count * capacity, model_width)
    )
    returned = jnp.where(kept_rows[:, None], result_low[slot_code].astype(jnp.float32), 0.0)
    layer_out = (hidden + gate_value[:, None] * returned).astype(jnp.bfloat16)
    sent_local = jnp.sum((route_picks & kept_rows[:, None]).astype(jnp.int32), axis=0)
    lost_local = jnp.sum((route_picks & ~kept_rows[:, None]).astype(jnp.int32), axis=0)
    count_sums = lax.psum(jnp.stack([sent_local, lost_local]), ("dp", "fsdp"))
    grad_out = cotangent.astype(jnp.float32)
    grad_gate = jnp.sum(grad_out * returned, axis=1)
    grad_back = gate_value[:, None] * grad_out
    grad_result = (
        jnp.where(slot_filled[:, None], grad_back[slot_token], 0.0)
        .astype(jnp.bfloat16)
        .reshape(expert_count, capacity, model_width)
    )
    grad_result = lax.all_gather(grad_result, "dp", axis=1, tiled=True)
    grad_active = jnp.einsum(
        "ecd,fed->ecf", grad_result, expert_out, preferred_element_type=jnp.float32
    )
    unused_value, gelu_pullback = jax.vjp(partial(jax.nn.gelu, approximate=True), expert_inner)
    grad_inner = gelu_pullback(grad_active)[0].astype(jnp.bfloat16)
    grad_slots = lax.psum_scatter(
        jnp.einsum("ecf,fed->ecd", grad_inner, expert_in, preferred_element_type=jnp.float32),
        "dp",
        scatter_dimension=1,
        tiled=True,
    ).reshape(expert_count * capacity, model_width)
    grad_normed_two = jnp.where(kept_rows[:, None], grad_slots[slot_code], 0.0)
    grad_probs = jnp.where(route_hot, grad_gate[:, None], 0.0)
    grad_logits = router_probs * (
        grad_probs - jnp.sum(router_probs * grad_probs, axis=1, keepdims=True)
    )
    grad_normed_two = grad_normed_two + jnp.dot(
        grad_logits, weight_router.astype(jnp.float32).T, precision=top_probability
    )
    grad_hidden = (
        rms_backward(normed_two, inverse_two, gain_ffn.astype(jnp.float32), grad_normed_two)
        + grad_out
    )
    grad_hidden_low = grad_hidden.astype(jnp.bfloat16)
    grad_mixed = jnp.dot(grad_hidden_low, weight_out.T, preferred_element_type=jnp.float32).astype(
        jnp.bfloat16
    )
    joined_blocks, table_grads = lax.map(
        partial(attend_backward, complete_position_bias, bucket_indicator),
        (
            qkv_blocks,
            bucket_len,
            live_blocks,
            grad_mixed.reshape(block_total, LONG, model_width),
            log_totals,
        ),
    )
    grad_qkv = joined_blocks.reshape(token_count, 3 * model_width)
    grad_normed_one = jnp.dot(grad_qkv, weight_qkv.T, preferred_element_type=jnp.float32)
    grad_rows = rms_backward(
        normed_one, inverse_one, gain_attn.astype(jnp.float32), grad_normed_one
    )
    tokens_grad = (grad_rows + grad_hidden).astype(jnp.bfloat16)
    table_grad = lax.psum(jnp.sum(table_grads, axis=0), ("dp", "fsdp"))
    attn_term = jnp.sum(grad_normed_one * normed_one, axis=0)
    qkv_term = jnp.dot(normed_low.T, grad_qkv, preferred_element_type=jnp.float32)
    out_term = jnp.dot(mixed_low.T, grad_hidden_low, preferred_element_type=jnp.float32)
    ffn_term = jnp.sum(grad_normed_two * normed_two, axis=0)
    router_term = jnp.dot(normed_two_full.T, grad_logits, precision=top_probability)
    layer_summed = lax.psum_scatter(
        jnp.concatenate(
            [attn_term[:, None], qkv_term, out_term, ffn_term[:, None], router_term], axis=1
        ),
        ("dp", "fsdp"),
        scatter_dimension=0,
        tiled=True,
    )
    out_term = jnp.einsum(
        "ecf,ecd->fed", active_low, grad_result, preferred_element_type=jnp.float32
    )
    in_term = jnp.einsum("ecd,ecf->fed", slot_rows, grad_inner, preferred_element_type=jnp.float32)
    w_in_grad = lax.psum_scatter(in_term, "fsdp", scatter_dimension=0, tiled=True)
    w_out_grad = lax.psum_scatter(out_term, "fsdp", scatter_dimension=0, tiled=True)
    attn_gain_grad = layer_summed[:, 0]
    qkv_grad = layer_summed[:, 1 : 1 + 3 * model_width]
    out_grad = layer_summed[:, 1 + 3 * model_width : 1 + 4 * model_width]
    ffn_gain_grad = layer_summed[:, 1 + 4 * model_width]
    router_weight_gradient = layer_summed[:, 2 + 4 * model_width :]
    return (
        layer_out,
        tokens_grad,
        attn_gain_grad,
        qkv_grad,
        out_grad,
        table_grad,
        ffn_gain_grad,
        router_weight_gradient,
        w_in_grad,
        w_out_grad,
        count_sums[0],
        count_sums[1],
    )


def solution(mesh):
    both = ("dp", "fsdp")
    body = fused if (mesh.shape["dp"], mesh.shape["fsdp"]) == (4, 8) else per_device
    placed = (
        P(both, None), P(both), P(both), P(both, None), P(both), P(both, None), P(both, None), P(), P(both),
        P(both, None), P(both, None, None), P(both, None, None), P(both, None),
    )
    return jax.shard_map(
        body,
        mesh=mesh,
        in_specs=placed,
        out_specs=(
            P(both, None), P(both, None), P(both), P(both, None), P(both, None), P(), P(both), P(both, None),
            P(both, None, None), P(both, None, None), P(), P(),
        ),
        check_vma=False,
    )
```

```python
from functools import partial
import math

import jax
import jax.numpy as jnp
from jax import lax
from jax.experimental import pallas as pl
from jax.experimental.pallas import tpu as pltpu
from jax.sharding import PartitionSpec as P

F32 = jnp.float32
BF16 = jnp.bfloat16
MESH = pl.DeviceIdType.MESH

HEADS = 12
BUCKETS = 32
MAXDIST = 128
LONG = 512
NEG = -1e30
EPS = 1e-06
GELU_C = math.sqrt(2.0 / math.pi)


def nt(a, b):
    return lax.dot_general(a, b, (((1,), (1,)), ((), ())), preferred_element_type=F32)


def nn(a, b):
    return lax.dot_general(a, b, (((1,), (0,)), ((), ())), preferred_element_type=F32)


def tn(a, b):
    return lax.dot_general(a, b, (((0,), (0,)), ((), ())), preferred_element_type=F32)


def exact(a, b, dims):
    return lax.dot_general(
        a, b, (dims, ((), ())), precision=lax.Precision.HIGHEST, preferred_element_type=F32
    )


def iota(shape, axis):
    return lax.broadcasted_iota(jnp.int32, shape, axis)


def bucket_of(offset):
    distance = jnp.abs(offset)
    halfway = BUCKETS // 2
    exact_span = halfway // 2
    distant = jnp.full(offset.shape, exact_span, jnp.int32)
    for number in range(1, halfway - exact_span):
        threshold = math.ceil(
            exact_span * (MAXDIST / exact_span) ** (number / (halfway - exact_span))
        )
        distant = distant + jnp.where(distance >= threshold, 1, 0)
    return jnp.where(distance < exact_span, distance, distant) + jnp.where(offset > 0, halfway, 0)


def diagonal_sums(tile):
    wide = jnp.concatenate([tile, jnp.zeros((128, 128), F32)], axis=1)
    rows = 64
    while rows >= 8:
        wide = wide[:rows] + pltpu.roll(wide[rows : 2 * rows], 256 - rows, 1)
        rows //= 2
    while rows >= 1:
        wide = wide + pltpu.roll(pltpu.roll(wide, 256 - rows, 1), 8 - rows, 0)
        rows //= 2
    return wide[0:1]


VMEM_LIMIT = 63 << 20


def layer_kernel(
    tok, cot, routes, valid, length, rel, gain_a, gain_f, rshard, qshard, oshard, wi_hbm, wo_hbm,
    layer_out, tokens_grad, qkv_grad, out_grad, small_grad, wi_grad, wo_grad, p_hbm,
    aq, ar, ao, wq, wo, sm_t, wb, xg, ycore, yx, ry, rz,
    qkvb, u1, obuf, u2, gobuf, hid, prob, code_row, cols, key_mask, tab, bias, pst, dst_s, gd, relg,
    smallp, lsc, lsx, lsy, lsz, fin,
    free,
    s1s, s1r, s3zs, s3ys, s3r, s3l, xs, xr, ycs, ycr, yxs, yxr, dys, dyr, dzs, dzr,
    rcs, rcr, rxs, rxr, rys, ryr, rzs, rzr, psem, fsem,
):
    dp = lax.axis_index("dp")
    fs = lax.axis_index("fsdp")
    x, c = dp // 2, lax.rem(dp, 2)
    z, y = fs // 2, lax.rem(fs, 2)
    xn, cn, yn = 1 - x, 1 - c, 1 - y
    NZ = 4
    NE = 4
    CAP = 160
    D = 768

    def at(xx, cc, zz, yy):
        return (xx * 2 + cc, zz * 2 + yy)

    core_d, x_d, y_d = at(x, cn, z, y), at(xn, c, z, y), at(x, c, z, yn)

    def zz_of(step):
        return lax.rem(z + step, NZ)

    def zb_of(step):
        return lax.rem(z - step + NZ, NZ)

    def z_d(step):
        return at(x, c, zz_of(step), y)

    def remote(src, dst, ss, rs, where):
        return pltpu.make_async_remote_copy(
            src_ref=src, dst_ref=dst, send_sem=ss, recv_sem=rs, device_id=where, device_id_type=MESH
        )

    for s in range(3):
        for half in range(2):
            for k in range(3):
                lanes = slice(half * 384 + k * 128, half * 384 + k * 128 + 128)
                piece = qshard[:, k * D + (2 * s + half) * 128 : k * D + (2 * s + half) * 128 + 128]
                if s < 2:
                    aq[dp, z, y, s, :, lanes] = piece
                else:
                    ar[dp, z, y, :, lanes] = piece
    ao[dp, z, y] = oshard[...]
    diagonal = iota((24, 24), 0) == iota((24, 24), 1)
    gain_cols = [
        jnp.sum(jnp.where(diagonal, g[...].astype(F32), 0.0), axis=1, keepdims=True) for g in (gain_a, gain_f)
    ]
    lane24 = iota((24, 128), 1)
    place4 = jnp.where(iota((NE, 128), 1) == iota((NE, 128), 0) + 2, 1.0, 0.0).astype(BF16)
    small = jnp.where(lane24 == 0, gain_cols[0], jnp.where(lane24 == 1, gain_cols[1], nn(rshard[...], place4)))
    ar[dp, z, y, :, D:] = small.astype(BF16)

    barrier = pltpu.get_barrier_semaphore()
    peers = [core_d, x_d, y_d, z_d(1), z_d(2), z_d(3)]
    for peer in peers:
        pl.semaphore_signal(barrier, inc=1, device_id=peer, device_id_type=MESH)
    pl.semaphore_wait(barrier, len(peers))

    def s1(part, slot, dpi, zi, yi, where):
        ref = (aq, ar, ao)[part].at[dpi, zi, yi]
        return remote(ref, ref, s1s.at[part, slot], s1r.at[part, dpi * 8 + zi * 2 + yi], where)

    started = ([], [], [])

    def go(part, *rest):
        copy = s1(part, *rest)
        copy.start()
        started[part].append(copy)

    dpx, dpc, dpd = xn * 2 + c, x * 2 + cn, xn * 2 + cn

    def s1_spread(part, st, zi):
        go(part, 3 + st, dp, zi, y, y_d)
        go(part, 7 + st, dp, zi, y, x_d)
        go(part, 15 + st, dp, zi, y, core_d)

    def s1_z(part, st):
        s1(part, 0, dp, zb_of(st), y, y_d).wait_recv()
        s1_spread(part, st, zb_of(st))

    def s1_second(part, st):
        zi = zb_of(st)
        if part == 0:
            s1(part, 0, dp, zi, yn, y_d).wait_recv()
            go(part, 11 + st, dp, zi, yn, x_d)
            go(part, 19 + st, dp, zi, yn, core_d)
        else:
            s1(part, 0, dpx, zi, y, x_d).wait_recv()
            go(part, 11 + st, dpx, zi, y, y_d)
            go(part, 19 + st, dpx, zi, y, core_d)

    def s1_third(part, st):
        zi = zb_of(st)
        for number, yi in ((0, y), (1, yn)):
            if part == 0:
                dpi, yj, where = dpx, yi, x_d
            else:
                dpi, yj, where = (dp, dpx)[number], yn, y_d
            s1(part, 0, dpi, zi, yj, where).wait_recv()
            go(part, 23 + number * 4 + st, dpi, zi, yj, core_d)

    def s1_end(part):
        for dpi in (dpc, dpd):
            for yi in range(2):
                for zi in range(4):
                    s1(part, 0, dpi, zi, yi, core_d).wait_recv()
        for copy in started[part]:
            copy.wait_send()

    for part in (0, 1):
        for st in (1, 2, 3):
            go(part, st - 1, dp, z, y, z_d(st))
        s1_spread(part, 0, z)

    LAST = 2 * NE - 1
    up_d, down_d = at(x, c, jnp.minimum(z + 1, NZ - 1), y), at(x, c, jnp.maximum(z - 1, 0), y)

    def s3_src(m, e):
        return (wi_hbm if m == 0 else wo_hbm).at[e]

    def s3_own(m, e):
        return pltpu.make_async_copy(s3_src(m, e), wb.at[m, e, z, y], s3l.at[m, e])

    def s3_y0(m, e):
        return remote(s3_src(m, e), wb.at[m, e, z, y], s3ys.at[m, e, 0], s3r.at[m, e, z, y], y_d)

    def s3_y(m, e, zi):
        ref = wb.at[m, e, zi, y]
        return remote(ref, ref, s3ys.at[m, e, lax.rem(zi - z + NZ, NZ)], s3r.at[m, e, zi, y], y_d)

    def s3_arrival(m, e, zi, yi):
        ref = wb.at[m, e, zi, yi]
        return remote(ref, ref, s3ys.at[m, e, 0], s3r.at[m, e, zi, yi], y_d)

    def s3_line(m, e, zi, yi, way, slot, src=None):
        dst = wb.at[m, e, zi, yi]
        return remote(
            dst if src is None else src, dst, s3zs.at[m, e, way * 8 + slot], s3r.at[m, e, zi, yi], (up_d, down_d)[way]
        )

    def onward(way):
        return z < NZ - 1 if way == 0 else z > 0

    def s3_issue_line(lo, hi):
        for i in range(lo, hi):
            m, e = i % 2, i // 2
            for way in (0, 1):
                pl.when(onward(way))(lambda: s3_line(m, e, z, y, way, 0, s3_src(m, e)).start())
            s3_own(m, e).start()

    def s3_issue_y(lo, hi):
        for i in range(lo, hi):
            s3_y0(i % 2, i // 2).start()

    def s3_pair(i, dist, across=False):
        m, e = (i % 2, i // 2) if isinstance(i, int) else (lax.rem(i, 2), i // 2)
        yi = yn if across else y
        for way in (0, 1):
            zi = z - dist if way == 0 else z + dist
            here = zi >= 0 if way == 0 else zi < NZ
            zi = jnp.clip(zi, 0, NZ - 1)

            @pl.when(here)
            def _():
                s3_arrival(m, e, zi, yi).wait_recv()

                @pl.when(onward(way))
                def _():
                    s3_line(m, e, zi, yi, way, dist + (4 if across else 0)).start()

                if not (isinstance(i, int) and i == LAST):
                    s3_y(m, e, zi).start()

    def s3_across():
        m, e = 1, NE - 1
        s3_arrival(m, e, z, yn).wait_recv()
        for way in (0, 1):
            pl.when(onward(way))(lambda: s3_line(m, e, z, yn, way, 4).start())

    def s3_finish(e):
        for m in range(2):
            s3_own(m, e).wait()
            if 2 * e + m != LAST:
                for st in range(4):
                    s3_arrival(m, e, zz_of(st), yn).wait_recv()

    def s3_sent(e):
        for m in range(2):
            last = 2 * e + m == LAST
            s3_y0(m, e).wait_send()
            for st in (1, 2, 3):
                if not last:
                    s3_y(m, e, zz_of(st)).wait_send()
            for way in (0, 1):
                for dist in range(4):
                    origin = z >= dist if way == 0 else z + dist < NZ
                    for slot in (dist, dist + 4)[: 2 if last else 1]:
                        pl.when(origin & onward(way))(lambda: s3_line(m, e, z, y, way, slot).wait_send())

    route_v = routes[...]
    live_v = valid[...] > 0
    picks = jnp.where((iota((8, LONG), 0) == route_v) & live_v, 1.0, 0.0)
    upto = jnp.where(iota((LONG, LONG), 0) <= iota((LONG, LONG), 1), 1.0, 0.0).astype(BF16)
    counts = nn(picks.astype(BF16), upto)
    place = jnp.sum(picks * counts, axis=0, keepdims=True).astype(jnp.int32) - 1
    kept = live_v & (place < CAP)
    code = jnp.where(kept, route_v * CAP + place, -1)
    code_row[...] = code
    keptf = jnp.where(kept, 1.0, 0.0)
    sent = jnp.sum(picks * keptf, axis=1, keepdims=True)
    lost = jnp.sum(picks * (1.0 - keptf), axis=1, keepdims=True)
    lane128 = iota((8, 128), 1)
    relg[3] = jnp.zeros((16, 256), F32)
    relg[3, 0:8, 0:128] = jnp.where(lane128 == 64, sent, 0.0) + jnp.where(lane128 == 65, lost, 0.0)
    stacked = jnp.concatenate(
        [
            jnp.broadcast_to(code.astype(F32), (8, LONG)),
            jnp.broadcast_to(route_v.astype(F32), (8, LONG)),
            jnp.zeros((112, LONG), F32),
        ],
        axis=0,
    )
    cols[...] = jnp.transpose(stacked)
    same = (iota((8, LONG), 1) // 128 == iota((8, LONG), 0)) | (length[0] >= LONG)
    key_mask[...] = jnp.where(same & live_v, 0.0, NEG)

    for st in (1, 2, 3):
        for part in (0, 1):
            s1_z(part, st)
    for st in (1, 2, 3):
        go(2, st - 1, dp, z, y, z_d(st))
    s3_issue_line(0, 4)
    s3_issue_y(0, 4)

    rel16 = jnp.concatenate([rel[...], jnp.zeros((4, BUCKETS), F32)], axis=0)

    def bucket_hot(kind, axis):
        shape = (BUCKETS, 256) if axis == 0 else (256, BUCKETS)
        lane = iota(shape, 1 - axis)
        offset = jnp.where(lane < 128, lane, lane - 256) + (0, 128, -128)[kind]
        return jnp.where(bucket_of(offset) == iota(shape, axis), 1.0, 0.0)

    rows_by_kind = [exact(rel16, bucket_hot(kind, 0), ((1,), (0,))) for kind in range(3)]
    for b in (BUCKETS // 2 - 1, BUCKETS - 1):
        rows_by_kind.append(exact(rel16, jnp.where(iota((BUCKETS, 256), 0) == b, 1.0, 0.0), ((1,), (0,))))
    for head in range(HEADS):
        for kind in range(5):
            tab[head, kind : kind + 1, :] = rows_by_kind[kind][head : head + 1]

    for st in range(4):
        for part in (0, 1):
            s1_second(part, st)
    for st in range(4):
        for part in (0, 1):
            s1_third(part, st)
    for part in (0, 1):
        s1_end(part)
    s1_spread(2, 0, z)
    for st in (1, 2, 3):
        s1_z(2, st)
    for pair in range(3):
        s3_pair(0, 1 + pair)

    @pl.loop(0, 4)
    def _(dpi):
        for zi in range(4):
            base = pl.multiple_of((dpi * 8 + zi * 2) * 24, 16)
            for s in range(2):
                v = aq[dpi, zi, :, s].astype(F32).reshape(48, D)
                wq[s, pl.ds(base, 48)] = v.astype(BF16)
            v = ar[dpi, zi].astype(F32).reshape(48, D + 128).astype(BF16)
            wq[2, pl.ds(base, 48)] = v[:, :D]
            wo[pl.ds(base, 48), D:] = v[:, D:]

    sm_t[...] = jnp.transpose(wo[:, D:].astype(F32))
    gain1 = sm_t[0:1, :]
    gain2 = sm_t[1:2, :]

    @pl.loop(0, 4)
    def _(rb):
        rows = pl.ds(pl.multiple_of(rb * 128, 128), 128)
        xf = tok[rows].astype(F32)
        r1 = lax.rsqrt(jnp.mean(xf * xf, axis=-1, keepdims=True) + EPS)
        u1[rows] = (xf * r1 * gain1).astype(BF16)

    for s in range(3):
        qkvb[s] = nn(u1[...], wq[s]).astype(BF16)

    lane_low = iota((LONG, 128), 1) < 64

    def head_mask(v, h2):
        return jnp.where(lane_low if h2 == 0 else ~lane_low, v, jnp.zeros((), v.dtype))

    def p_copy(hp, out):
        slot = lax.rem(hp, 2)
        if out:
            return pltpu.make_async_copy(pst.at[slot], p_hbm.at[hp], psem.at[slot])
        return pltpu.make_async_copy(p_hbm.at[hp], pst.at[slot], psem.at[slot])

    def forward(hp):
        slot = lax.rem(hp, 2)
        s, base = hp // 2, pl.multiple_of(lax.rem(hp, 2) * 384, 128)
        q2 = qkvb[s, :, pl.ds(base, 128)]
        k2 = qkvb[s, :, pl.ds(base + 128, 128)]
        v2 = qkvb[s, :, pl.ds(base + 256, 128)]

        @pl.when(hp >= 2)
        def _():
            p_copy(hp, True).wait()

        for h2 in range(2):
            head = hp * 2 + h2
            qm = head_mask(q2, h2) * jnp.asarray(0.125, BF16)
            vm = head_mask(v2, h2)
            for kind in range(3):
                row = tab[head, kind : kind + 1, :]
                tile = pltpu.roll(jnp.broadcast_to(row, (128, 256)), 0, 1, stride=1, stride_axis=0)
                bias[kind] = tile[:, :128]
            left = jnp.broadcast_to(tab[head, 3:4, 0:128], (128, 128))
            right = jnp.broadcast_to(tab[head, 4:5, 0:128], (128, 128))
            for bi in range(4):
                rows = slice(bi * 128, bi * 128 + 128)
                sc = nt(qm[rows], k2)
                tiles = [
                    bias[0] if bj == bi else bias[1] if bj == bi + 1 else bias[2] if bj == bi - 1
                    else right if bj > bi else left
                    for bj in range(4)
                ]
                sc = sc + jnp.concatenate(tiles, axis=1) + key_mask[bi : bi + 1, :]
                peak = jnp.max(sc, axis=-1, keepdims=True)
                ex = jnp.exp(sc - peak)
                p = (ex * (1.0 / jnp.sum(ex, axis=-1, keepdims=True))).astype(BF16)
                pst[slot, h2, rows] = p
                part = nn(p, vm)
                if h2 == 0:
                    hid[rows, 0:128] = part
                else:
                    obuf[rows, pl.ds(pl.multiple_of(hp * 128, 128), 128)] = (
                        hid[rows, 0:128] + part
                    ).astype(BF16)
        p_copy(hp, True).start()
        for number in range(2):
            pair = 3 + 2 * hp + number
            s3_pair(pair // 3, 1 + lax.rem(pair, 3))


    pl.loop(0, 2)(forward)
    for st in range(4):
        s1_second(2, st)
    s3_issue_line(4, 8)
    s3_issue_y(4, 8)
    pl.loop(2, 4)(forward)
    for st in range(4):
        s1_third(2, st)
    pl.loop(4, HEADS // 2)(forward)
    s1_end(2)
    s3_across()
    @pl.loop(0, 4)
    def _(dpi):
        for zi in range(4):
            base = pl.multiple_of((dpi * 8 + zi * 2) * 24, 16)
            wo[pl.ds(base, 48), :D] = ao[dpi, zi].astype(F32).reshape(48, D).astype(BF16)

    for peer in peers:
        pl.semaphore_signal(free, inc=1, device_id=peer, device_id_type=MESH)

    lane = iota((128, 128), 1)
    is_logit = (lane >= 2) & (lane < 2 + NE)

    def probs_of(logits):
        lm = jnp.where(is_logit, logits, NEG)
        ex = jnp.where(is_logit, jnp.exp(lm - jnp.max(lm, axis=-1, keepdims=True)), 0.0)
        return ex / jnp.sum(ex, axis=-1, keepdims=True)

    @pl.loop(0, 4)
    def _(rb):
        rows = pl.ds(pl.multiple_of(rb * 128, 128), 128)
        h = tok[rows].astype(F32) + nn(obuf[rows], wo[:, :D])
        hid[rows] = h
        r2 = lax.rsqrt(jnp.mean(h * h, axis=-1, keepdims=True) + EPS)
        u = (h * r2 * gain2).astype(BF16)
        u2[rows] = u
        pr = probs_of(nn(u, wo[:, D:]))
        prob[rows] = pr
        hot = (lane - 2) == cols[rows, 8:9].astype(jnp.int32)
        gate = jnp.sum(jnp.where(hot, pr, 0.0), axis=-1, keepdims=True)
        gobuf[rows] = (gate * cot[rows].astype(F32)).astype(BF16)

    def xg_send(kind, e):
        if kind == 0:
            return remote(xg.at[dp, e], xg.at[dp, e], xs.at[0, e], xr.at[dp, e], x_d)
        if kind == 1:
            return remote(xg.at[dp, e], xg.at[dp, e], xs.at[1, e], xr.at[dp, e], core_d)
        return remote(xg.at[dpx, e], xg.at[dpx, e], xs.at[2, e], xr.at[dpx, e], core_d)

    def xg_arrival(dpi, e):
        return remote(xg.at[dpi, e], xg.at[dpi, e], xs.at[0, e], xr.at[dpi, e], x_d)

    for e in range(NE):
        hot = jnp.where(iota((CAP, LONG), 0) + e * CAP == code_row[...], 1.0, 0.0).astype(BF16)
        xg[dp, e, 0] = nn(hot, u2[...]).astype(BF16)
        xg[dp, e, 1] = nn(hot, gobuf[...]).astype(BF16)
        if e == 0:
            xg_send(0, e).start()
        xg_send(1, e).start()

    for dist in (1, 2, 3):
        s3_pair(5, dist)

    def yc_send(xi, e):
        return remote(xg.at[xi * 2 + cn, e], ycore.at[xi, e], ycs.at[xi, e], ycr.at[xi, e], core_d)

    def yx_send(e):
        return remote(xg.at[dpx, e], yx.at[e], yxs.at[e], yxr.at[e], x_d)

    def dy_send(m, e):
        return remote(wb.at[m, e, :, yn], ry.at[m, e], dys.at[m, e], dyr.at[m, e], y_d)

    z1 = z + 1 - 2 * lax.rem(z, 2)
    z2 = zz_of(2)
    z3 = lax.rem(z1 + 2, NZ)

    def dz_send(m, e, slot):
        zi, zd = ((z1, z1), (z3, z1), (z2, z2))[slot]
        return remote(
            wb.at[m, e, zi, y], rz.at[m, e, slot], dzs.at[m, e, slot], dzr.at[m, e, slot], at(x, c, zd, y)
        )

    def sum_x(e):
        for xi in range(2):
            yc_send(xi, e).wait_recv()
        xg[dpx, e] = (xg[dpx, e].astype(F32) + ycore[xn, e].astype(F32)).astype(BF16)
        yx_send(e).start()

    def sum_z(e):
        for m in range(2):
            dy_send(m, e).wait_recv()
            for zi, slot in ((z3, 1), (z1, 0), (z2, None), (z, None)):
                wb[m, e, zi, y] = (wb[m, e, zi, y].astype(F32) + ry[m, e, zi].astype(F32)).astype(BF16)
                if slot is not None:
                    dz_send(m, e, slot).start()

    def dl_z1(m, slot):
        return remote(
            wb.at[m, NE - 1, (z1, z3)[slot]], ry.at[m, NE - 1, pl.ds(2 * slot, 2)],
            dzs.at[m, NE - 1, slot], dzr.at[m, NE - 1, slot], at(x, c, z1, y),
        )

    def dl_z2(m):
        return remote(
            wb.at[m, NE - 1, z2], rz.at[m, NE - 1, pl.ds(0, 2)], dzs.at[m, NE - 1, 2], dzr.at[m, NE - 1, 2],
            at(x, c, z2, y),
        )

    def dl_y(m):
        return remote(wb.at[m, NE - 1, z, yn], rz.at[m, NE - 1, 2], dys.at[m, NE - 1], dyr.at[m, NE - 1], y_d)

    def last_issue():
        for m in range(2):
            for slot in (1, 0):
                dl_z1(m, slot).start()

    def last_z2():
        e = NE - 1
        for m in range(2):
            dl_z1(m, 1).wait_recv()
            wb[m, e, z2] = (wb[m, e, z2].astype(F32) + ry[m, e, 2:4].astype(F32)).astype(BF16)
            dl_z2(m).start()

    def last_y():
        e = NE - 1
        for m in range(2):
            dl_z1(m, 0).wait_recv()
            dl_z2(m).wait_recv()
            wb[m, e, z] = (
                wb[m, e, z].astype(F32) + ry[m, e, 0:2].astype(F32) + rz[m, e, 0:2].astype(F32)
            ).astype(BF16)
            dl_y(m).start()

    def sum_w(e):
        for m in range(2):
            dz_send(m, e, 1).wait_recv()
            wb[m, e, z2, y] = (wb[m, e, z2, y].astype(F32) + rz[m, e, 1].astype(F32)).astype(BF16)
            dz_send(m, e, 2).start()

    def fin_copy(number):
        e, m = number // 2, number % 2
        return pltpu.make_async_copy(fin.at[m], (wi_grad if m == 0 else wo_grad).at[e], fsem.at[m])

    def grad_final(e):
        for m in range(2):
            total = wb[m, e, z, y].astype(F32)
            if e == NE - 1:
                dl_y(m).wait_recv()
                total = total + rz[m, e, 2].astype(F32)
            else:
                for slot in (0, 2):
                    dz_send(m, e, slot).wait_recv()
                    total = total + rz[m, e, slot].astype(F32)
            number = e * 2 + m
            if number >= 2:
                fin_copy(number - 2).wait()
            fin[m] = total
            fin_copy(number).start()

    def forward_x(e):
        xg_arrival(dpx, e).wait_recv()
        if e < NE - 1:
            xg_send(0, e + 1).start()
        xg_send(2, e).start()

    PAIRS = (
        ((6, 1),), ((6, 2),), ((6, 3),), ((LAST, 1), (LAST, 1, True)),
        ((LAST, 2), (LAST, 2, True)), ((LAST, 3), (LAST, 3, True)), (), (),
    )
    forward_x(0)
    for e in range(NE):
        if e >= 1:
            sum_x(e - 1)
        xg_arrival(dpc, e).wait_recv()
        xg_arrival(xn * 2 + cn, e).wait_recv()
        s3_finish(e)
        for kind in range(3):
            xg_send(kind, e).wait_send()
        s3_sent(e)
        half = 4 * 96
        for fc in range(2):
            zs = slice(2 * fc, 2 * fc + 2)
            xv = xg[:, e, 0].reshape(4 * CAP, D)
            gv = xg[:, e, 1].reshape(4 * CAP, D)
            wi_v = wb[0, e, zs].reshape(half, D)
            wo_v = wb[1, e, zs].reshape(half, D)
            zv = nt(xv, wi_v)
            ga = nt(gv, wo_v)
            t = jnp.tanh(GELU_C * (zv + 0.044715 * (zv * zv * zv)))
            act = (0.5 * zv * (1.0 + t)).astype(BF16)
            slope = 0.5 * (1.0 + t) + (0.5 * GELU_C) * zv * (1.0 - t * t) * (
                1.0 + (3 * 0.044715) * (zv * zv)
            )
            gz = (ga * slope).astype(BF16)
            if fc == 0:
                yacc = nn(act, wo_v)
                gacc = nn(gz, wi_v)
                pst_y, pst_g = yacc, gacc
            else:
                pst_y = pst_y + nn(act, wo_v)
                pst_g = pst_g + nn(gz, wi_v)
            wb[1, e, zs] = tn(act, gv).astype(BF16).reshape(2, 2, 96, D)
            wb[0, e, zs] = tn(gz, xv).astype(BF16).reshape(2, 2, 96, D)
            for pair in PAIRS[e * 2 + fc]:
                s3_pair(*pair)
            if fc == 1 and e < NE - 1:
                forward_x(e + 1)
        xg[:, e, 0] = pst_y.astype(BF16).reshape(4, CAP, D)
        xg[:, e, 1] = pst_g.astype(BF16).reshape(4, CAP, D)
        for xi in range(2):
            yc_send(xi, e).start()
        if e < NE - 1:
            for m in range(2):
                dy_send(m, e).start()
        else:
            last_issue()
        if e == 2:
            sum_z(0)
    sum_x(NE - 1)
    sum_z(1)

    for e in range(NE):
        yx_send(e).wait_recv()
        xg[dp, e] = (xg[dp, e].astype(F32) + ycore[x, e].astype(F32) + yx[e].astype(F32)).astype(BF16)
    gd[0:8] = jnp.zeros((8, D), F32)

    @pl.loop(0, 4)
    def _(rb):
        rows = pl.ds(pl.multiple_of(rb * 128, 128), 128)
        code_col = cols[rows, 0:1].astype(jnp.int32)
        back = jnp.where(iota((128, NE * CAP), 1) == code_col, 1.0, 0.0).astype(BF16)
        yt = nn(back, xg[dp, :, 0].reshape(NE * CAP, D))
        gxt = nn(back, xg[dp, :, 1].reshape(NE * CAP, D))
        h = hid[rows]
        g = cot[rows].astype(F32)
        pr = prob[rows]
        hot = (lane - 2) == cols[rows, 8:9].astype(jnp.int32)
        gate = jnp.sum(jnp.where(hot, pr, 0.0), axis=-1, keepdims=True)
        layer_out[rows] = (h + gate * yt).astype(BF16)
        ggate = jnp.sum(g * yt, axis=-1, keepdims=True)
        dprob = jnp.where(hot, ggate, 0.0)
        dlog = pr * (dprob - jnp.sum(pr * dprob, axis=-1, keepdims=True))
        prob[rows] = dlog
        hi = dlog.astype(BF16)
        lo = (dlog - hi.astype(F32)).astype(BF16)
        wr_t = sm_t[...].astype(BF16)
        gu = gxt + nn(hi, wr_t) + nn(lo, wr_t)
        r2 = lax.rsqrt(jnp.mean(h * h, axis=-1, keepdims=True) + EPS)
        n2 = h * r2
        gd[1:2] = gd[1:2] + jnp.sum(gu * n2, axis=0, keepdims=True)
        mm = gu * gain2
        gh = g + r2 * (mm - n2 * jnp.mean(mm * n2, axis=-1, keepdims=True))
        hid[rows] = gh
        ghb = gh.astype(BF16)
        gobuf[rows] = nt(ghb, wo[:, :D]).astype(BF16)
        tokens_grad[rows] = ghb

    dlog = prob[...]
    dlog_hi = dlog.astype(BF16)
    router_part = tn(u2[...], dlog_hi) + tn(u2[...], (dlog - dlog_hi.astype(F32)).astype(BF16))

    for e in range(NE):
        for xi in range(2):
            yc_send(xi, e).wait_send()
        yx_send(e).wait_send()
    pl.semaphore_wait(free, len(peers))

    def pack(unit, lanes, width, value):
        for d in range(32):
            xg[d // 8, d % 8 // 2, d % 2, unit * 32 : unit * 32 + 24, lanes] = value[
                24 * d : 24 * d + 24
            ].astype(BF16)

    def lands(unit):
        if unit == 4:
            return lsc, lsx, lsy, lsz
        if unit == 3:
            return ao.at[0:2], ao.at[2], ao.at[3, :, 0], ao.at[3, 0:3, 1]
        if unit == 2:
            full = pl.ds(0, D)
            return (
                ar.at[0:2, :, :, :, full], ar.at[2, :, :, :, full],
                ar.at[3, :, 0, :, full], ar.at[3, 0:3, 1, :, full],
            )
        return aq.at[0:2, :, :, unit], aq.at[2, :, :, unit], aq.at[3, :, 0, unit], aq.at[3, 0:3, 1, unit]

    def part_ref(unit):
        if unit == 4:
            return smallp
        return xg.at[:, :, :, pl.ds(unit * 32, 24), :]

    def narrow(unit, v):
        return v if unit == 4 else v.astype(BF16)

    def rs_core(unit, xi):
        return remote(
            part_ref(unit).at[xi * 2 + cn], lands(unit)[0].at[xi], rcs.at[unit, xi], rcr.at[unit, xi], core_d
        )

    def rs_x(unit):
        return remote(part_ref(unit).at[dpx], lands(unit)[1], rxs.at[unit], rxr.at[unit], x_d)

    def rs_y(unit):
        return remote(part_ref(unit).at[dp, :, yn], lands(unit)[2], rys.at[unit], ryr.at[unit], y_d)

    def rs_z(unit, st):
        dst = lands(unit)[3].at[z] if unit == 4 else lands(unit)[3].at[st - 1]
        return remote(
            part_ref(unit).at[dp, zz_of(st), y], dst, rzs.at[unit, st - 1], rzr.at[unit, st - 1], z_d(st)
        )

    def st_core(unit):
        for xi in range(2):
            rs_core(unit, xi).start()

    def st_x(unit):
        mine, (lc, _, _, _) = part_ref(unit), lands(unit)
        for xi in range(2):
            rs_core(unit, xi).wait_recv()
        for zi in range(4):
            mine[dpx, zi] = narrow(unit, mine[dpx, zi].astype(F32) + lc[xn, zi].astype(F32))
        rs_x(unit).start()

    def st_y(unit):
        mine, (lc, lx, _, _) = part_ref(unit), lands(unit)
        rs_x(unit).wait_recv()
        for zi in range(4):
            mine[dp, zi] = narrow(
                unit, mine[dp, zi].astype(F32) + lc[x, zi].astype(F32) + lx[zi].astype(F32)
            )
        rs_y(unit).start()

    def st_z(unit):
        mine, (_, _, ly, _) = part_ref(unit), lands(unit)
        rs_y(unit).wait_recv()
        for zi in range(4):
            mine[dp, zi, y] = narrow(unit, mine[dp, zi, y].astype(F32) + ly[zi].astype(F32))
        for st in (1, 2, 3):
            rs_z(unit, st).start()

    def st_final(unit):
        mine, (_, _, _, lz) = part_ref(unit), lands(unit)
        for st in (1, 2, 3):
            rs_z(unit, st).wait_recv()
        if unit == 4:
            lz[z] = mine[dp, z, y]
            return (lz[0] + lz[1]) + (lz[2] + lz[3])
        total = mine[dp, z, y].astype(F32)
        for st in (1, 2, 3):
            total = total + lz[st - 1].astype(F32)
        return total

    def st_sent(unit):
        for xi in range(2):
            rs_core(unit, xi).wait_send()
        rs_x(unit).wait_send()
        rs_y(unit).wait_send()
        for st in (1, 2, 3):
            rs_z(unit, st).wait_send()

    for half in range(2):
        lanes = slice(half * 384, half * 384 + 384)
        pack(3, lanes, 384, tn(obuf[...], tokens_grad[:, lanes]))
    st_core(3)
    sum_w(0)
    last_z2()
    sum_z(2)

    relg[0] = jnp.zeros((16, 256), F32)
    relg[1] = jnp.zeros((16, 256), F32)
    relg[2] = jnp.zeros((16, 256), F32)
    p_copy(4, True).wait()
    p_copy(5, True).wait()
    p_copy(0, False).start()

    def backward(hp):
        slot = hp % 2
        s, base = hp // 2, (hp % 2) * 384
        p_copy(hp, False).wait()
        if hp < 5:
            p_copy(hp + 1, False).start()
        q2 = qkvb[s, :, base : base + 128]
        k2 = qkvb[s, :, base + 128 : base + 256]
        v2 = qkvb[s, :, base + 256 : base + 384]
        go2 = gobuf[:, hp * 128 : hp * 128 + 128]
        eighth = jnp.asarray(0.125, BF16)
        for h2 in range(2):
            head = hp * 2 + h2
            qm = head_mask(q2, h2) * eighth
            km = head_mask(k2, h2) * eighth
            gm = head_mask(go2, h2)
            tiles = [None] * 5
            for bi in range(4):
                rows = slice(bi * 128, bi * 128 + 128)
                pv = pst[slot, h2, rows].astype(F32)
                dpv = nt(gm[rows], v2)
                ds = pv * (dpv - jnp.sum(pv * dpv, axis=-1, keepdims=True))
                dst_s[rows] = ds.astype(BF16)
                for bj in range(4):
                    kind = 0 if bj == bi else 1 if bj == bi + 1 else 2 if bj == bi - 1 else 4 if bj > bi else 3
                    tile = ds[:, bj * 128 : bj * 128 + 128]
                    tiles[kind] = tile if tiles[kind] is None else tiles[kind] + tile
            for kind in range(3):
                relg[kind, head : head + 1, :] = diagonal_sums(tiles[kind])
            relg[3, head : head + 1, 128:256] = jnp.sum(tiles[3], axis=0, keepdims=True)
            relg[4, head : head + 1, 0:128] = jnp.sum(tiles[4], axis=0, keepdims=True)
            dsb = dst_s[...]
            dq = nn(dsb, km)
            dk = tn(dsb, qm)
            dv = tn(pst[slot, h2], gm)
            if h2 == 0:
                grad3 = [dq, dk, dv]
            else:
                grad3 = [a + b for a, b in zip(grad3, (dq, dk, dv))]
        for k in range(3):
            qkvb[s, :, base + k * 128 : base + k * 128 + 128] = grad3[k].astype(BF16)
        pack(s, slice(base, base + 384), 384, tn(u1[...], qkvb[s, :, base : base + 384]))

    backward(0)
    st_x(3)
    backward(1)
    st_core(0)
    st_y(3)
    sum_w(1)
    last_y()
    backward(2)
    st_x(0)
    st_z(3)
    backward(3)
    st_core(1)
    st_y(0)
    backward(4)
    sum_w(2)
    st_x(1)
    st_z(0)
    backward(5)
    st_core(2)
    st_y(1)

    @pl.loop(0, 4)
    def _(rb):
        rows = pl.ds(pl.multiple_of(rb * 128, 128), 128)
        gu = nt(qkvb[0, rows], wq[0]) + nt(qkvb[1, rows], wq[1]) + nt(qkvb[2, rows], wq[2])
        xf = tok[rows].astype(F32)
        r1 = lax.rsqrt(jnp.mean(xf * xf, axis=-1, keepdims=True) + EPS)
        n1 = xf * r1
        gd[0:1] = gd[0:1] + jnp.sum(gu * n1, axis=0, keepdims=True)
        mm = gu * gain1
        grad = hid[rows] + r1 * (mm - n1 * jnp.mean(mm * n1, axis=-1, keepdims=True))
        tokens_grad[rows] = grad.astype(BF16)

    st_x(2)
    st_z(1)

    gains = jnp.concatenate([gd[0:8], jnp.zeros((120, D), F32)], axis=0)
    gain_cols = jnp.transpose(gains)
    lane768 = iota((D, 128), 1)
    small_cols = jnp.where(lane768 < 2, gain_cols, jnp.where(lane768 < 2 + NE, router_part, 0.0))
    table = jnp.zeros((16, BUCKETS), F32)
    for kind in range(3):
        table = table + exact(relg[kind], bucket_hot(kind, 1), ((1,), (0,)))
    far_b = iota((128, BUCKETS), 1)
    table = table + exact(
        relg[3, :, 128:256], jnp.where(far_b == BUCKETS // 2 - 1, 1.0, 0.0), ((1,), (0,))
    )
    table = table + exact(relg[4, :, 0:128], jnp.where(far_b == BUCKETS - 1, 1.0, 0.0), ((1,), (0,)))
    extra = jnp.concatenate(
        [
            jnp.zeros((16, 32), F32),
            table,
            relg[3, :, 64:128],
        ],
        axis=1,
    )
    extra = jnp.concatenate([extra, jnp.zeros((8, 128), F32)], axis=0)
    for d in range(32):
        smallp[d // 8, d % 8 // 2, d % 2] = small_cols[24 * d : 24 * d + 24] + extra
    st_core(4)
    st_y(2)
    st_x(4)
    grad_final(0)
    grad_final(1)
    st_z(2)
    st_y(4)
    grad_final(2)
    out_grad[...] = st_final(3)
    st_z(4)

    def write_qkv(unit):
        total = st_final(unit)
        for half in range(2):
            for k in range(3):
                qkv_grad[:, k * D + (2 * unit + half) * 128 : k * D + (2 * unit + half) * 128 + 128] = total[
                    :, half * 384 + k * 128 : half * 384 + k * 128 + 128
                ]

    write_qkv(0)
    write_qkv(1)
    grad_final(3)
    write_qkv(2)
    small_grad[...] = st_final(4)
    fin_copy(2 * NE - 2).wait()
    fin_copy(2 * NE - 1).wait()

    for e in range(NE):
        for m in range(2):
            if e == NE - 1:
                for copy in (dl_z1(m, 0), dl_z1(m, 1), dl_z2(m), dl_y(m)):
                    copy.wait_send()
            else:
                dy_send(m, e).wait_send()
                for slot in range(3):
                    dz_send(m, e, slot).wait_send()
    for unit in range(5):
        st_sent(unit)


def fused(
    tokens, bucket_len, valid, routes, attn_gain, qkv_weight, out_weight, rel, ffn_gain, router_weight,
    w_in, w_out, cotangent,
):
    tok_n, D = tokens.shape
    vm = pl.BlockSpec(memory_space=pltpu.VMEM)
    hbm = pl.BlockSpec(memory_space=pl.ANY)
    sds = jax.ShapeDtypeStruct
    V = pltpu.VMEM
    sem = lambda *s: pltpu.SemaphoreType.DMA(s)
    outs = pl.pallas_call(
        layer_kernel,
        out_shape=(
            sds((512, 768), BF16), sds((512, 768), BF16), sds((24, 2304), F32), sds((24, 768), F32),
            sds((24, 128), F32), sds((4, 96, 768), F32), sds((4, 96, 768), F32), sds((6, 2, 512, 512), BF16),
        ),
        in_specs=[vm, vm, vm, vm, pl.BlockSpec(memory_space=pltpu.SMEM), vm, vm, vm, vm, vm, vm, hbm, hbm],
        out_specs=(vm,) * 5 + (hbm,) * 3,
        scratch_shapes=[
            V((4, 4, 2, 2, 24, 768), BF16),
            V((4, 4, 2, 24, 896), BF16),
            V((4, 4, 2, 24, 768), BF16),
            V((3, 768, 768), BF16),
            V((768, 896), BF16),
            V((128, 768), F32),
            V((2, 4, 4, 2, 96, 768), BF16),
            V((4, 4, 2, 160, 768), BF16),
            V((2, 4, 2, 160, 768), BF16),
            V((4, 2, 160, 768), BF16),
            V((2, 4, 4, 96, 768), BF16),
            V((2, 4, 3, 96, 768), BF16),
            V((3, 512, 768), BF16),
            V((512, 768), BF16),
            V((512, 768), BF16),
            V((512, 768), BF16),
            V((512, 768), BF16),
            V((512, 768), F32),
            V((512, 128), F32),
            V((1, 512), jnp.int32),
            V((512, 128), F32),
            V((8, 512), F32),
            V((12, 8, 256), F32),
            V((3, 128, 128), F32),
            V((2, 2, 512, 512), BF16),
            V((512, 512), BF16),
            V((8, 768), F32),
            V((5, 16, 256), F32),
            V((4, 4, 2, 24, 128), F32),
            V((2, 4, 2, 24, 128), F32),
            V((4, 2, 24, 128), F32),
            V((4, 24, 128), F32),
            V((4, 24, 128), F32),
            V((2, 96, 768), F32),
            pltpu.SemaphoreType.REGULAR,
            sem(3, 31), sem(3, 32), sem(2, 4, 16), sem(2, 4, 4), sem(2, 4, 4, 2), sem(2, 4),
            sem(3, 4), sem(4, 4), sem(2, 4), sem(2, 4), sem(4), sem(4), sem(2, 4), sem(2, 4),
            sem(2, 4, 3), sem(2, 4, 3),
            sem(5, 2), sem(5, 2), sem(5), sem(5), sem(5), sem(5), sem(5, 3), sem(5, 4), sem(2), sem(2),
        ],
        compiler_params=pltpu.CompilerParams(
            collective_id=0, has_side_effects=True, vmem_limit_bytes=VMEM_LIMIT
        ),
        cost_estimate=pl.CostEstimate(flops=40_000_000_000, bytes_accessed=30_000_000, transcendentals=8_000_000),
    )(
        tokens, cotangent, routes.reshape(1, tok_n), valid.reshape(1, tok_n), bucket_len, rel,
        attn_gain[None, :], ffn_gain[None, :], router_weight, qkv_weight, out_weight, jnp.transpose(w_in, (1, 0, 2)), jnp.transpose(w_out, (1, 0, 2)),
    )
    lo, tg, qg, og, sg, wig, wog, _ = outs
    counts = sg[:4, 64:66].astype(jnp.int32)
    return (
        lo, tg, sg[:, 0], qg, og, sg[:12, 32:64], sg[:, 1], sg[:, 2:6],
        jnp.transpose(wig, (1, 0, 2)), jnp.transpose(wog, (1, 0, 2)), counts[:, 0], counts[:, 1],
    )


epsilon = 1e-06


def bucket_codes(block_span, bucket_count, reach):
    position = jnp.arange(block_span, dtype=jnp.int32)
    offset_grid = position[None, :] - position[:, None]
    distance = jnp.abs(offset_grid)
    halfway = bucket_count // 2
    exact_span = halfway // 2
    distant = jnp.full(offset_grid.shape, exact_span, jnp.int32)
    for number in range(1, halfway - exact_span):
        threshold = math.ceil(
            exact_span * (reach / exact_span) ** (number / (halfway - exact_span))
        )
        distant = distant + (distance >= threshold).astype(jnp.int32)
    return jnp.where(distance < exact_span, distance, distant) + jnp.where(
        offset_grid > 0, halfway, 0
    )


def block_allowed(length, live_block):
    position = jnp.arange(live_block.shape[0], dtype=jnp.int32)
    segment = position // length
    return (segment[:, None] == segment[None, :]) & (live_block[None, :] > 0)


def rms_forward(values, gain_vector):
    inverse = lax.rsqrt(jnp.mean(values * values, axis=-1, keepdims=True) + epsilon)
    normed = values * inverse
    return (normed, inverse, normed * gain_vector)


def rms_backward(normed, inverse, gain_vector, grad_scaled):
    weighted = grad_scaled * gain_vector
    return inverse * (weighted - normed * jnp.mean(weighted * normed, axis=-1, keepdims=True))


def split_heads(block_rows):
    block_span = block_rows.shape[0]
    model_width = block_rows.shape[1] // 3
    head_size = model_width // HEADS
    return tuple(
        (
            block_rows[:, part_index * model_width : (part_index + 1) * model_width].reshape(
                block_span, HEADS, head_size
            )
            for part_index in range(3)
        )
    )


def block_scores(queries, keys_part, complete_position_bias, allowed):
    score_scale = queries.shape[-1] ** (-0.5)
    scores = (
        jnp.einsum("qhd,khd->hqk", queries, keys_part, preferred_element_type=jnp.float32)
        * score_scale
        + complete_position_bias
    )
    return jnp.where(allowed[None], scores, -1e30)


def attend_forward(complete_position_bias, packed):
    block_rows, length, live_block = packed
    queries, keys_part, values_part = split_heads(block_rows)
    scores = block_scores(
        queries, keys_part, complete_position_bias, block_allowed(length, live_block)
    )
    row_peak = jnp.max(scores, axis=-1, keepdims=True)
    exponent = jnp.exp(scores - row_peak)
    row_total = jnp.sum(exponent, axis=-1, keepdims=True)
    weights_low = (exponent / row_total).astype(jnp.bfloat16)
    mixed_rows = jnp.einsum(
        "hqk,khd->qhd", weights_low, values_part, preferred_element_type=jnp.float32
    )
    return (
        mixed_rows.reshape(block_rows.shape[0], -1).astype(jnp.bfloat16),
        (row_peak + jnp.log(row_total))[..., 0],
    )


def attend_backward(complete_position_bias, bucket_indicator, packed):
    block_rows, length, live_block, grad_mixed, log_total = packed
    queries, keys_part, values_part = split_heads(block_rows)
    scores = block_scores(
        queries, keys_part, complete_position_bias, block_allowed(length, live_block)
    )
    probs_full = jnp.exp(scores - log_total[:, :, None])
    grad_heads = grad_mixed.reshape(queries.shape)
    grad_probs = jnp.einsum(
        "qhd,khd->hqk", grad_heads, values_part, preferred_element_type=jnp.float32
    )
    score_gradient_rows = (
        probs_full * (grad_probs - jnp.sum(probs_full * grad_probs, axis=-1, keepdims=True))
    ).astype(jnp.bfloat16)
    score_scale = queries.shape[-1] ** (-0.5)
    grad_queries = (
        jnp.einsum(
            "hqk,khd->qhd", score_gradient_rows, keys_part, preferred_element_type=jnp.float32
        )
        * score_scale
    )
    grad_keys = (
        jnp.einsum("hqk,qhd->khd", score_gradient_rows, queries, preferred_element_type=jnp.float32)
        * score_scale
    )
    grad_values = jnp.einsum(
        "hqk,qhd->khd",
        probs_full.astype(jnp.bfloat16),
        grad_heads,
        preferred_element_type=jnp.float32,
    )
    table_grad = jnp.einsum(
        "wif,nif->wn", score_gradient_rows, bucket_indicator, preferred_element_type=jnp.float32
    )
    block_span = block_rows.shape[0]
    joined = jnp.concatenate(
        [
            grad_queries.reshape(block_span, -1),
            grad_keys.reshape(block_span, -1),
            grad_values.reshape(block_span, -1),
        ],
        axis=1,
    )
    return (joined.astype(jnp.bfloat16), table_grad)


def per_device(
    tokens,
    bucket_len,
    valid,
    routes,
    attn_gain,
    qkv_weight,
    out_weight,
    relative_head_bias,
    ffn_gain,
    router_weight,
    w_in,
    w_out,
    cotangent,
):
    top_probability = lax.Precision.HIGHEST
    gain_attn, weight_qkv, weight_out, gain_ffn, weight_router = (
        lax.all_gather(attn_gain, ("dp", "fsdp"), axis=0, tiled=True),
        lax.all_gather(qkv_weight, ("dp", "fsdp"), axis=0, tiled=True),
        lax.all_gather(out_weight, ("dp", "fsdp"), axis=0, tiled=True),
        lax.all_gather(ffn_gain, ("dp", "fsdp"), axis=0, tiled=True),
        lax.all_gather(router_weight, ("dp", "fsdp"), axis=0, tiled=True),
    )
    expert_in, expert_out = (
        lax.all_gather(w_in, "fsdp", axis=0, tiled=True),
        lax.all_gather(w_out, "fsdp", axis=0, tiled=True),
    )
    token_count, model_width = tokens.shape
    block_total = token_count // LONG
    expert_count = expert_in.shape[1]
    capacity = (5 * token_count + 4 * expert_count - 1) // (4 * expert_count)
    bucket_grid = bucket_codes(LONG, BUCKETS, MAXDIST)
    selected_bucket = bucket_grid[None] == jnp.arange(BUCKETS, dtype=jnp.int32)[:, None, None]
    bucket_indicator = selected_bucket.astype(jnp.bfloat16)
    complete_position_bias = jnp.einsum(
        "eo,ozm->ezm",
        relative_head_bias,
        selected_bucket.astype(jnp.float32),
        precision=top_probability,
    )
    live_blocks = valid.reshape(block_total, LONG)
    rows_in = tokens.astype(jnp.float32)
    normed_one, inverse_one, scaled_one = rms_forward(rows_in, gain_attn.astype(jnp.float32))
    normed_low = scaled_one.astype(jnp.bfloat16)
    qkv_low = jnp.dot(normed_low, weight_qkv, preferred_element_type=jnp.float32).astype(
        jnp.bfloat16
    )
    qkv_blocks = qkv_low.reshape(block_total, LONG, 3 * model_width)
    mixed_blocks, log_totals = lax.map(
        partial(attend_forward, complete_position_bias), (qkv_blocks, bucket_len, live_blocks)
    )
    mixed_low = mixed_blocks.reshape(token_count, model_width)
    hidden = rows_in + jnp.dot(mixed_low, weight_out, preferred_element_type=jnp.float32)
    normed_two, inverse_two, scaled_two = rms_forward(hidden, gain_ffn.astype(jnp.float32))
    normed_two_low = scaled_two.astype(jnp.bfloat16)
    normed_two_full = normed_two_low.astype(jnp.float32)
    router_probs = jax.nn.softmax(
        jnp.dot(normed_two_full, weight_router.astype(jnp.float32), precision=top_probability),
        axis=-1,
    )
    chosen = routes[:, 0]
    route_hot = chosen[:, None] == jnp.arange(expert_count, dtype=jnp.int32)[None, :]
    gate_value = jnp.sum(jnp.where(route_hot, router_probs, 0.0), axis=1)
    surviving_rows = valid > 0
    route_picks = route_hot & surviving_rows[:, None]
    places = jnp.cumsum(route_picks.astype(jnp.int32), axis=0) - 1
    slot_place = jnp.sum(jnp.where(route_picks, places, 0), axis=1)
    kept_rows = surviving_rows & (slot_place < capacity)
    slot_code = jnp.where(kept_rows, chosen * capacity + slot_place, 0)
    slot_match = (
        jnp.arange(expert_count * capacity, dtype=jnp.int32)[:, None]
        == jnp.where(kept_rows, slot_code, -1)[None, :]
    )
    slot_filled = jnp.any(slot_match, axis=1)
    slot_token = jnp.sum(
        jnp.where(slot_match, jnp.arange(token_count, dtype=jnp.int32)[None, :], 0), axis=1
    )
    slot_rows = jnp.where(
        slot_filled[:, None], normed_two_low[slot_token], jnp.zeros((), jnp.bfloat16)
    ).reshape(expert_count, capacity, model_width)
    slot_rows = lax.all_gather(slot_rows, "dp", axis=1, tiled=True)
    expert_inner = jnp.einsum(
        "ecd,fed->ecf", slot_rows, expert_in, preferred_element_type=jnp.float32
    )
    active_low = jax.nn.gelu(expert_inner, approximate=True).astype(jnp.bfloat16)
    result_low = (
        lax.psum_scatter(
            jnp.einsum("ecf,fed->ecd", active_low, expert_out, preferred_element_type=jnp.float32),
            "dp",
            scatter_dimension=1,
            tiled=True,
        )
        .astype(jnp.bfloat16)
        .reshape(expert_count * capacity, model_width)
    )
    returned = jnp.where(kept_rows[:, None], result_low[slot_code].astype(jnp.float32), 0.0)
    layer_out = (hidden + gate_value[:, None] * returned).astype(jnp.bfloat16)
    sent_local = jnp.sum((route_picks & kept_rows[:, None]).astype(jnp.int32), axis=0)
    lost_local = jnp.sum((route_picks & ~kept_rows[:, None]).astype(jnp.int32), axis=0)
    count_sums = lax.psum(jnp.stack([sent_local, lost_local]), ("dp", "fsdp"))
    grad_out = cotangent.astype(jnp.float32)
    grad_gate = jnp.sum(grad_out * returned, axis=1)
    grad_back = gate_value[:, None] * grad_out
    grad_result = (
        jnp.where(slot_filled[:, None], grad_back[slot_token], 0.0)
        .astype(jnp.bfloat16)
        .reshape(expert_count, capacity, model_width)
    )
    grad_result = lax.all_gather(grad_result, "dp", axis=1, tiled=True)
    grad_active = jnp.einsum(
        "ecd,fed->ecf", grad_result, expert_out, preferred_element_type=jnp.float32
    )
    unused_value, gelu_pullback = jax.vjp(partial(jax.nn.gelu, approximate=True), expert_inner)
    grad_inner = gelu_pullback(grad_active)[0].astype(jnp.bfloat16)
    grad_slots = lax.psum_scatter(
        jnp.einsum("ecf,fed->ecd", grad_inner, expert_in, preferred_element_type=jnp.float32),
        "dp",
        scatter_dimension=1,
        tiled=True,
    ).reshape(expert_count * capacity, model_width)
    grad_normed_two = jnp.where(kept_rows[:, None], grad_slots[slot_code], 0.0)
    grad_probs = jnp.where(route_hot, grad_gate[:, None], 0.0)
    grad_logits = router_probs * (
        grad_probs - jnp.sum(router_probs * grad_probs, axis=1, keepdims=True)
    )
    grad_normed_two = grad_normed_two + jnp.dot(
        grad_logits, weight_router.astype(jnp.float32).T, precision=top_probability
    )
    grad_hidden = (
        rms_backward(normed_two, inverse_two, gain_ffn.astype(jnp.float32), grad_normed_two)
        + grad_out
    )
    grad_hidden_low = grad_hidden.astype(jnp.bfloat16)
    grad_mixed = jnp.dot(grad_hidden_low, weight_out.T, preferred_element_type=jnp.float32).astype(
        jnp.bfloat16
    )
    joined_blocks, table_grads = lax.map(
        partial(attend_backward, complete_position_bias, bucket_indicator),
        (
            qkv_blocks,
            bucket_len,
            live_blocks,
            grad_mixed.reshape(block_total, LONG, model_width),
            log_totals,
        ),
    )
    grad_qkv = joined_blocks.reshape(token_count, 3 * model_width)
    grad_normed_one = jnp.dot(grad_qkv, weight_qkv.T, preferred_element_type=jnp.float32)
    grad_rows = rms_backward(
        normed_one, inverse_one, gain_attn.astype(jnp.float32), grad_normed_one
    )
    tokens_grad = (grad_rows + grad_hidden).astype(jnp.bfloat16)
    table_grad = lax.psum(jnp.sum(table_grads, axis=0), ("dp", "fsdp"))
    attn_term = jnp.sum(grad_normed_one * normed_one, axis=0)
    qkv_term = jnp.dot(normed_low.T, grad_qkv, preferred_element_type=jnp.float32)
    out_term = jnp.dot(mixed_low.T, grad_hidden_low, preferred_element_type=jnp.float32)
    ffn_term = jnp.sum(grad_normed_two * normed_two, axis=0)
    router_term = jnp.dot(normed_two_full.T, grad_logits, precision=top_probability)
    layer_summed = lax.psum_scatter(
        jnp.concatenate(
            [attn_term[:, None], qkv_term, out_term, ffn_term[:, None], router_term], axis=1
        ),
        ("dp", "fsdp"),
        scatter_dimension=0,
        tiled=True,
    )
    out_term = jnp.einsum(
        "ecf,ecd->fed", active_low, grad_result, preferred_element_type=jnp.float32
    )
    in_term = jnp.einsum("ecd,ecf->fed", slot_rows, grad_inner, preferred_element_type=jnp.float32)
    w_in_grad = lax.psum_scatter(in_term, "fsdp", scatter_dimension=0, tiled=True)
    w_out_grad = lax.psum_scatter(out_term, "fsdp", scatter_dimension=0, tiled=True)
    attn_gain_grad = layer_summed[:, 0]
    qkv_grad = layer_summed[:, 1 : 1 + 3 * model_width]
    out_grad = layer_summed[:, 1 + 3 * model_width : 1 + 4 * model_width]
    ffn_gain_grad = layer_summed[:, 1 + 4 * model_width]
    router_weight_gradient = layer_summed[:, 2 + 4 * model_width :]
    return (
        layer_out,
        tokens_grad,
        attn_gain_grad,
        qkv_grad,
        out_grad,
        table_grad,
        ffn_gain_grad,
        router_weight_gradient,
        w_in_grad,
        w_out_grad,
        count_sums[0],
        count_sums[1],
    )


def solution(mesh):
    both = ("dp", "fsdp")
    body = fused if (mesh.shape["dp"], mesh.shape["fsdp"]) == (4, 8) else per_device
    placed = (
        P(both, None), P(both), P(both), P(both, None), P(both), P(both, None), P(both, None), P(), P(both),
        P(both, None), P(both, None, None), P(both, None, None), P(both, None),
    )
    return jax.shard_map(
        body,
        mesh=mesh,
        in_specs=placed,
        out_specs=(
            P(both, None), P(both, None), P(both), P(both, None), P(both, None), P(), P(both), P(both, None),
            P(both, None, None), P(both, None, None), P(), P(),
        ),
        check_vma=False,
    )
```

```python
from functools import partial
import math

import jax
import jax.numpy as jnp
from jax import lax
from jax.experimental import pallas as pl
from jax.experimental.pallas import tpu as pltpu
from jax.sharding import PartitionSpec as P

F32 = jnp.float32
BF16 = jnp.bfloat16
MESH = pl.DeviceIdType.MESH

HEADS = 12
BUCKETS = 32
MAXDIST = 128
LONG = 512
NEG = -1e30
EPS = 1e-06
GELU_C = math.sqrt(2.0 / math.pi)


def nt(a, b):
    return lax.dot_general(a, b, (((1,), (1,)), ((), ())), preferred_element_type=F32)


def nn(a, b):
    return lax.dot_general(a, b, (((1,), (0,)), ((), ())), preferred_element_type=F32)


def tn(a, b):
    return lax.dot_general(a, b, (((0,), (0,)), ((), ())), preferred_element_type=F32)


def exact(a, b, dims):
    return lax.dot_general(
        a, b, (dims, ((), ())), precision=lax.Precision.HIGHEST, preferred_element_type=F32
    )


def iota(shape, axis):
    return lax.broadcasted_iota(jnp.int32, shape, axis)


def bucket_of(offset):
    distance = jnp.abs(offset)
    halfway = BUCKETS // 2
    exact_span = halfway // 2
    distant = jnp.full(offset.shape, exact_span, jnp.int32)
    for number in range(1, halfway - exact_span):
        threshold = math.ceil(
            exact_span * (MAXDIST / exact_span) ** (number / (halfway - exact_span))
        )
        distant = distant + jnp.where(distance >= threshold, 1, 0)
    return jnp.where(distance < exact_span, distance, distant) + jnp.where(offset > 0, halfway, 0)


def diagonal_sums(tile):
    wide = jnp.concatenate([tile, jnp.zeros((128, 128), F32)], axis=1)
    rows = 64
    while rows >= 8:
        wide = wide[:rows] + pltpu.roll(wide[rows : 2 * rows], 256 - rows, 1)
        rows //= 2
    while rows >= 1:
        wide = wide + pltpu.roll(pltpu.roll(wide, 256 - rows, 1), 8 - rows, 0)
        rows //= 2
    return wide[0:1]


VMEM_LIMIT = 63 << 20


def layer_kernel(
    tok, cot, routes, valid, length, rel, gain_a, gain_f, rshard, qshard, oshard, wi_hbm, wo_hbm,
    layer_out, tokens_grad, qkv_grad, out_grad, small_grad, router_grad, rel_grad, wi_grad, wo_grad, p_hbm,
    aq, ar, ao, wq, wo, sm_t, wb, xg, ycore, yx, ry, rz,
    qkvb, u1, obuf, u2, gobuf, hid, prob, code_row, cols, key_mask, tab, bias, pst, dst_s, gd, relg,
    smallp, lsc, lsx, lsy, lsz, fin,
    free,
    s1s, s1r, s3zs, s3ys, s3r, s3l, xs, xr, ycs, ycr, yxs, yxr, dys, dyr, dzs, dzr,
    rcs, rcr, rxs, rxr, rys, ryr, rzs, rzr, psem, fsem,
):
    dp = lax.axis_index("dp")
    fs = lax.axis_index("fsdp")
    x, c = dp // 2, lax.rem(dp, 2)
    z, y = fs // 2, lax.rem(fs, 2)
    xn, cn, yn = 1 - x, 1 - c, 1 - y
    NZ = 4
    NE = 4
    CAP = 160
    D = 768

    def at(xx, cc, zz, yy):
        return (xx * 2 + cc, zz * 2 + yy)

    core_d, x_d, y_d = at(x, cn, z, y), at(xn, c, z, y), at(x, c, z, yn)

    def zz_of(step):
        return lax.rem(z + step, NZ)

    def zb_of(step):
        return lax.rem(z - step + NZ, NZ)

    def z_d(step):
        return at(x, c, zz_of(step), y)

    def remote(src, dst, ss, rs, where):
        return pltpu.make_async_remote_copy(
            src_ref=src, dst_ref=dst, send_sem=ss, recv_sem=rs, device_id=where, device_id_type=MESH
        )

    for s in range(3):
        for half in range(2):
            for k in range(3):
                lanes = slice(half * 384 + k * 128, half * 384 + k * 128 + 128)
                piece = qshard[:, k * D + (2 * s + half) * 128 : k * D + (2 * s + half) * 128 + 128]
                if s < 2:
                    aq[dp, z, y, s, :, lanes] = piece
                else:
                    ar[dp, z, y, :, lanes] = piece
    ao[dp, z, y] = oshard[...]
    diagonal = iota((24, 24), 0) == iota((24, 24), 1)
    gain_cols = [
        jnp.sum(jnp.where(diagonal, g[...].astype(F32), 0.0), axis=1, keepdims=True) for g in (gain_a, gain_f)
    ]
    lane24 = iota((24, 128), 1)
    place4 = jnp.where(iota((NE, 128), 1) == iota((NE, 128), 0) + 2, 1.0, 0.0).astype(BF16)
    small = jnp.where(lane24 == 0, gain_cols[0], jnp.where(lane24 == 1, gain_cols[1], nn(rshard[...], place4)))
    ar[dp, z, y, :, D:] = small.astype(BF16)

    barrier = pltpu.get_barrier_semaphore()
    peers = [core_d, x_d, y_d, z_d(1), z_d(2), z_d(3)]
    for peer in peers:
        pl.semaphore_signal(barrier, inc=1, device_id=peer, device_id_type=MESH)
    pl.semaphore_wait(barrier, len(peers))

    def s1(part, slot, dpi, zi, yi, where):
        ref = (aq, ar, ao)[part].at[dpi, zi, yi]
        return remote(ref, ref, s1s.at[part, slot], s1r.at[part, dpi * 8 + zi * 2 + yi], where)

    started = ([], [], [])

    def go(part, *rest):
        copy = s1(part, *rest)
        copy.start()
        started[part].append(copy)

    dpx, dpc, dpd = xn * 2 + c, x * 2 + cn, xn * 2 + cn

    def s1_spread(part, st, zi):
        go(part, 3 + st, dp, zi, y, y_d)
        go(part, 7 + st, dp, zi, y, x_d)
        go(part, 15 + st, dp, zi, y, core_d)

    def s1_z(part, st):
        s1(part, 0, dp, zb_of(st), y, y_d).wait_recv()
        s1_spread(part, st, zb_of(st))

    def s1_second(part, st):
        zi = zb_of(st)
        if part == 0:
            s1(part, 0, dp, zi, yn, y_d).wait_recv()
            go(part, 11 + st, dp, zi, yn, x_d)
            go(part, 19 + st, dp, zi, yn, core_d)
        else:
            s1(part, 0, dpx, zi, y, x_d).wait_recv()
            go(part, 11 + st, dpx, zi, y, y_d)
            go(part, 19 + st, dpx, zi, y, core_d)

    def s1_third(part, st):
        zi = zb_of(st)
        for number, yi in ((0, y), (1, yn)):
            if part == 0:
                dpi, yj, where = dpx, yi, x_d
            else:
                dpi, yj, where = (dp, dpx)[number], yn, y_d
            s1(part, 0, dpi, zi, yj, where).wait_recv()
            go(part, 23 + number * 4 + st, dpi, zi, yj, core_d)

    def s1_end(part):
        for dpi in (dpc, dpd):
            for yi in range(2):
                for zi in range(4):
                    s1(part, 0, dpi, zi, yi, core_d).wait_recv()
        for copy in started[part]:
            copy.wait_send()

    for part in (0, 1):
        for st in (1, 2, 3):
            go(part, st - 1, dp, z, y, z_d(st))
        s1_spread(part, 0, z)

    LAST = 2 * NE - 1
    up_d, down_d = at(x, c, jnp.minimum(z + 1, NZ - 1), y), at(x, c, jnp.maximum(z - 1, 0), y)

    def s3_src(m, e):
        return (wi_hbm if m == 0 else wo_hbm).at[e]

    def s3_own(m, e):
        return pltpu.make_async_copy(s3_src(m, e), wb.at[m, e, z, y], s3l.at[m, e])

    def s3_y0(m, e):
        return remote(s3_src(m, e), wb.at[m, e, z, y], s3ys.at[m, e, 0], s3r.at[m, e, z, y], y_d)

    def s3_y(m, e, zi):
        ref = wb.at[m, e, zi, y]
        return remote(ref, ref, s3ys.at[m, e, lax.rem(zi - z + NZ, NZ)], s3r.at[m, e, zi, y], y_d)

    def s3_arrival(m, e, zi, yi):
        ref = wb.at[m, e, zi, yi]
        return remote(ref, ref, s3ys.at[m, e, 0], s3r.at[m, e, zi, yi], y_d)

    def s3_line(m, e, zi, yi, way, slot, src=None):
        dst = wb.at[m, e, zi, yi]
        return remote(
            dst if src is None else src, dst, s3zs.at[m, e, way * 8 + slot], s3r.at[m, e, zi, yi], (up_d, down_d)[way]
        )

    def onward(way):
        return z < NZ - 1 if way == 0 else z > 0

    def s3_issue_line(lo, hi):
        for i in range(lo, hi):
            m, e = i % 2, i // 2
            for way in (0, 1):
                pl.when(onward(way))(lambda: s3_line(m, e, z, y, way, 0, s3_src(m, e)).start())
            s3_own(m, e).start()

    def s3_issue_y(lo, hi):
        for i in range(lo, hi):
            s3_y0(i % 2, i // 2).start()

    def s3_pair(i, dist, across=False):
        m, e = (i % 2, i // 2) if isinstance(i, int) else (lax.rem(i, 2), i // 2)
        yi = yn if across else y
        for way in (0, 1):
            zi = z - dist if way == 0 else z + dist
            here = zi >= 0 if way == 0 else zi < NZ
            zi = jnp.clip(zi, 0, NZ - 1)

            @pl.when(here)
            def _():
                s3_arrival(m, e, zi, yi).wait_recv()

                @pl.when(onward(way))
                def _():
                    s3_line(m, e, zi, yi, way, dist + (4 if across else 0)).start()

                if not (isinstance(i, int) and i == LAST):
                    s3_y(m, e, zi).start()

    def s3_across():
        m, e = 1, NE - 1
        s3_arrival(m, e, z, yn).wait_recv()
        for way in (0, 1):
            pl.when(onward(way))(lambda: s3_line(m, e, z, yn, way, 4).start())

    def s3_finish(e):
        for m in range(2):
            s3_own(m, e).wait()
            if 2 * e + m != LAST:
                for st in range(4):
                    s3_arrival(m, e, zz_of(st), yn).wait_recv()

    def s3_sent(e):
        for m in range(2):
            last = 2 * e + m == LAST
            s3_y0(m, e).wait_send()
            for st in (1, 2, 3):
                if not last:
                    s3_y(m, e, zz_of(st)).wait_send()
            for way in (0, 1):
                for dist in range(4):
                    origin = z >= dist if way == 0 else z + dist < NZ
                    for slot in (dist, dist + 4)[: 2 if last else 1]:
                        pl.when(origin & onward(way))(lambda: s3_line(m, e, z, y, way, slot).wait_send())

    route_v = routes[...]
    live_v = valid[...] > 0
    picks = jnp.where((iota((8, LONG), 0) == route_v) & live_v, 1.0, 0.0)
    upto = jnp.where(iota((LONG, LONG), 0) <= iota((LONG, LONG), 1), 1.0, 0.0).astype(BF16)
    counts = nn(picks.astype(BF16), upto)
    place = jnp.sum(picks * counts, axis=0, keepdims=True).astype(jnp.int32) - 1
    kept = live_v & (place < CAP)
    code = jnp.where(kept, route_v * CAP + place, -1)
    code_row[...] = code
    keptf = jnp.where(kept, 1.0, 0.0)
    sent = jnp.sum(picks * keptf, axis=1, keepdims=True)
    lost = jnp.sum(picks * (1.0 - keptf), axis=1, keepdims=True)
    lane128 = iota((8, 128), 1)
    relg[3] = jnp.zeros((16, 256), F32)
    relg[3, 0:8, 0:128] = jnp.where(lane128 == 64, sent, 0.0) + jnp.where(lane128 == 65, lost, 0.0)
    stacked = jnp.concatenate(
        [
            jnp.broadcast_to(code.astype(F32), (8, LONG)),
            jnp.broadcast_to(route_v.astype(F32), (8, LONG)),
            jnp.zeros((112, LONG), F32),
        ],
        axis=0,
    )
    cols[...] = jnp.transpose(stacked)
    same = (iota((8, LONG), 1) // 128 == iota((8, LONG), 0)) | (length[0] >= LONG)
    key_mask[...] = jnp.where(same & live_v, 0.0, NEG)

    for st in (1, 2, 3):
        for part in (0, 1):
            s1_z(part, st)
    for st in (1, 2, 3):
        go(2, st - 1, dp, z, y, z_d(st))
    s3_issue_line(0, 4)
    s3_issue_y(0, 4)

    rel16 = jnp.concatenate([rel[...], jnp.zeros((4, BUCKETS), F32)], axis=0)

    def bucket_hot(kind, axis):
        shape = (BUCKETS, 256) if axis == 0 else (256, BUCKETS)
        lane = iota(shape, 1 - axis)
        offset = jnp.where(lane < 128, lane, lane - 256) + (0, 128, -128)[kind]
        return jnp.where(bucket_of(offset) == iota(shape, axis), 1.0, 0.0)

    rows_by_kind = [exact(rel16, bucket_hot(kind, 0), ((1,), (0,))) for kind in range(3)]
    for b in (BUCKETS // 2 - 1, BUCKETS - 1):
        rows_by_kind.append(exact(rel16, jnp.where(iota((BUCKETS, 256), 0) == b, 1.0, 0.0), ((1,), (0,))))
    for head in range(HEADS):
        for kind in range(5):
            tab[head, kind : kind + 1, :] = rows_by_kind[kind][head : head + 1]

    for st in range(4):
        for part in (0, 1):
            s1_second(part, st)
    for st in range(4):
        for part in (0, 1):
            s1_third(part, st)
    for part in (0, 1):
        s1_end(part)
    s1_spread(2, 0, z)
    for st in (1, 2, 3):
        s1_z(2, st)
    for pair in range(3):
        s3_pair(0, 1 + pair)

    @pl.loop(0, 4)
    def _(dpi):
        for zi in range(4):
            base = pl.multiple_of((dpi * 8 + zi * 2) * 24, 16)
            for s in range(2):
                v = aq[dpi, zi, :, s].astype(F32).reshape(48, D)
                wq[s, pl.ds(base, 48)] = v.astype(BF16)
            v = ar[dpi, zi].astype(F32).reshape(48, D + 128).astype(BF16)
            wq[2, pl.ds(base, 48)] = v[:, :D]
            wo[pl.ds(base, 48), D:] = v[:, D:]

    sm_t[...] = jnp.transpose(wo[:, D:].astype(F32))
    gain1 = sm_t[0:1, :]
    gain2 = sm_t[1:2, :]

    @pl.loop(0, 4)
    def _(rb):
        rows = pl.ds(pl.multiple_of(rb * 128, 128), 128)
        xf = tok[rows].astype(F32)
        r1 = lax.rsqrt(jnp.mean(xf * xf, axis=-1, keepdims=True) + EPS)
        u1[rows] = (xf * r1 * gain1).astype(BF16)

    for s in range(3):
        qkvb[s] = nn(u1[...], wq[s]).astype(BF16)

    lane_low = iota((LONG, 128), 1) < 64

    def head_mask(v, h2):
        return jnp.where(lane_low if h2 == 0 else ~lane_low, v, jnp.zeros((), v.dtype))

    def p_copy(hp, out):
        slot = lax.rem(hp, 2)
        if out:
            return pltpu.make_async_copy(pst.at[slot], p_hbm.at[hp], psem.at[slot])
        return pltpu.make_async_copy(p_hbm.at[hp], pst.at[slot], psem.at[slot])

    def forward(hp):
        slot = lax.rem(hp, 2)
        s, base = hp // 2, pl.multiple_of(lax.rem(hp, 2) * 384, 128)
        q2 = qkvb[s, :, pl.ds(base, 128)]
        k2 = qkvb[s, :, pl.ds(base + 128, 128)]
        v2 = qkvb[s, :, pl.ds(base + 256, 128)]

        @pl.when(hp >= 2)
        def _():
            p_copy(hp, True).wait()

        for h2 in range(2):
            head = hp * 2 + h2
            qm = head_mask(q2, h2) * jnp.asarray(0.125, BF16)
            vm = head_mask(v2, h2)
            for kind in range(3):
                row = tab[head, kind : kind + 1, :]
                tile = pltpu.roll(jnp.broadcast_to(row, (128, 256)), 0, 1, stride=1, stride_axis=0)
                bias[kind] = tile[:, :128]
            left = jnp.broadcast_to(tab[head, 3:4, 0:128], (128, 128))
            right = jnp.broadcast_to(tab[head, 4:5, 0:128], (128, 128))
            for bi in range(4):
                rows = slice(bi * 128, bi * 128 + 128)
                sc = nt(qm[rows], k2)
                tiles = [
                    bias[0] if bj == bi else bias[1] if bj == bi + 1 else bias[2] if bj == bi - 1
                    else right if bj > bi else left
                    for bj in range(4)
                ]
                sc = sc + jnp.concatenate(tiles, axis=1) + key_mask[bi : bi + 1, :]
                peak = jnp.max(sc, axis=-1, keepdims=True)
                ex = jnp.exp(sc - peak)
                p = (ex * (1.0 / jnp.sum(ex, axis=-1, keepdims=True))).astype(BF16)
                pst[slot, h2, rows] = p
                part = nn(p, vm)
                if h2 == 0:
                    hid[rows, 0:128] = part
                else:
                    obuf[rows, pl.ds(pl.multiple_of(hp * 128, 128), 128)] = (
                        hid[rows, 0:128] + part
                    ).astype(BF16)
        p_copy(hp, True).start()
        for number in range(2):
            pair = 3 + 2 * hp + number
            s3_pair(pair // 3, 1 + lax.rem(pair, 3))


    pl.loop(0, 2)(forward)
    for st in range(4):
        s1_second(2, st)
    s3_issue_line(4, 8)
    s3_issue_y(4, 8)
    pl.loop(2, 4)(forward)
    for st in range(4):
        s1_third(2, st)
    pl.loop(4, HEADS // 2)(forward)
    s1_end(2)
    s3_across()
    @pl.loop(0, 4)
    def _(dpi):
        for zi in range(4):
            base = pl.multiple_of((dpi * 8 + zi * 2) * 24, 16)
            wo[pl.ds(base, 48), :D] = ao[dpi, zi].astype(F32).reshape(48, D).astype(BF16)

    for peer in peers:
        pl.semaphore_signal(free, inc=1, device_id=peer, device_id_type=MESH)

    lane = iota((128, 128), 1)
    is_logit = (lane >= 2) & (lane < 2 + NE)

    def probs_of(logits):
        lm = jnp.where(is_logit, logits, NEG)
        ex = jnp.where(is_logit, jnp.exp(lm - jnp.max(lm, axis=-1, keepdims=True)), 0.0)
        return ex / jnp.sum(ex, axis=-1, keepdims=True)

    @pl.loop(0, 4)
    def _(rb):
        rows = pl.ds(pl.multiple_of(rb * 128, 128), 128)
        h = tok[rows].astype(F32) + nn(obuf[rows], wo[:, :D])
        hid[rows] = h
        r2 = lax.rsqrt(jnp.mean(h * h, axis=-1, keepdims=True) + EPS)
        u = (h * r2 * gain2).astype(BF16)
        u2[rows] = u
        pr = probs_of(nn(u, wo[:, D:]))
        prob[rows] = pr
        hot = (lane - 2) == cols[rows, 8:9].astype(jnp.int32)
        gate = jnp.sum(jnp.where(hot, pr, 0.0), axis=-1, keepdims=True)
        gobuf[rows] = (gate * cot[rows].astype(F32)).astype(BF16)

    def xg_send(kind, e):
        if kind == 0:
            return remote(xg.at[dp, e], xg.at[dp, e], xs.at[0, e], xr.at[dp, e], x_d)
        if kind == 1:
            return remote(xg.at[dp, e], xg.at[dp, e], xs.at[1, e], xr.at[dp, e], core_d)
        return remote(xg.at[dpx, e], xg.at[dpx, e], xs.at[2, e], xr.at[dpx, e], core_d)

    def xg_arrival(dpi, e):
        return remote(xg.at[dpi, e], xg.at[dpi, e], xs.at[0, e], xr.at[dpi, e], x_d)

    for e in range(NE):
        hot = jnp.where(iota((CAP, LONG), 0) + e * CAP == code_row[...], 1.0, 0.0).astype(BF16)
        xg[dp, e, 0] = nn(hot, u2[...]).astype(BF16)
        xg[dp, e, 1] = nn(hot, gobuf[...]).astype(BF16)
        if e == 0:
            xg_send(0, e).start()
        xg_send(1, e).start()

    for dist in (1, 2, 3):
        s3_pair(5, dist)

    def yc_send(xi, e):
        return remote(xg.at[xi * 2 + cn, e], ycore.at[xi, e], ycs.at[xi, e], ycr.at[xi, e], core_d)

    def yx_send(e):
        return remote(xg.at[dpx, e], yx.at[e], yxs.at[e], yxr.at[e], x_d)

    def dy_send(m, e):
        return remote(wb.at[m, e, :, yn], ry.at[m, e], dys.at[m, e], dyr.at[m, e], y_d)

    z1 = z + 1 - 2 * lax.rem(z, 2)
    z2 = zz_of(2)
    z3 = lax.rem(z1 + 2, NZ)

    def dz_send(m, e, slot):
        zi, zd = ((z1, z1), (z3, z1), (z2, z2))[slot]
        return remote(
            wb.at[m, e, zi, y], rz.at[m, e, slot], dzs.at[m, e, slot], dzr.at[m, e, slot], at(x, c, zd, y)
        )

    def sum_x(e):
        for xi in range(2):
            yc_send(xi, e).wait_recv()
        xg[dpx, e] = (xg[dpx, e].astype(F32) + ycore[xn, e].astype(F32)).astype(BF16)
        yx_send(e).start()

    def sum_z(e):
        for m in range(2):
            dy_send(m, e).wait_recv()
            for zi, slot in ((z3, 1), (z1, 0), (z2, None), (z, None)):
                wb[m, e, zi, y] = (wb[m, e, zi, y].astype(F32) + ry[m, e, zi].astype(F32)).astype(BF16)
                if slot is not None:
                    dz_send(m, e, slot).start()

    def dl_z1(m, slot):
        return remote(
            wb.at[m, NE - 1, (z1, z3)[slot]], ry.at[m, NE - 1, pl.ds(2 * slot, 2)],
            dzs.at[m, NE - 1, slot], dzr.at[m, NE - 1, slot], at(x, c, z1, y),
        )

    def dl_z2(m):
        return remote(
            wb.at[m, NE - 1, z2], rz.at[m, NE - 1, pl.ds(0, 2)], dzs.at[m, NE - 1, 2], dzr.at[m, NE - 1, 2],
            at(x, c, z2, y),
        )

    def dl_y(m):
        return remote(wb.at[m, NE - 1, z, yn], rz.at[m, NE - 1, 2], dys.at[m, NE - 1], dyr.at[m, NE - 1], y_d)

    def last_issue():
        for m in range(2):
            for slot in (1, 0):
                dl_z1(m, slot).start()

    def last_z2():
        e = NE - 1
        for m in range(2):
            dl_z1(m, 1).wait_recv()
            wb[m, e, z2] = (wb[m, e, z2].astype(F32) + ry[m, e, 2:4].astype(F32)).astype(BF16)
            dl_z2(m).start()

    def last_y():
        e = NE - 1
        for m in range(2):
            dl_z1(m, 0).wait_recv()
            dl_z2(m).wait_recv()
            wb[m, e, z] = (
                wb[m, e, z].astype(F32) + ry[m, e, 0:2].astype(F32) + rz[m, e, 0:2].astype(F32)
            ).astype(BF16)
            dl_y(m).start()

    def sum_w(e):
        for m in range(2):
            dz_send(m, e, 1).wait_recv()
            wb[m, e, z2, y] = (wb[m, e, z2, y].astype(F32) + rz[m, e, 1].astype(F32)).astype(BF16)
            dz_send(m, e, 2).start()

    def fin_copy(number):
        e, m = number // 2, number % 2
        return pltpu.make_async_copy(fin.at[m], (wi_grad if m == 0 else wo_grad).at[e], fsem.at[m])

    def grad_final(e):
        for m in range(2):
            total = wb[m, e, z, y].astype(F32)
            if e == NE - 1:
                dl_y(m).wait_recv()
                total = total + rz[m, e, 2].astype(F32)
            else:
                for slot in (0, 2):
                    dz_send(m, e, slot).wait_recv()
                    total = total + rz[m, e, slot].astype(F32)
            number = e * 2 + m
            if number >= 2:
                fin_copy(number - 2).wait()
            fin[m] = total
            fin_copy(number).start()

    def forward_x(e):
        xg_arrival(dpx, e).wait_recv()
        if e < NE - 1:
            xg_send(0, e + 1).start()
        xg_send(2, e).start()

    PAIRS = (
        ((6, 1),), ((6, 2),), ((6, 3),), ((LAST, 1), (LAST, 1, True)),
        ((LAST, 2), (LAST, 2, True)), ((LAST, 3), (LAST, 3, True)), (), (),
    )
    forward_x(0)
    for e in range(NE):
        if e >= 1:
            sum_x(e - 1)
        xg_arrival(dpc, e).wait_recv()
        xg_arrival(xn * 2 + cn, e).wait_recv()
        s3_finish(e)
        for kind in range(3):
            xg_send(kind, e).wait_send()
        s3_sent(e)
        half = 4 * 96
        for fc in range(2):
            zs = slice(2 * fc, 2 * fc + 2)
            xv = xg[:, e, 0].reshape(4 * CAP, D)
            gv = xg[:, e, 1].reshape(4 * CAP, D)
            wi_v = wb[0, e, zs].reshape(half, D)
            wo_v = wb[1, e, zs].reshape(half, D)
            zv = nt(xv, wi_v)
            ga = nt(gv, wo_v)
            t = jnp.tanh(GELU_C * (zv + 0.044715 * (zv * zv * zv)))
            act = (0.5 * zv * (1.0 + t)).astype(BF16)
            slope = 0.5 * (1.0 + t) + (0.5 * GELU_C) * zv * (1.0 - t * t) * (
                1.0 + (3 * 0.044715) * (zv * zv)
            )
            gz = (ga * slope).astype(BF16)
            if fc == 0:
                yacc = nn(act, wo_v)
                gacc = nn(gz, wi_v)
                pst_y, pst_g = yacc, gacc
            else:
                pst_y = pst_y + nn(act, wo_v)
                pst_g = pst_g + nn(gz, wi_v)
            wb[1, e, zs] = tn(act, gv).astype(BF16).reshape(2, 2, 96, D)
            wb[0, e, zs] = tn(gz, xv).astype(BF16).reshape(2, 2, 96, D)
            for pair in PAIRS[e * 2 + fc]:
                s3_pair(*pair)
            if fc == 1 and e < NE - 1:
                forward_x(e + 1)
        xg[:, e, 0] = pst_y.astype(BF16).reshape(4, CAP, D)
        xg[:, e, 1] = pst_g.astype(BF16).reshape(4, CAP, D)
        for xi in range(2):
            yc_send(xi, e).start()
        if e < NE - 1:
            for m in range(2):
                dy_send(m, e).start()
        else:
            last_issue()
        if e == 2:
            sum_z(0)
    sum_x(NE - 1)
    sum_z(1)

    for e in range(NE):
        yx_send(e).wait_recv()
        xg[dp, e] = (xg[dp, e].astype(F32) + ycore[x, e].astype(F32) + yx[e].astype(F32)).astype(BF16)
    gd[0:8] = jnp.zeros((8, D), F32)

    @pl.loop(0, 4)
    def _(rb):
        rows = pl.ds(pl.multiple_of(rb * 128, 128), 128)
        code_col = cols[rows, 0:1].astype(jnp.int32)
        back = jnp.where(iota((128, NE * CAP), 1) == code_col, 1.0, 0.0).astype(BF16)
        yt = nn(back, xg[dp, :, 0].reshape(NE * CAP, D))
        gxt = nn(back, xg[dp, :, 1].reshape(NE * CAP, D))
        h = hid[rows]
        g = cot[rows].astype(F32)
        pr = prob[rows]
        hot = (lane - 2) == cols[rows, 8:9].astype(jnp.int32)
        gate = jnp.sum(jnp.where(hot, pr, 0.0), axis=-1, keepdims=True)
        layer_out[rows] = (h + gate * yt).astype(BF16)
        ggate = jnp.sum(g * yt, axis=-1, keepdims=True)
        dprob = jnp.where(hot, ggate, 0.0)
        dlog = pr * (dprob - jnp.sum(pr * dprob, axis=-1, keepdims=True))
        prob[rows] = dlog
        hi = dlog.astype(BF16)
        lo = (dlog - hi.astype(F32)).astype(BF16)
        wr_t = sm_t[...].astype(BF16)
        gu = gxt + nn(hi, wr_t) + nn(lo, wr_t)
        r2 = lax.rsqrt(jnp.mean(h * h, axis=-1, keepdims=True) + EPS)
        n2 = h * r2
        gd[1:2] = gd[1:2] + jnp.sum(gu * n2, axis=0, keepdims=True)
        mm = gu * gain2
        gh = g + r2 * (mm - n2 * jnp.mean(mm * n2, axis=-1, keepdims=True))
        hid[rows] = gh
        ghb = gh.astype(BF16)
        gobuf[rows] = nt(ghb, wo[:, :D]).astype(BF16)
        tokens_grad[rows] = ghb

    dlog = prob[...]
    dlog_hi = dlog.astype(BF16)
    router_part = tn(u2[...], dlog_hi) + tn(u2[...], (dlog - dlog_hi.astype(F32)).astype(BF16))

    for e in range(NE):
        for xi in range(2):
            yc_send(xi, e).wait_send()
        yx_send(e).wait_send()
    pl.semaphore_wait(free, len(peers))

    def pack(unit, lanes, width, value):
        for d in range(32):
            xg[d // 8, d % 8 // 2, d % 2, unit * 32 : unit * 32 + 24, lanes] = value[
                24 * d : 24 * d + 24
            ].astype(BF16)

    def lands(unit):
        if unit == 4:
            return lsc, lsx, lsy, lsz
        if unit == 3:
            return ao.at[0:2], ao.at[2], ao.at[3, :, 0], ao.at[3, 0:3, 1]
        if unit == 2:
            full = pl.ds(0, D)
            return (
                ar.at[0:2, :, :, :, full], ar.at[2, :, :, :, full],
                ar.at[3, :, 0, :, full], ar.at[3, 0:3, 1, :, full],
            )
        return aq.at[0:2, :, :, unit], aq.at[2, :, :, unit], aq.at[3, :, 0, unit], aq.at[3, 0:3, 1, unit]

    def part_ref(unit):
        if unit == 4:
            return smallp
        return xg.at[:, :, :, pl.ds(unit * 32, 24), :]

    def narrow(unit, v):
        return v if unit == 4 else v.astype(BF16)

    def rs_core(unit, xi):
        return remote(
            part_ref(unit).at[xi * 2 + cn], lands(unit)[0].at[xi], rcs.at[unit, xi], rcr.at[unit, xi], core_d
        )

    def rs_x(unit):
        return remote(part_ref(unit).at[dpx], lands(unit)[1], rxs.at[unit], rxr.at[unit], x_d)

    def rs_y(unit):
        return remote(part_ref(unit).at[dp, :, yn], lands(unit)[2], rys.at[unit], ryr.at[unit], y_d)

    def rs_z(unit, st):
        dst = lands(unit)[3].at[z] if unit == 4 else lands(unit)[3].at[st - 1]
        return remote(
            part_ref(unit).at[dp, zz_of(st), y], dst, rzs.at[unit, st - 1], rzr.at[unit, st - 1], z_d(st)
        )

    def st_core(unit):
        for xi in range(2):
            rs_core(unit, xi).start()

    def st_x(unit):
        mine, (lc, _, _, _) = part_ref(unit), lands(unit)
        for xi in range(2):
            rs_core(unit, xi).wait_recv()
        for zi in range(4):
            mine[dpx, zi] = narrow(unit, mine[dpx, zi].astype(F32) + lc[xn, zi].astype(F32))
        rs_x(unit).start()

    def st_y(unit):
        mine, (lc, lx, _, _) = part_ref(unit), lands(unit)
        rs_x(unit).wait_recv()
        for zi in range(4):
            mine[dp, zi] = narrow(
                unit, mine[dp, zi].astype(F32) + lc[x, zi].astype(F32) + lx[zi].astype(F32)
            )
        rs_y(unit).start()

    def st_z(unit):
        mine, (_, _, ly, _) = part_ref(unit), lands(unit)
        rs_y(unit).wait_recv()
        for zi in range(4):
            mine[dp, zi, y] = narrow(unit, mine[dp, zi, y].astype(F32) + ly[zi].astype(F32))
        for st in (1, 2, 3):
            rs_z(unit, st).start()

    def st_final(unit):
        mine, (_, _, _, lz) = part_ref(unit), lands(unit)
        for st in (1, 2, 3):
            rs_z(unit, st).wait_recv()
        if unit == 4:
            lz[z] = mine[dp, z, y]
            return (lz[0] + lz[1]) + (lz[2] + lz[3])
        total = mine[dp, z, y].astype(F32)
        for st in (1, 2, 3):
            total = total + lz[st - 1].astype(F32)
        return total

    def st_sent(unit):
        for xi in range(2):
            rs_core(unit, xi).wait_send()
        rs_x(unit).wait_send()
        rs_y(unit).wait_send()
        for st in (1, 2, 3):
            rs_z(unit, st).wait_send()

    for half in range(2):
        lanes = slice(half * 384, half * 384 + 384)
        pack(3, lanes, 384, tn(obuf[...], tokens_grad[:, lanes]))
    st_core(3)
    sum_w(0)
    last_z2()
    sum_z(2)

    relg[0] = jnp.zeros((16, 256), F32)
    relg[1] = jnp.zeros((16, 256), F32)
    relg[2] = jnp.zeros((16, 256), F32)
    p_copy(4, True).wait()
    p_copy(5, True).wait()
    p_copy(0, False).start()

    def backward(hp):
        slot = hp % 2
        s, base = hp // 2, (hp % 2) * 384
        p_copy(hp, False).wait()
        if hp < 5:
            p_copy(hp + 1, False).start()
        q2 = qkvb[s, :, base : base + 128]
        k2 = qkvb[s, :, base + 128 : base + 256]
        v2 = qkvb[s, :, base + 256 : base + 384]
        go2 = gobuf[:, hp * 128 : hp * 128 + 128]
        eighth = jnp.asarray(0.125, BF16)
        for h2 in range(2):
            head = hp * 2 + h2
            qm = head_mask(q2, h2) * eighth
            km = head_mask(k2, h2) * eighth
            gm = head_mask(go2, h2)
            tiles = [None] * 5
            for bi in range(4):
                rows = slice(bi * 128, bi * 128 + 128)
                pv = pst[slot, h2, rows].astype(F32)
                dpv = nt(gm[rows], v2)
                ds = pv * (dpv - jnp.sum(pv * dpv, axis=-1, keepdims=True))
                dst_s[rows] = ds.astype(BF16)
                for bj in range(4):
                    kind = 0 if bj == bi else 1 if bj == bi + 1 else 2 if bj == bi - 1 else 4 if bj > bi else 3
                    tile = ds[:, bj * 128 : bj * 128 + 128]
                    tiles[kind] = tile if tiles[kind] is None else tiles[kind] + tile
            for kind in range(3):
                relg[kind, head : head + 1, :] = diagonal_sums(tiles[kind])
            relg[3, head : head + 1, 128:256] = jnp.sum(tiles[3], axis=0, keepdims=True)
            relg[4, head : head + 1, 0:128] = jnp.sum(tiles[4], axis=0, keepdims=True)
            dsb = dst_s[...]
            dq = nn(dsb, km)
            dk = tn(dsb, qm)
            dv = tn(pst[slot, h2], gm)
            if h2 == 0:
                grad3 = [dq, dk, dv]
            else:
                grad3 = [a + b for a, b in zip(grad3, (dq, dk, dv))]
        for k in range(3):
            qkvb[s, :, base + k * 128 : base + k * 128 + 128] = grad3[k].astype(BF16)
        pack(s, slice(base, base + 384), 384, tn(u1[...], qkvb[s, :, base : base + 384]))

    backward(0)
    st_x(3)
    backward(1)
    st_core(0)
    st_y(3)
    sum_w(1)
    last_y()
    backward(2)
    st_x(0)
    st_z(3)
    backward(3)
    st_core(1)
    st_y(0)
    backward(4)
    sum_w(2)
    st_x(1)
    st_z(0)
    backward(5)
    st_core(2)
    st_y(1)

    @pl.loop(0, 4)
    def _(rb):
        rows = pl.ds(pl.multiple_of(rb * 128, 128), 128)
        gu = nt(qkvb[0, rows], wq[0]) + nt(qkvb[1, rows], wq[1]) + nt(qkvb[2, rows], wq[2])
        xf = tok[rows].astype(F32)
        r1 = lax.rsqrt(jnp.mean(xf * xf, axis=-1, keepdims=True) + EPS)
        n1 = xf * r1
        gd[0:1] = gd[0:1] + jnp.sum(gu * n1, axis=0, keepdims=True)
        mm = gu * gain1
        grad = hid[rows] + r1 * (mm - n1 * jnp.mean(mm * n1, axis=-1, keepdims=True))
        tokens_grad[rows] = grad.astype(BF16)

    st_x(2)
    st_z(1)

    gains = jnp.concatenate([gd[0:8], jnp.zeros((120, D), F32)], axis=0)
    gain_cols = jnp.transpose(gains)
    lane768 = iota((D, 128), 1)
    small_cols = jnp.where(lane768 < 2, gain_cols, jnp.where(lane768 < 2 + NE, router_part, 0.0))
    table = jnp.zeros((16, BUCKETS), F32)
    for kind in range(3):
        table = table + exact(relg[kind], bucket_hot(kind, 1), ((1,), (0,)))
    far_b = iota((128, BUCKETS), 1)
    table = table + exact(
        relg[3, :, 128:256], jnp.where(far_b == BUCKETS // 2 - 1, 1.0, 0.0), ((1,), (0,))
    )
    table = table + exact(relg[4, :, 0:128], jnp.where(far_b == BUCKETS - 1, 1.0, 0.0), ((1,), (0,)))
    extra = jnp.concatenate(
        [
            jnp.zeros((16, 32), F32),
            table,
            relg[3, :, 64:128],
        ],
        axis=1,
    )
    extra = jnp.concatenate([extra, jnp.zeros((8, 128), F32)], axis=0)
    for d in range(32):
        smallp[d // 8, d % 8 // 2, d % 2] = small_cols[24 * d : 24 * d + 24] + extra
    st_core(4)
    st_y(2)
    st_x(4)
    grad_final(0)
    grad_final(1)
    st_z(2)
    st_y(4)
    grad_final(2)
    out_grad[...] = st_final(3)
    st_z(4)

    def write_qkv(unit):
        total = st_final(unit)
        for half in range(2):
            for k in range(3):
                qkv_grad[:, k * D + (2 * unit + half) * 128 : k * D + (2 * unit + half) * 128 + 128] = total[
                    :, half * 384 + k * 128 : half * 384 + k * 128 + 128
                ]

    write_qkv(0)
    write_qkv(1)
    grad_final(3)
    write_qkv(2)
    small_total = st_final(4)
    small_grad[...] = small_total
    router_grad[...] = small_total[:, 2 : 2 + NE]
    rel_grad[...] = small_total[:HEADS, 32 : 32 + BUCKETS]
    fin_copy(2 * NE - 2).wait()
    fin_copy(2 * NE - 1).wait()

    for e in range(NE):
        for m in range(2):
            if e == NE - 1:
                for copy in (dl_z1(m, 0), dl_z1(m, 1), dl_z2(m), dl_y(m)):
                    copy.wait_send()
            else:
                dy_send(m, e).wait_send()
                for slot in range(3):
                    dz_send(m, e, slot).wait_send()
    for unit in range(5):
        st_sent(unit)


def fused(
    tokens, bucket_len, valid, routes, attn_gain, qkv_weight, out_weight, rel, ffn_gain, router_weight,
    w_in, w_out, cotangent,
):
    tok_n, D = tokens.shape
    vm = pl.BlockSpec(memory_space=pltpu.VMEM)
    hbm = pl.BlockSpec(memory_space=pl.ANY)
    sds = jax.ShapeDtypeStruct
    V = pltpu.VMEM
    sem = lambda *s: pltpu.SemaphoreType.DMA(s)
    outs = pl.pallas_call(
        layer_kernel,
        out_shape=(
            sds((512, 768), BF16), sds((512, 768), BF16), sds((24, 2304), F32), sds((24, 768), F32),
            sds((24, 128), F32), sds((24, 4), F32), sds((12, 32), F32), sds((4, 96, 768), F32), sds((4, 96, 768), F32), sds((6, 2, 512, 512), BF16),
        ),
        in_specs=[vm, vm, vm, vm, pl.BlockSpec(memory_space=pltpu.SMEM), vm, vm, vm, vm, vm, vm, hbm, hbm],
        out_specs=(vm,) * 7 + (hbm,) * 3,
        scratch_shapes=[
            V((4, 4, 2, 2, 24, 768), BF16),
            V((4, 4, 2, 24, 896), BF16),
            V((4, 4, 2, 24, 768), BF16),
            V((3, 768, 768), BF16),
            V((768, 896), BF16),
            V((128, 768), F32),
            V((2, 4, 4, 2, 96, 768), BF16),
            V((4, 4, 2, 160, 768), BF16),
            V((2, 4, 2, 160, 768), BF16),
            V((4, 2, 160, 768), BF16),
            V((2, 4, 4, 96, 768), BF16),
            V((2, 4, 3, 96, 768), BF16),
            V((3, 512, 768), BF16),
            V((512, 768), BF16),
            V((512, 768), BF16),
            V((512, 768), BF16),
            V((512, 768), BF16),
            V((512, 768), F32),
            V((512, 128), F32),
            V((1, 512), jnp.int32),
            V((512, 128), F32),
            V((8, 512), F32),
            V((12, 8, 256), F32),
            V((3, 128, 128), F32),
            V((2, 2, 512, 512), BF16),
            V((512, 512), BF16),
            V((8, 768), F32),
            V((5, 16, 256), F32),
            V((4, 4, 2, 24, 128), F32),
            V((2, 4, 2, 24, 128), F32),
            V((4, 2, 24, 128), F32),
            V((4, 24, 128), F32),
            V((4, 24, 128), F32),
            V((2, 96, 768), F32),
            pltpu.SemaphoreType.REGULAR,
            sem(3, 31), sem(3, 32), sem(2, 4, 16), sem(2, 4, 4), sem(2, 4, 4, 2), sem(2, 4),
            sem(3, 4), sem(4, 4), sem(2, 4), sem(2, 4), sem(4), sem(4), sem(2, 4), sem(2, 4),
            sem(2, 4, 3), sem(2, 4, 3),
            sem(5, 2), sem(5, 2), sem(5), sem(5), sem(5), sem(5), sem(5, 3), sem(5, 4), sem(2), sem(2),
        ],
        compiler_params=pltpu.CompilerParams(
            collective_id=0, has_side_effects=True, vmem_limit_bytes=VMEM_LIMIT
        ),
        cost_estimate=pl.CostEstimate(flops=40_000_000_000, bytes_accessed=30_000_000, transcendentals=8_000_000),
    )(
        tokens, cotangent, routes.reshape(1, tok_n), valid.reshape(1, tok_n), bucket_len, rel,
        attn_gain[None, :], ffn_gain[None, :], router_weight, qkv_weight, out_weight, jnp.transpose(w_in, (1, 0, 2)), jnp.transpose(w_out, (1, 0, 2)),
    )
    lo, tg, qg, og, sg, rg, tb, wig, wog, _ = outs
    counts = sg[:4, 64:66].astype(jnp.int32)
    return (
        lo, tg, sg[:, 0], qg, og, tb, sg[:, 1], rg,
        jnp.transpose(wig, (1, 0, 2)), jnp.transpose(wog, (1, 0, 2)), counts[:, 0], counts[:, 1],
    )


epsilon = 1e-06


def bucket_codes(block_span, bucket_count, reach):
    position = jnp.arange(block_span, dtype=jnp.int32)
    offset_grid = position[None, :] - position[:, None]
    distance = jnp.abs(offset_grid)
    halfway = bucket_count // 2
    exact_span = halfway // 2
    distant = jnp.full(offset_grid.shape, exact_span, jnp.int32)
    for number in range(1, halfway - exact_span):
        threshold = math.ceil(
            exact_span * (reach / exact_span) ** (number / (halfway - exact_span))
        )
        distant = distant + (distance >= threshold).astype(jnp.int32)
    return jnp.where(distance < exact_span, distance, distant) + jnp.where(
        offset_grid > 0, halfway, 0
    )


def block_allowed(length, live_block):
    position = jnp.arange(live_block.shape[0], dtype=jnp.int32)
    segment = position // length
    return (segment[:, None] == segment[None, :]) & (live_block[None, :] > 0)


def rms_forward(values, gain_vector):
    inverse = lax.rsqrt(jnp.mean(values * values, axis=-1, keepdims=True) + epsilon)
    normed = values * inverse
    return (normed, inverse, normed * gain_vector)


def rms_backward(normed, inverse, gain_vector, grad_scaled):
    weighted = grad_scaled * gain_vector
    return inverse * (weighted - normed * jnp.mean(weighted * normed, axis=-1, keepdims=True))


def split_heads(block_rows):
    block_span = block_rows.shape[0]
    model_width = block_rows.shape[1] // 3
    head_size = model_width // HEADS
    return tuple(
        (
            block_rows[:, part_index * model_width : (part_index + 1) * model_width].reshape(
                block_span, HEADS, head_size
            )
            for part_index in range(3)
        )
    )


def block_scores(queries, keys_part, complete_position_bias, allowed):
    score_scale = queries.shape[-1] ** (-0.5)
    scores = (
        jnp.einsum("qhd,khd->hqk", queries, keys_part, preferred_element_type=jnp.float32)
        * score_scale
        + complete_position_bias
    )
    return jnp.where(allowed[None], scores, -1e30)


def attend_forward(complete_position_bias, packed):
    block_rows, length, live_block = packed
    queries, keys_part, values_part = split_heads(block_rows)
    scores = block_scores(
        queries, keys_part, complete_position_bias, block_allowed(length, live_block)
    )
    row_peak = jnp.max(scores, axis=-1, keepdims=True)
    exponent = jnp.exp(scores - row_peak)
    row_total = jnp.sum(exponent, axis=-1, keepdims=True)
    weights_low = (exponent / row_total).astype(jnp.bfloat16)
    mixed_rows = jnp.einsum(
        "hqk,khd->qhd", weights_low, values_part, preferred_element_type=jnp.float32
    )
    return (
        mixed_rows.reshape(block_rows.shape[0], -1).astype(jnp.bfloat16),
        (row_peak + jnp.log(row_total))[..., 0],
    )


def attend_backward(complete_position_bias, bucket_indicator, packed):
    block_rows, length, live_block, grad_mixed, log_total = packed
    queries, keys_part, values_part = split_heads(block_rows)
    scores = block_scores(
        queries, keys_part, complete_position_bias, block_allowed(length, live_block)
    )
    probs_full = jnp.exp(scores - log_total[:, :, None])
    grad_heads = grad_mixed.reshape(queries.shape)
    grad_probs = jnp.einsum(
        "qhd,khd->hqk", grad_heads, values_part, preferred_element_type=jnp.float32
    )
    score_gradient_rows = (
        probs_full * (grad_probs - jnp.sum(probs_full * grad_probs, axis=-1, keepdims=True))
    ).astype(jnp.bfloat16)
    score_scale = queries.shape[-1] ** (-0.5)
    grad_queries = (
        jnp.einsum(
            "hqk,khd->qhd", score_gradient_rows, keys_part, preferred_element_type=jnp.float32
        )
        * score_scale
    )
    grad_keys = (
        jnp.einsum("hqk,qhd->khd", score_gradient_rows, queries, preferred_element_type=jnp.float32)
        * score_scale
    )
    grad_values = jnp.einsum(
        "hqk,qhd->khd",
        probs_full.astype(jnp.bfloat16),
        grad_heads,
        preferred_element_type=jnp.float32,
    )
    table_grad = jnp.einsum(
        "wif,nif->wn", score_gradient_rows, bucket_indicator, preferred_element_type=jnp.float32
    )
    block_span = block_rows.shape[0]
    joined = jnp.concatenate(
        [
            grad_queries.reshape(block_span, -1),
            grad_keys.reshape(block_span, -1),
            grad_values.reshape(block_span, -1),
        ],
        axis=1,
    )
    return (joined.astype(jnp.bfloat16), table_grad)


def per_device(
    tokens,
    bucket_len,
    valid,
    routes,
    attn_gain,
    qkv_weight,
    out_weight,
    relative_head_bias,
    ffn_gain,
    router_weight,
    w_in,
    w_out,
    cotangent,
):
    top_probability = lax.Precision.HIGHEST
    gain_attn, weight_qkv, weight_out, gain_ffn, weight_router = (
        lax.all_gather(attn_gain, ("dp", "fsdp"), axis=0, tiled=True),
        lax.all_gather(qkv_weight, ("dp", "fsdp"), axis=0, tiled=True),
        lax.all_gather(out_weight, ("dp", "fsdp"), axis=0, tiled=True),
        lax.all_gather(ffn_gain, ("dp", "fsdp"), axis=0, tiled=True),
        lax.all_gather(router_weight, ("dp", "fsdp"), axis=0, tiled=True),
    )
    expert_in, expert_out = (
        lax.all_gather(w_in, "fsdp", axis=0, tiled=True),
        lax.all_gather(w_out, "fsdp", axis=0, tiled=True),
    )
    token_count, model_width = tokens.shape
    block_total = token_count // LONG
    expert_count = expert_in.shape[1]
    capacity = (5 * token_count + 4 * expert_count - 1) // (4 * expert_count)
    bucket_grid = bucket_codes(LONG, BUCKETS, MAXDIST)
    selected_bucket = bucket_grid[None] == jnp.arange(BUCKETS, dtype=jnp.int32)[:, None, None]
    bucket_indicator = selected_bucket.astype(jnp.bfloat16)
    complete_position_bias = jnp.einsum(
        "eo,ozm->ezm",
        relative_head_bias,
        selected_bucket.astype(jnp.float32),
        precision=top_probability,
    )
    live_blocks = valid.reshape(block_total, LONG)
    rows_in = tokens.astype(jnp.float32)
    normed_one, inverse_one, scaled_one = rms_forward(rows_in, gain_attn.astype(jnp.float32))
    normed_low = scaled_one.astype(jnp.bfloat16)
    qkv_low = jnp.dot(normed_low, weight_qkv, preferred_element_type=jnp.float32).astype(
        jnp.bfloat16
    )
    qkv_blocks = qkv_low.reshape(block_total, LONG, 3 * model_width)
    mixed_blocks, log_totals = lax.map(
        partial(attend_forward, complete_position_bias), (qkv_blocks, bucket_len, live_blocks)
    )
    mixed_low = mixed_blocks.reshape(token_count, model_width)
    hidden = rows_in + jnp.dot(mixed_low, weight_out, preferred_element_type=jnp.float32)
    normed_two, inverse_two, scaled_two = rms_forward(hidden, gain_ffn.astype(jnp.float32))
    normed_two_low = scaled_two.astype(jnp.bfloat16)
    normed_two_full = normed_two_low.astype(jnp.float32)
    router_probs = jax.nn.softmax(
        jnp.dot(normed_two_full, weight_router.astype(jnp.float32), precision=top_probability),
        axis=-1,
    )
    chosen = routes[:, 0]
    route_hot = chosen[:, None] == jnp.arange(expert_count, dtype=jnp.int32)[None, :]
    gate_value = jnp.sum(jnp.where(route_hot, router_probs, 0.0), axis=1)
    surviving_rows = valid > 0
    route_picks = route_hot & surviving_rows[:, None]
    places = jnp.cumsum(route_picks.astype(jnp.int32), axis=0) - 1
    slot_place = jnp.sum(jnp.where(route_picks, places, 0), axis=1)
    kept_rows = surviving_rows & (slot_place < capacity)
    slot_code = jnp.where(kept_rows, chosen * capacity + slot_place, 0)
    slot_match = (
        jnp.arange(expert_count * capacity, dtype=jnp.int32)[:, None]
        == jnp.where(kept_rows, slot_code, -1)[None, :]
    )
    slot_filled = jnp.any(slot_match, axis=1)
    slot_token = jnp.sum(
        jnp.where(slot_match, jnp.arange(token_count, dtype=jnp.int32)[None, :], 0), axis=1
    )
    slot_rows = jnp.where(
        slot_filled[:, None], normed_two_low[slot_token], jnp.zeros((), jnp.bfloat16)
    ).reshape(expert_count, capacity, model_width)
    slot_rows = lax.all_gather(slot_rows, "dp", axis=1, tiled=True)
    expert_inner = jnp.einsum(
        "ecd,fed->ecf", slot_rows, expert_in, preferred_element_type=jnp.float32
    )
    active_low = jax.nn.gelu(expert_inner, approximate=True).astype(jnp.bfloat16)
    result_low = (
        lax.psum_scatter(
            jnp.einsum("ecf,fed->ecd", active_low, expert_out, preferred_element_type=jnp.float32),
            "dp",
            scatter_dimension=1,
            tiled=True,
        )
        .astype(jnp.bfloat16)
        .reshape(expert_count * capacity, model_width)
    )
    returned = jnp.where(kept_rows[:, None], result_low[slot_code].astype(jnp.float32), 0.0)
    layer_out = (hidden + gate_value[:, None] * returned).astype(jnp.bfloat16)
    sent_local = jnp.sum((route_picks & kept_rows[:, None]).astype(jnp.int32), axis=0)
    lost_local = jnp.sum((route_picks & ~kept_rows[:, None]).astype(jnp.int32), axis=0)
    count_sums = lax.psum(jnp.stack([sent_local, lost_local]), ("dp", "fsdp"))
    grad_out = cotangent.astype(jnp.float32)
    grad_gate = jnp.sum(grad_out * returned, axis=1)
    grad_back = gate_value[:, None] * grad_out
    grad_result = (
        jnp.where(slot_filled[:, None], grad_back[slot_token], 0.0)
        .astype(jnp.bfloat16)
        .reshape(expert_count, capacity, model_width)
    )
    grad_result = lax.all_gather(grad_result, "dp", axis=1, tiled=True)
    grad_active = jnp.einsum(
        "ecd,fed->ecf", grad_result, expert_out, preferred_element_type=jnp.float32
    )
    unused_value, gelu_pullback = jax.vjp(partial(jax.nn.gelu, approximate=True), expert_inner)
    grad_inner = gelu_pullback(grad_active)[0].astype(jnp.bfloat16)
    grad_slots = lax.psum_scatter(
        jnp.einsum("ecf,fed->ecd", grad_inner, expert_in, preferred_element_type=jnp.float32),
        "dp",
        scatter_dimension=1,
        tiled=True,
    ).reshape(expert_count * capacity, model_width)
    grad_normed_two = jnp.where(kept_rows[:, None], grad_slots[slot_code], 0.0)
    grad_probs = jnp.where(route_hot, grad_gate[:, None], 0.0)
    grad_logits = router_probs * (
        grad_probs - jnp.sum(router_probs * grad_probs, axis=1, keepdims=True)
    )
    grad_normed_two = grad_normed_two + jnp.dot(
        grad_logits, weight_router.astype(jnp.float32).T, precision=top_probability
    )
    grad_hidden = (
        rms_backward(normed_two, inverse_two, gain_ffn.astype(jnp.float32), grad_normed_two)
        + grad_out
    )
    grad_hidden_low = grad_hidden.astype(jnp.bfloat16)
    grad_mixed = jnp.dot(grad_hidden_low, weight_out.T, preferred_element_type=jnp.float32).astype(
        jnp.bfloat16
    )
    joined_blocks, table_grads = lax.map(
        partial(attend_backward, complete_position_bias, bucket_indicator),
        (
            qkv_blocks,
            bucket_len,
            live_blocks,
            grad_mixed.reshape(block_total, LONG, model_width),
            log_totals,
        ),
    )
    grad_qkv = joined_blocks.reshape(token_count, 3 * model_width)
    grad_normed_one = jnp.dot(grad_qkv, weight_qkv.T, preferred_element_type=jnp.float32)
    grad_rows = rms_backward(
        normed_one, inverse_one, gain_attn.astype(jnp.float32), grad_normed_one
    )
    tokens_grad = (grad_rows + grad_hidden).astype(jnp.bfloat16)
    table_grad = lax.psum(jnp.sum(table_grads, axis=0), ("dp", "fsdp"))
    attn_term = jnp.sum(grad_normed_one * normed_one, axis=0)
    qkv_term = jnp.dot(normed_low.T, grad_qkv, preferred_element_type=jnp.float32)
    out_term = jnp.dot(mixed_low.T, grad_hidden_low, preferred_element_type=jnp.float32)
    ffn_term = jnp.sum(grad_normed_two * normed_two, axis=0)
    router_term = jnp.dot(normed_two_full.T, grad_logits, precision=top_probability)
    layer_summed = lax.psum_scatter(
        jnp.concatenate(
            [attn_term[:, None], qkv_term, out_term, ffn_term[:, None], router_term], axis=1
        ),
        ("dp", "fsdp"),
        scatter_dimension=0,
        tiled=True,
    )
    out_term = jnp.einsum(
        "ecf,ecd->fed", active_low, grad_result, preferred_element_type=jnp.float32
    )
    in_term = jnp.einsum("ecd,ecf->fed", slot_rows, grad_inner, preferred_element_type=jnp.float32)
    w_in_grad = lax.psum_scatter(in_term, "fsdp", scatter_dimension=0, tiled=True)
    w_out_grad = lax.psum_scatter(out_term, "fsdp", scatter_dimension=0, tiled=True)
    attn_gain_grad = layer_summed[:, 0]
    qkv_grad = layer_summed[:, 1 : 1 + 3 * model_width]
    out_grad = layer_summed[:, 1 + 3 * model_width : 1 + 4 * model_width]
    ffn_gain_grad = layer_summed[:, 1 + 4 * model_width]
    router_weight_gradient = layer_summed[:, 2 + 4 * model_width :]
    return (
        layer_out,
        tokens_grad,
        attn_gain_grad,
        qkv_grad,
        out_grad,
        table_grad,
        ffn_gain_grad,
        router_weight_gradient,
        w_in_grad,
        w_out_grad,
        count_sums[0],
        count_sums[1],
    )


def solution(mesh):
    both = ("dp", "fsdp")
    body = fused if (mesh.shape["dp"], mesh.shape["fsdp"]) == (4, 8) else per_device
    placed = (
        P(both, None), P(both), P(both), P(both, None), P(both), P(both, None), P(both, None), P(), P(both),
        P(both, None), P(both, None, None), P(both, None, None), P(both, None),
    )
    return jax.shard_map(
        body,
        mesh=mesh,
        in_specs=placed,
        out_specs=(
            P(both, None), P(both, None), P(both), P(both, None), P(both, None), P(), P(both), P(both, None),
            P(both, None, None), P(both, None, None), P(), P(),
        ),
        check_vma=False,
    )
```
